512 devices in a mesh: roll: 128 (over y, z, core), rep: 4 (over x).
Axes of the slice: x: 4, y: 8, z: 8, core: 2. Of those that a mesh axis runs over, the one named last changes fastest.
Arguments:
- rollout: bfloat16 [1048576, 256], P(('roll', 'rep')), may hold values from -7.8 to 7.8
- demo: bfloat16 [262144, 256], P('roll'), may hold values from -6 to 6
- projection: bfloat16 [256, 256], replicated, may hold values from -0.375 to 0.375
- location: int32 [2048], replicated, may hold values from 0 to 2047, as said below
- pair_block: int32 [8192, 8], P(('roll', 'rep')), may hold values from 0 to 2047, as said below
- pair_count: int32 [8192], P(('roll', 'rep')), may hold values from 1 to 8, as said below
Outputs:
- reward: float32 [1048576], P(('roll', 'rep'))
- rollout_potential: float32 [1048576], P(('roll', 'rep'))
- demo_potential: float32 [262144], P('roll')
The draws below stay inside these ranges and needn't reach their ends.
Inputs may be any that keep to these rules, and one draw needn't show every extreme that they name: location is a permutation; demonstration block d is stored block location[d], held by roll index location[d] // 16. `pair_block`: among the slots in use of the 16 rollout blocks of one device, at most 1 name blocks stored on any one roll index, and some device reaches 1. `pair_count`: on one roll index every rollout block uses all 8 slots.
All inputs are finite; a program needn't handle non-finite values.
Results may differ from the reference program's by a relative error of at most 0.0024.
Values may be sent and summed in bfloat16 or wider, within the bound.
No kernel may reach another device: no remote copies, remote signals or barrier semaphores. Data moves between devices by JAX's collectives and lax.ppermute only.
A program may use at most 128 MiB of HBM per device.

```python
import jax
import jax.numpy as jnp
from jax import lax

E = 256
BLK = 128
PAIRS = 8
ITERS = 2
RBD = 16
DBD = 16
NRB = 8192
NDB = 2048
ROLL_FRAMES = 1048576
DEMO_FRAMES = 262144
N_ROLL = 128
N_REP = 4


def demo_places(key):
    return jax.random.permutation(jax.random.fold_in(key, 7), NDB).astype(jnp.int32)


def draw_rollout(key, part):
    noise = jnp.clip(jax.random.normal(jax.random.fold_in(key, 31), (ROLL_FRAMES, E), jnp.float32), -6.0, 6.0)
    devices = NRB // RBD
    rank_keys = jax.random.split(jax.random.fold_in(key, 37), devices)
    ranks = jax.vmap(lambda subkey: jax.random.permutation(subkey, RBD))(rank_keys).astype(jnp.float32)
    offsets = jax.random.uniform(jax.random.fold_in(key, 41), (devices, RBD), jnp.float32)
    signs = jnp.where(jax.random.bernoulli(jax.random.fold_in(key, 43), 0.5, (devices, RBD)), 1.0, -1.0)
    levels = 1.8 * (ranks + offsets) / RBD * signs
    shift = jnp.repeat(levels.reshape(NRB), BLK, total_repeat_length=ROLL_FRAMES)
    return (noise + shift[:, None]).astype(jnp.bfloat16)


def draw_location(key, part):
    return demo_places(key)


def draw_pair_block(key, part):
    places = demo_places(key)
    inverse = jnp.zeros((NDB,), jnp.int32).at[places].set(jnp.arange(NDB, dtype=jnp.int32))
    devices = NRB // RBD
    slot_count = RBD * PAIRS
    owner_keys = jax.random.split(jax.random.fold_in(key, 13), devices)
    owners = jax.vmap(lambda subkey: jax.random.permutation(subkey, N_ROLL).astype(jnp.int32))(owner_keys)
    slot_owner = jnp.arange(slot_count, dtype=jnp.int32) % N_ROLL
    owner_roll = owners[:, slot_owner]
    local_block = jax.random.randint(jax.random.fold_in(key, 17), (devices, slot_count), 0, DBD).astype(jnp.int32)
    chosen = inverse[owner_roll * DBD + local_block]
    return chosen.reshape(NRB, PAIRS).astype(jnp.int32)


def draw_pair_count(key, part):
    counts = jax.random.randint(jax.random.fold_in(key, 23), (NRB,), 1, PAIRS + 1).astype(jnp.int32)
    chosen_roll = jax.random.randint(jax.random.fold_in(key, 29), (), 0, N_ROLL).astype(jnp.int32)
    roll_of = jnp.arange(NRB, dtype=jnp.int32) // (RBD * N_REP)
    return jnp.where(roll_of == chosen_roll, PAIRS, counts).astype(jnp.int32)


def steps_of(own_key, dims, shards, smallest, top_value):
    gain = 1.0
    for position, shards_of in shards:
        steps = jax.random.uniform(jax.random.fold_in(jax.random.fold_in(own_key, 6), position), (shards_of,), jnp.float32, smallest / len(shards), top_value / len(shards))
        gain = gain * jnp.repeat(jnp.exp(steps), dims[position] // shards_of).reshape((-1,) + (1,) * (len(dims) - 1 - position))
    return gain


def bell_draw(stream_key, extent, scale, bound, shards=(), held_as=jnp.bfloat16):
    values = scale * jax.random.normal(stream_key, extent, jnp.float32)
    if shards:
        values = values * steps_of(stream_key, extent, shards, -0.22, 0.18)
    return jnp.clip(values, -bound, bound).astype(held_as)


def setup_inputs(seed: int = 0) -> dict:
    streams_of = jax.random.split(jax.random.key(seed), 7)
    return {
        "rollout": draw_rollout(jax.random.fold_in(streams_of[6], 71), 0),
        "demo": bell_draw(streams_of[1], (DEMO_FRAMES, E), 1.0, 6.0, ((0, 128),)),
        "projection": bell_draw(streams_of[2], (E, E), E ** -0.5, 0.375),
        "location": draw_location(jax.random.fold_in(streams_of[6], 71), 0),
        "pair_block": draw_pair_block(jax.random.fold_in(streams_of[6], 71), 0),
        "pair_count": draw_pair_count(jax.random.fold_in(streams_of[6], 71), 0),
    }


EPSILON = 0.02
UNMATCHED = 2.0
SLACK = -100.0
NEGLIGIBLE = -1.0e30


def reference(rollout, demo, projection, location, pair_block, pair_count):
    roll_count = pair_block.shape[0]
    pair_slots = pair_block.shape[1]
    demo_count = location.shape[0]
    block_len = rollout.shape[0] // roll_count
    features = projection.shape[1]
    roll_codes = jnp.dot(rollout, projection, preferred_element_type=jnp.float32).astype(jnp.bfloat16)
    demo_codes = jnp.dot(demo, projection, preferred_element_type=jnp.float32).astype(jnp.bfloat16)
    roll_tiles = roll_codes.reshape(roll_count, block_len, features)
    demo_tiles = demo_codes.reshape(demo_count, block_len, features)
    stored = location[pair_block].astype(jnp.int32)
    active = jnp.arange(pair_slots, dtype=jnp.int32)[None, :] < pair_count[:, None]
    group_size = RBD
    groups = roll_count // group_size
    group_ids = jnp.arange(groups, dtype=jnp.int32)

    def costs_of(group_index):
        start = (group_index * group_size).astype(jnp.int32)
        rows_x = lax.dynamic_slice_in_dim(roll_tiles, start, group_size, 0).astype(jnp.float32)
        targets = lax.dynamic_slice_in_dim(stored, start, group_size, 0)
        rows_y = demo_tiles[targets].astype(jnp.float32)
        crossed = jnp.einsum("gie,gpje->gpij", rows_x, rows_y)
        norm_x = jnp.sum(rows_x * rows_x, axis=2)
        norm_y = jnp.sum(rows_y * rows_y, axis=3)
        return (norm_x[:, None, :, None] + norm_y[:, :, None, :] - 2.0 * crossed) / features

    def column_pass(roll_pot):
        def per_group(group_index):
            costs = costs_of(group_index)
            start = (group_index * group_size).astype(jnp.int32)
            pots = lax.dynamic_slice_in_dim(roll_pot, start, group_size, 0)
            scores = (pots[:, None, :, None] - costs) / EPSILON
            largest = jnp.max(scores, axis=2)
            return largest + jnp.log(jnp.sum(jnp.exp(scores - largest[:, :, None, :]), axis=2))

        partials = lax.map(per_group, group_ids).reshape(roll_count * pair_slots, block_len)
        segment_ids = jnp.where(active, stored, demo_count).reshape(-1).astype(jnp.int32)
        largest = jax.ops.segment_max(partials, segment_ids, num_segments=demo_count + 1)[:demo_count]
        highest = jnp.maximum(largest, SLACK)
        padded = jnp.concatenate([highest, jnp.zeros((1, block_len), highest.dtype)], axis=0)
        summed = jax.ops.segment_sum(jnp.exp(partials - padded[segment_ids]), segment_ids, num_segments=demo_count + 1)[:demo_count]
        log_total = highest + jnp.log(summed + jnp.exp(SLACK - highest))
        return -EPSILON * log_total

    def row_pass(demo_pot):
        def per_group(group_index):
            costs = costs_of(group_index)
            start = (group_index * group_size).astype(jnp.int32)
            targets = lax.dynamic_slice_in_dim(stored, start, group_size, 0)
            in_use = lax.dynamic_slice_in_dim(active, start, group_size, 0)
            pots = demo_pot[targets]
            scores = (pots[:, :, None, :] - costs) / EPSILON
            scores = jnp.where(in_use[:, :, None, None], scores, NEGLIGIBLE)
            largest = jnp.maximum(jnp.max(scores, axis=(1, 3)), SLACK)
            summed = jnp.sum(jnp.exp(scores - largest[:, None, :, None]), axis=(1, 3)) + jnp.exp(SLACK - largest)
            log_total = largest + jnp.log(summed)
            weights = jnp.exp(scores - log_total[:, None, :, None])
            reward = -(jnp.sum(weights * costs, axis=(1, 3)) + jnp.exp(SLACK - log_total) * UNMATCHED)
            return -EPSILON * log_total, reward

        potentials, rewards = lax.map(per_group, group_ids)
        return potentials.reshape(roll_count, block_len), rewards.reshape(roll_count, block_len)

    roll_pot = jnp.zeros((roll_count, block_len), jnp.float32)
    demo_pot = jnp.zeros((demo_count, block_len), jnp.float32)
    reward = jnp.zeros((roll_count, block_len), jnp.float32)
    for iteration in range(ITERS):
        demo_pot = column_pass(roll_pot)
        roll_pot, reward = row_pass(demo_pot)
    return reward.reshape(-1), roll_pot.reshape(-1), demo_pot.reshape(-1)
```

```python
import functools
import math

import jax
import jax.numpy as jnp
from jax import lax
from jax.experimental import pallas as pl
from jax.experimental.pallas import tpu as pltpu
from jax.sharding import Mesh
from jax.sharding import PartitionSpec as P

EPSILON = 0.02
UNMATCHED = 2.0
SLACK = 100.0
SHIFT = 46.0
LOG2E = 1.4426950408889634
SHIFT2 = SHIFT * LOG2E
FLOOR = math.exp(SHIFT - SLACK)
OFF = -1.0e30

BLK = 128
E = 256
NY, NZ, NC, NX = 8, 8, 2, 4
KB = 16
ROWS = KB * BLK
AUX = 2 * KB
LOAD = ROWS + AUX
SOURCES = NY * NC
POS = SOURCES * NZ
BETA = LOG2E * 2.0 / (E * EPSILON)
VMEM = 52 * 2**20

NT = (((1,), (1,)), ((), ()))
TN = (((0,), (0,)), ((), ()))
NN = (((1,), (0,)), ((), ()))


def exact_sum(onehot, values):
    return lax.dot_general(
        onehot,
        values,
        NN,
        precision=lax.Precision.HIGHEST,
        preferred_element_type=jnp.float32,
    )


def spread(places, count):
    rows = lax.broadcasted_iota(jnp.int32, (count, POS), 0)
    return jnp.where(rows == places, 1.0, 0.0)


def project_kernel(frames, projection, out, norms):
    for k in range(KB):
        rows = pl.ds(k * BLK, BLK)
        codes = jnp.dot(
            frames[rows, :], projection[...], preferred_element_type=jnp.float32
        ).astype(jnp.bfloat16)
        out[rows, :] = codes
        wide = codes.astype(jnp.float32)
        square = wide * wide
        high = square.astype(jnp.bfloat16)
        low = (square - high.astype(jnp.float32)).astype(jnp.bfloat16)
        ones = jnp.ones((16, E), jnp.bfloat16)
        total = lax.dot_general(ones, high, NT, preferred_element_type=jnp.float32)
        total += lax.dot_general(ones, low, NT, preferred_element_type=jnp.float32)
        norms[k : k + 1, :] = total[0:1, :]
    norm = norms[...]
    high = norm.astype(jnp.bfloat16)
    rest = norm - high.astype(jnp.float32)
    middle = rest.astype(jnp.bfloat16)
    low = (rest - middle.astype(jnp.float32)).astype(jnp.bfloat16)
    out[ROWS : ROWS + KB, 0:BLK] = high
    out[ROWS : ROWS + KB, BLK:E] = middle
    out[ROWS + KB : LOAD, 0:BLK] = low
    out[ROWS + KB : LOAD, BLK:E] = jnp.zeros((KB, BLK), jnp.bfloat16)


def project(frames, projection):
    return pl.pallas_call(
        project_kernel,
        out_shape=jax.ShapeDtypeStruct((LOAD, E), jnp.bfloat16),
        in_specs=[pl.BlockSpec(memory_space=pltpu.VMEM)] * 2,
        out_specs=pl.BlockSpec(memory_space=pltpu.VMEM),
        scratch_shapes=[pltpu.VMEM((KB, BLK), jnp.float32)],
        compiler_params=pltpu.CompilerParams(vmem_limit_bytes=VMEM),
        cost_estimate=pl.CostEstimate(
            flops=2 * ROWS * E * E, bytes_accessed=4 * ROWS * E, transcendentals=0
        ),
    )(frames, projection)


def picked(which):
    rows = lax.broadcasted_iota(jnp.int32, (4 * KB, BLK), 0)
    return jnp.where(rows % KB == which, -0.5, 0.0).astype(jnp.bfloat16)


def parts(held):
    aux = held[ROWS:LOAD, :]
    return jnp.concatenate([aux[:, 0:BLK], aux[:, BLK:E]], axis=0)


def first_kernel(code, col_place, left, *rest):
    rights, (cross, columns, sums) = rest[:NZ], rest[NZ:]
    step = pl.program_id(0)
    left_parts = parts(left)
    rows = []
    for z in range(NZ):
        value = code[step * NZ + z]
        active = value >= 0
        value = jnp.maximum(value, 0)
        k, t = value // KB, value % KB
        u = left[pl.ds(pl.multiple_of(k * BLK, BLK), BLK), :]
        v = rights[z][pl.ds(pl.multiple_of(t * BLK, BLK), BLK), :]
        w = lax.dot_general(u, v, NT, preferred_element_type=jnp.float32)
        w += lax.dot_general(
            jnp.concatenate([left_parts, picked(t)], axis=0),
            jnp.concatenate([picked(k), parts(rights[z])], axis=0),
            TN,
            preferred_element_type=jnp.float32,
        )
        cross[z] = w
        shifted = jnp.exp2(w * BETA + jnp.where(active, SHIFT2, OFF))
        rows.append(jnp.sum(shifted, axis=0, keepdims=True))
    sums[pl.ds(pl.multiple_of(step * NZ, NZ), NZ), :] = jnp.concatenate(rows, axis=0)

    @pl.when(step == SOURCES - 1)
    def _():
        columns[...] = exact_sum(spread(col_place[...], NZ * KB), sums[...])


def first_pass(code, col_place, left, rights):
    whole = pl.BlockSpec(memory_space=pltpu.VMEM)
    return pl.pallas_call(
        first_kernel,
        grid_spec=pltpu.PrefetchScalarGridSpec(
            num_scalar_prefetch=1,
            grid=(SOURCES,),
            in_specs=[whole, pl.BlockSpec((None, LOAD, E), lambda s, *_: (s, 0, 0))]
            + [whole] * NZ,
            out_specs=[pl.BlockSpec((NZ, BLK, BLK), lambda s, *_: (s, 0, 0)), whole],
            scratch_shapes=[pltpu.VMEM((POS, BLK), jnp.float32)],
        ),
        out_shape=[
            jax.ShapeDtypeStruct((POS, BLK, BLK), jnp.float32),
            jax.ShapeDtypeStruct((NZ * KB, BLK), jnp.float32),
        ],
        compiler_params=pltpu.CompilerParams(vmem_limit_bytes=VMEM),
        cost_estimate=pl.CostEstimate(
            flops=2 * POS * BLK * BLK * 384,
            bytes_accessed=32 * 2**20,
            transcendentals=POS * BLK * BLK,
        ),
    )(code, col_place, left, *rights)


TILES = 16


def second_kernel(col_at, row_place, column_sum, cross, kernel, costed, rows_out, potential, sums):
    step = pl.program_id(0)

    @pl.when(step == 0)
    def _():
        potential[...] = 2.0 * SHIFT2 - jnp.log2(FLOOR + column_sum[...])

    ones = jnp.ones((16, BLK), jnp.bfloat16)
    rows = []
    for n in range(TILES):
        at = col_at[step * TILES + n]
        pot = potential[pl.ds(jnp.maximum(at, 0), 1), :] + jnp.where(at >= 0, 0.0, OFF)
        w = cross[n]
        rounded = jnp.exp2(w * BETA + pot).astype(jnp.bfloat16)
        kernel[n] = rounded
        costed[n] = (rounded.astype(jnp.float32) * (w * (-2.0 / E))).astype(jnp.bfloat16)
        rows.append(
            lax.dot_general(ones, rounded, NT, preferred_element_type=jnp.float32)[0:1, :]
        )
    sums[pl.ds(pl.multiple_of(step * TILES, TILES), TILES), :] = jnp.concatenate(rows, axis=0)

    @pl.when(step == POS // TILES - 1)
    def _():
        rows_out[...] = exact_sum(spread(row_place[...], SOURCES * KB), sums[...])


def tiles_spec():
    return pl.BlockSpec((TILES, BLK, BLK), lambda s, *_: (s, 0, 0))


def second_pass(col_at, row_place, column_sum, cross):
    whole = pl.BlockSpec(memory_space=pltpu.VMEM)
    return pl.pallas_call(
        second_kernel,
        grid_spec=pltpu.PrefetchScalarGridSpec(
            num_scalar_prefetch=1,
            grid=(POS // TILES,),
            in_specs=[whole, whole, tiles_spec()],
            out_specs=[tiles_spec(), tiles_spec(), whole],
            scratch_shapes=[
                pltpu.VMEM((NZ * KB, BLK), jnp.float32),
                pltpu.VMEM((POS, BLK), jnp.float32),
            ],
        ),
        out_shape=[
            jax.ShapeDtypeStruct((POS, BLK, BLK), jnp.bfloat16),
            jax.ShapeDtypeStruct((POS, BLK, BLK), jnp.bfloat16),
            jax.ShapeDtypeStruct((SOURCES * KB, BLK), jnp.float32),
        ],
        compiler_params=pltpu.CompilerParams(vmem_limit_bytes=VMEM),
    )(col_at, row_place, column_sum, cross)


def two_parts(row):
    high = row.astype(jnp.bfloat16).astype(jnp.float32)
    at = lax.broadcasted_iota(jnp.int32, (16, BLK), 0)
    return jnp.where(at == 0, high, jnp.where(at == 1, row - high, 0.0)).astype(jnp.bfloat16)


def third_kernel(row_at, col_place, scale, kernel, columns, sums):
    step = pl.program_id(0)
    rows = []
    for n in range(TILES):
        at = jnp.maximum(row_at[step * TILES + n], 0)
        both = lax.dot_general(
            two_parts(scale[pl.ds(at, 1), :]),
            kernel[n],
            NN,
            preferred_element_type=jnp.float32,
        )
        rows.append(both[0:1, :] + both[1:2, :])
    sums[pl.ds(pl.multiple_of(step * TILES, TILES), TILES), :] = jnp.concatenate(rows, axis=0)

    @pl.when(step == POS // TILES - 1)
    def _():
        columns[...] = exact_sum(spread(col_place[...], NZ * KB), sums[...])


def third_pass(row_at, col_place, scale, kernel):
    whole = pl.BlockSpec(memory_space=pltpu.VMEM)
    return pl.pallas_call(
        third_kernel,
        grid_spec=pltpu.PrefetchScalarGridSpec(
            num_scalar_prefetch=1,
            grid=(POS // TILES,),
            in_specs=[whole, whole, tiles_spec()],
            out_specs=whole,
            scratch_shapes=[pltpu.VMEM((POS, BLK), jnp.float32)],
        ),
        out_shape=jax.ShapeDtypeStruct((NZ * KB, BLK), jnp.float32),
        compiler_params=pltpu.CompilerParams(vmem_limit_bytes=VMEM),
    )(row_at, col_place, scale, kernel)


def fourth_kernel(col_at, row_place, scale, kernel, costed, rows_out, sums, weighed):
    step = pl.program_id(0)
    rows, heavy = [], []
    for n in range(TILES):
        at = jnp.maximum(col_at[step * TILES + n], 0)
        pair = two_parts(scale[pl.ds(at, 1), :])
        both = lax.dot_general(pair, kernel[n], NT, preferred_element_type=jnp.float32)
        rows.append(both[0:1, :] + both[1:2, :])
        both = lax.dot_general(pair, costed[n], NT, preferred_element_type=jnp.float32)
        heavy.append(both[0:1, :] + both[1:2, :])
    place = pl.ds(pl.multiple_of(step * TILES, TILES), TILES)
    sums[place, :] = jnp.concatenate(rows, axis=0)
    weighed[place, :] = jnp.concatenate(heavy, axis=0)

    @pl.when(step == POS // TILES - 1)
    def _():
        which = spread(row_place[...], SOURCES * KB)
        total = exact_sum(which, sums[...])
        heavy_total = exact_sum(which, weighed[...])
        for s in range(SOURCES):
            rows_out[s, 0:KB, :] = total[s * KB : (s + 1) * KB, :]
            rows_out[s, KB : 2 * KB, :] = heavy_total[s * KB : (s + 1) * KB, :]


def fourth_pass(col_at, row_place, scale, kernel, costed):
    whole = pl.BlockSpec(memory_space=pltpu.VMEM)
    return pl.pallas_call(
        fourth_kernel,
        grid_spec=pltpu.PrefetchScalarGridSpec(
            num_scalar_prefetch=1,
            grid=(POS // TILES,),
            in_specs=[whole, whole, tiles_spec(), tiles_spec()],
            out_specs=whole,
            scratch_shapes=[pltpu.VMEM((POS, BLK), jnp.float32)] * 2,
        ),
        out_shape=jax.ShapeDtypeStruct((SOURCES, 2 * KB, BLK), jnp.float32),
        compiler_params=pltpu.CompilerParams(vmem_limit_bytes=VMEM),
    )(col_at, row_place, scale, kernel, costed)


def ring_pieces(block, axis, n):
    up = [(i, (i + 1) % n) for i in range(n)]
    down = [(i, (i - 1) % n) for i in range(n)]
    half = block.shape[0] // 2
    held = [block] + [None] * (n - 1)
    right = left = block
    for k in range(1, n // 2):
        right = lax.ppermute(right, axis, up)
        left = lax.ppermute(left, axis, down)
        held[n - k], held[k] = right, left
    first = lax.ppermute(right[:half], axis, up)
    second = lax.ppermute(left[half:], axis, down)
    held[n // 2] = jnp.concatenate([first, second], axis=0)
    return held


def swap(value, axes):
    return lax.all_to_all(value, axes, split_axis=0, concat_axis=0, tiled=True)


def to_all(value, axes, n):
    return swap(jnp.broadcast_to(value[None], (n,) + value.shape), axes)


def column_total(columns):
    mine = jnp.sum(swap(columns.reshape(NZ, KB, BLK), "z"), axis=0)
    return jnp.sum(to_all(mine, "x", NX), axis=0)


def slot_codes(location, pair_block, pair_count):
    slots = pair_block.shape[1]
    stored = location[pair_block.reshape(-1)]
    used = (
        jnp.arange(slots, dtype=jnp.int32)[None, :] < pair_count[:, None]
    ).reshape(-1)
    block = jnp.arange(KB * slots, dtype=jnp.int32) // slots
    owner, local = stored // KB, stored % KB
    holders = jnp.arange(NY * NZ * NC, dtype=jnp.int32)
    match = (owner[None, :] == holders[:, None]) & used[None, :]
    return jnp.max(jnp.where(match, (block * KB + local)[None, :], -1), axis=1)


def body(rollout, demo, projection, location, pair_block, pair_count):
    codes = slot_codes(location, pair_block, pair_count)
    codes = codes.reshape(NY, NZ, NC).transpose(0, 2, 1).reshape(SOURCES, NZ)
    codes = swap(codes[:, None, :], ("y", "c")).reshape(SOURCES, NZ)
    turned = (lax.axis_index("z") + jnp.arange(NZ, dtype=jnp.int32)) % NZ
    pick = turned[:, None] == jnp.arange(NZ, dtype=jnp.int32)[None, :]
    codes = jnp.max(jnp.where(pick[None], codes[:, None, :], -1), axis=2)
    used = codes >= 0
    col_at = jnp.where(used, turned[None, :] * KB + codes % KB, -1).reshape(POS)
    sources = jnp.arange(SOURCES, dtype=jnp.int32)[:, None]
    row_at = jnp.where(used, sources * KB + codes // KB, -1).reshape(POS)
    col_place, row_place = col_at.reshape(1, POS), row_at.reshape(1, POS)
    codes = codes.reshape(POS)

    left = lax.all_gather(project(rollout, projection), ("y", "c"))
    rights = ring_pieces(project(demo, projection), "z", NZ)

    cross, columns = first_pass(codes, col_place, left, rights)
    column_sum = column_total(columns)
    kernel, costed, rows = second_pass(
        col_at, row_place, to_all(column_sum, "z", NZ).reshape(NZ * KB, BLK), cross
    )
    row_sum = jnp.sum(swap(rows.reshape(SOURCES, KB, BLK), ("y", "c")), axis=0)
    roll_scale = 1.0 / (FLOOR + row_sum)
    columns = third_pass(
        row_at,
        col_place,
        to_all(roll_scale, ("y", "c"), SOURCES).reshape(SOURCES * KB, BLK),
        kernel,
    )
    plan_sum = column_total(columns)
    demo_scale = 1.0 / (FLOOR / (FLOOR + column_sum) + plan_sum)
    demo_pot = EPSILON * (SHIFT - jnp.log(FLOOR + (FLOOR + column_sum) * plan_sum))
    both = fourth_pass(
        col_at,
        row_place,
        to_all(demo_scale, "z", NZ).reshape(NZ * KB, BLK),
        kernel,
        costed,
    )
    both = jnp.sum(swap(both, ("y", "c")), axis=0)
    total = FLOOR + both[:KB]
    reward = -(both[KB:] + UNMATCHED * FLOOR) / total
    roll_pot = EPSILON * (SHIFT - jnp.log(total))
    return reward.reshape(-1), roll_pot.reshape(-1), demo_pot.reshape(-1)


def solution(mesh):
    grid = Mesh(mesh.devices.reshape(NY, NZ, NC, NX), ("y", "z", "c", "x"))
    every, roll = ("y", "z", "c", "x"), ("y", "z", "c")
    return jax.shard_map(
        body,
        mesh=grid,
        in_specs=(P(every, None), P(roll, None), P(), P(), P(every, None), P(every)),
        out_specs=(P(every), P(every), P(roll)),
        check_vma=False,
    )
```

```python
import math

import jax
import jax.numpy as jnp
from jax import lax
from jax.experimental import pallas as pl
from jax.experimental.pallas import tpu as pltpu
from jax.sharding import Mesh
from jax.sharding import PartitionSpec as P

EPSILON = 0.02
UNMATCHED = 2.0
SLACK = 100.0
SHIFT = 46.0
LOG2E = 1.4426950408889634
SHIFT2 = SHIFT * LOG2E
FLOOR = math.exp(SHIFT - SLACK)
OFF = -1.0e30

BLK = 128
E = 256
NY, NZ, NC, NX = 8, 8, 2, 4
KB = 16
HB = KB // 2
HALF = HB * BLK + 2 * HB
SOURCES = NY * NC
POS = SOURCES * NZ
TILES = 16
STEPS = POS // TILES
BETA = LOG2E * 2.0 / (E * EPSILON)
MIB = 2**20

F32, BF16 = jnp.float32, jnp.bfloat16
NT = (((1,), (1,)), ((), ()))
NN = (((1,), (0,)), ((), ()))
VMEM_WHOLE = pl.BlockSpec(memory_space=pltpu.VMEM)
SMEM_WHOLE = pl.BlockSpec(memory_space=pltpu.SMEM)
ANYWHERE = pl.BlockSpec(memory_space=pl.ANY)
TILE_BLOCK = pl.BlockSpec((TILES, BLK, BLK), lambda s: (s, 0, 0))


def dot(left, right, dims):
    return lax.dot_general(left, right, dims, preferred_element_type=F32)


def exact_sum(onehot, values):
    return lax.dot_general(
        onehot, values, NN, precision=lax.Precision.HIGHEST, preferred_element_type=F32
    )


def spread(places, count):
    rows = lax.broadcasted_iota(jnp.int32, (count, POS), 0)
    return jnp.where(rows == places, 1.0, 0.0)


def project_kernel(frames, projection, out, norms):
    for k in range(KB):
        codes = dot(frames[pl.ds(k * BLK, BLK), :], projection[...], NN).astype(BF16)
        out[k // HB, pl.ds(k % HB * BLK, BLK), :] = codes
        wide = codes.astype(F32)
        square = wide * wide
        high = square.astype(BF16)
        low = (square - high.astype(F32)).astype(BF16)
        ones = jnp.ones((16, E), BF16)
        norms[k : k + 1, :] = (dot(ones, high, NT) + dot(ones, low, NT))[0:1, :]
    for h in range(2):
        norm = norms[h * HB : (h + 1) * HB, :]
        high = norm.astype(BF16).astype(F32)
        middle = (norm - high).astype(BF16).astype(F32)
        low = norm - high - middle
        left = jnp.concatenate([high, low], axis=0)
        right = jnp.concatenate([middle, jnp.zeros_like(low)], axis=0)
        out[h, HB * BLK : HALF, :] = jnp.concatenate([left, right], axis=1).astype(BF16)


def project(frames, projection):
    return pl.pallas_call(
        project_kernel,
        out_shape=jax.ShapeDtypeStruct((2, HALF, E), BF16),
        in_specs=[VMEM_WHOLE] * 2,
        out_specs=VMEM_WHOLE,
        scratch_shapes=[pltpu.VMEM((KB, BLK), F32)],
        compiler_params=pltpu.CompilerParams(vmem_limit_bytes=60 * MIB),
    )(frames, projection)


def first_kernel(code, col_place, left, *rest):
    rights = rest[: 2 * NZ]
    cross, columns, sums, taken, tails, held, picks, norms, sems, right_sem = rest[2 * NZ :]
    step = pl.program_id(0)

    def moves(step):
        slot = step % 2
        copies = []
        for z in range(NZ):
            k = jnp.maximum(code[step * NZ + z], 0) // KB
            start = pl.multiple_of(k % HB * BLK, BLK)
            copies.append((left.at[step, k // HB, pl.ds(start, BLK)], taken.at[slot, z]))
        for h in range(2):
            copies.append((left.at[step, h, pl.ds(HB * BLK, 2 * HB)], tails.at[slot, h]))
        return [
            pltpu.make_async_copy(a, b, sems.at[slot, n]) for n, (a, b) in enumerate(copies)
        ]

    into = [
        pltpu.make_async_copy(rights[i], held.at[i // 2, i % 2], right_sem.at[i])
        for i in range(2 * NZ)
    ]
    @pl.when(step == 0)
    def _():
        for copy in moves(0) + into:
            copy.start()
        row = lax.broadcasted_iota(jnp.int32, (4 * KB, BLK), 0)
        for k in range(KB):
            ours = (row // (2 * KB) == k // HB) & (row % HB == k % HB)
            picks[k] = jnp.where(ours, -0.5, 0.0).astype(BF16)
        for copy in into:
            copy.wait()
        for i in range(2 * NZ):
            tail = held[i // 2, i % 2, HB * BLK : HALF, :].astype(F32)
            norm = tail[0:HB, 0:BLK] + tail[0:HB, BLK:E] + tail[HB : 2 * HB, 0:BLK]
            norms[i * HB : (i + 1) * HB, :] = 0.5 * norm

    @pl.when(step + 1 < SOURCES)
    def _():
        for copy in moves(step + 1):
            copy.start()

    for copy in moves(step):
        copy.wait()
    slot = step % 2
    stacked = []
    for h in range(2):
        tail = tails[slot, h].astype(F32)
        stacked += [tail[:, 0:BLK], tail[:, BLK:E]]
    parts = jnp.concatenate(stacked, axis=0).T.astype(BF16)
    rows = []
    for z in range(NZ):
        value = code[step * NZ + z]
        off = jnp.where(value >= 0, SHIFT2, OFF)
        value = jnp.maximum(value, 0)
        k, t = value // KB, value % KB
        v = held[z, t // HB, pl.ds(pl.multiple_of(t % HB * BLK, BLK), BLK), :]
        w = dot(taken[slot, z], v, NT) + dot(parts, picks[k], NN)
        w = w - norms[pl.ds(z * KB + t, 1), :]
        cross[z] = w
        rows.append(jnp.sum(jnp.exp2(w * BETA + off), axis=0, keepdims=True))
    sums[pl.ds(pl.multiple_of(step * NZ, NZ), NZ), :] = jnp.concatenate(rows, axis=0)

    @pl.when(step == SOURCES - 1)
    def _():
        columns[...] = exact_sum(spread(col_place[...], NZ * KB), sums[...]).astype(BF16)


def first_pass(code, col_place, left, rights):
    return pl.pallas_call(
        first_kernel,
        grid=(SOURCES,),
        in_specs=[SMEM_WHOLE, VMEM_WHOLE, ANYWHERE] + [ANYWHERE] * (2 * NZ),
        out_specs=[pl.BlockSpec((NZ, BLK, BLK), lambda s: (s, 0, 0)), VMEM_WHOLE],
        scratch_shapes=[
            pltpu.VMEM((POS, BLK), F32),
            pltpu.VMEM((2, NZ, BLK, E), BF16),
            pltpu.VMEM((2, 2, 2 * HB, E), BF16),
            pltpu.VMEM((NZ, 2, HALF, E), BF16),
            pltpu.VMEM((KB, 4 * KB, BLK), BF16),
            pltpu.VMEM((NZ * KB, BLK), F32),
            pltpu.SemaphoreType.DMA((2, NZ + 2)),
            pltpu.SemaphoreType.DMA((2 * NZ,)),
        ],
        out_shape=[
            jax.ShapeDtypeStruct((POS, BLK, BLK), F32),
            jax.ShapeDtypeStruct((NZ * KB, BLK), BF16),
        ],
        compiler_params=pltpu.CompilerParams(vmem_limit_bytes=60 * MIB),
    )(code, col_place, left, *rights)


def total_of(received):
    total = received[0].astype(F32)
    for n in range(1, received.shape[0]):
        total += received[n].astype(F32)
    return total


def second_kernel(col_at, row_place, received, cross, kernel, costed, rows_out, column_sum, potential, sums):
    step = pl.program_id(0)

    @pl.when(step == 0)
    def _():
        column_sum[...] = total_of(received)
        potential[...] = 2.0 * SHIFT2 - jnp.log2(FLOOR + column_sum[...])

    ones = jnp.ones((16, BLK), BF16)
    rows = []
    for n in range(TILES):
        at = col_at[step * TILES + n]
        pot = potential[pl.ds(jnp.maximum(at, 0), 1), :] + jnp.where(at >= 0, 0.0, OFF)
        w = cross[n]
        rounded = jnp.exp2(w * BETA + pot).astype(BF16)
        kernel[n] = rounded
        costed[n] = (rounded.astype(F32) * (w * (-2.0 / E))).astype(BF16)
        rows.append(dot(ones, rounded, NT)[0:1, :])
    sums[pl.ds(pl.multiple_of(step * TILES, TILES), TILES), :] = jnp.concatenate(rows, axis=0)

    @pl.when(step == STEPS - 1)
    def _():
        rows_out[...] = exact_sum(spread(row_place[...], SOURCES * KB), sums[...]).astype(BF16)


def second_pass(col_at, row_place, received, cross):
    return pl.pallas_call(
        second_kernel,
        grid=(STEPS,),
        in_specs=[SMEM_WHOLE, VMEM_WHOLE, VMEM_WHOLE, TILE_BLOCK],
        out_specs=[TILE_BLOCK, TILE_BLOCK, VMEM_WHOLE, VMEM_WHOLE],
        scratch_shapes=[pltpu.VMEM((NZ * KB, BLK), F32), pltpu.VMEM((POS, BLK), F32)],
        out_shape=[
            jax.ShapeDtypeStruct((POS, BLK, BLK), BF16),
            jax.ShapeDtypeStruct((POS, BLK, BLK), BF16),
            jax.ShapeDtypeStruct((SOURCES * KB, BLK), BF16),
            jax.ShapeDtypeStruct((NZ * KB, BLK), F32),
        ],
        compiler_params=pltpu.CompilerParams(vmem_limit_bytes=60 * MIB),
    )(col_at, row_place, received, cross)


def two_parts(row):
    high = row.astype(BF16).astype(F32)
    at = lax.broadcasted_iota(jnp.int32, (16, BLK), 0)
    return jnp.where(at == 0, high, jnp.where(at == 1, row - high, 0.0)).astype(BF16)


def third_kernel(row_at, col_place, received, kernel, columns, scale, sums):
    step = pl.program_id(0)

    @pl.when(step == 0)
    def _():
        scale[...] = 1.0 / (FLOOR + received[...].astype(F32))

    rows = []
    for n in range(TILES):
        at = jnp.maximum(row_at[step * TILES + n], 0)
        both = dot(two_parts(scale[pl.ds(at, 1), :]), kernel[n], NN)
        rows.append(both[0:1, :] + both[1:2, :])
    sums[pl.ds(pl.multiple_of(step * TILES, TILES), TILES), :] = jnp.concatenate(rows, axis=0)

    @pl.when(step == STEPS - 1)
    def _():
        columns[...] = exact_sum(spread(col_place[...], NZ * KB), sums[...]).astype(BF16)


def third_pass(row_at, col_place, received, kernel):
    return pl.pallas_call(
        third_kernel,
        grid=(STEPS,),
        in_specs=[SMEM_WHOLE, VMEM_WHOLE, VMEM_WHOLE, TILE_BLOCK],
        out_specs=VMEM_WHOLE,
        scratch_shapes=[pltpu.VMEM((SOURCES * KB, BLK), F32), pltpu.VMEM((POS, BLK), F32)],
        out_shape=jax.ShapeDtypeStruct((NZ * KB, BLK), BF16),
        compiler_params=pltpu.CompilerParams(vmem_limit_bytes=60 * MIB),
    )(row_at, col_place, received, kernel)


def fourth_kernel(col_at, row_place, received, column_sum, kernel, costed, rows_out, plan_out, scale, sums, weighed):
    step = pl.program_id(0)

    @pl.when(step == 0)
    def _():
        plan_sum = total_of(received)
        plan_out[...] = plan_sum
        scale[...] = 1.0 / (FLOOR / (FLOOR + column_sum[...]) + plan_sum)

    rows, heavy = [], []
    for n in range(TILES):
        pair = two_parts(scale[pl.ds(jnp.maximum(col_at[step * TILES + n], 0), 1), :])
        both = dot(pair, kernel[n], NT)
        rows.append(both[0:1, :] + both[1:2, :])
        both = dot(pair, costed[n], NT)
        heavy.append(both[0:1, :] + both[1:2, :])
    place = pl.ds(pl.multiple_of(step * TILES, TILES), TILES)
    sums[place, :] = jnp.concatenate(rows, axis=0)
    weighed[place, :] = jnp.concatenate(heavy, axis=0)

    @pl.when(step == STEPS - 1)
    def _():
        which = spread(row_place[...], SOURCES * KB)
        total = exact_sum(which, sums[...])
        heavy_total = exact_sum(which, weighed[...])
        for s in range(SOURCES):
            c, y = s // NY, s % NY
            rows_out[y * NC + c, 0:KB, :] = total[s * KB : (s + 1) * KB, :]
            rows_out[y * NC + c, KB : 2 * KB, :] = heavy_total[s * KB : (s + 1) * KB, :]


def fourth_pass(col_at, row_place, received, column_sum, kernel, costed):
    return pl.pallas_call(
        fourth_kernel,
        grid=(STEPS,),
        in_specs=[SMEM_WHOLE] + [VMEM_WHOLE] * 3 + [TILE_BLOCK] * 2,
        out_specs=[VMEM_WHOLE] * 2,
        scratch_shapes=[pltpu.VMEM((NZ * KB, BLK), F32)] + [pltpu.VMEM((POS, BLK), F32)] * 2,
        out_shape=[
            jax.ShapeDtypeStruct((SOURCES, 2 * KB, BLK), F32),
            jax.ShapeDtypeStruct((NZ * KB, BLK), F32),
        ],
        compiler_params=pltpu.CompilerParams(vmem_limit_bytes=60 * MIB),
    )(col_at, row_place, received, column_sum, kernel, costed)


def ring_pieces(block, axis, n):
    up = [(i, (i + 1) % n) for i in range(n)]
    down = [(i, (i - 1) % n) for i in range(n)]
    top, low = block[0], block[1]
    held = [[top, low]] + [[None, None] for _ in range(n - 1)]
    right, left = [top, low], [low, top]
    for k in range(1, n // 2 + 1):
        for i in range(2 if k < n // 2 else 1):
            right[i] = lax.ppermute(right[i], axis, up)
            left[i] = lax.ppermute(left[i], axis, down)
            held[n - k][i] = right[i]
            held[k][1 - i] = left[i]
    return [half for pair in held for half in pair]


def swap(value, axes):
    return lax.all_to_all(value, axes, split_axis=0, concat_axis=0, tiled=True)


def to_all(value, axes, n):
    return swap(jnp.broadcast_to(value[None], (n,) + value.shape), axes)


def columns_to_row(columns):
    over_rep = jnp.sum(to_all(columns, "x", NX).astype(F32), axis=0)
    return to_all(over_rep.astype(BF16), "z", NZ)


def own_columns(columns):
    at = lax.axis_index("z") * KB
    return lax.dynamic_slice_in_dim(columns, at, KB, 0)


def slot_codes(location, pair_block, pair_count):
    slots = pair_block.shape[1]
    stored = location[pair_block.reshape(-1)]
    used = (
        jnp.arange(slots, dtype=jnp.int32)[None, :] < pair_count[:, None]
    ).reshape(-1)
    block = jnp.arange(KB * slots, dtype=jnp.int32) // slots
    owner, local = stored // KB, stored % KB
    holders = jnp.arange(NY * NZ * NC, dtype=jnp.int32)
    match = (owner[None, :] == holders[:, None]) & used[None, :]
    return jnp.max(jnp.where(match, (block * KB + local)[None, :], -1), axis=1)


def body(rollout, demo, projection, location, pair_block, pair_count):
    codes = slot_codes(location, pair_block, pair_count)
    codes = codes.reshape(NY, NZ, NC).transpose(0, 2, 1).reshape(SOURCES, NZ)
    codes = swap(codes[:, None, :], ("y", "c")).reshape(SOURCES, NZ)
    turned = (lax.axis_index("z") + jnp.arange(NZ, dtype=jnp.int32)) % NZ
    pick = turned[:, None] == jnp.arange(NZ, dtype=jnp.int32)[None, :]
    codes = jnp.max(jnp.where(pick[None], codes[:, None, :], -1), axis=2)
    used = codes >= 0
    col_at = jnp.where(used, turned[None, :] * KB + codes % KB, -1).reshape(POS)
    source = jnp.arange(SOURCES, dtype=jnp.int32)
    source = (source % NC * NY + source // NC)[:, None]
    row_at = jnp.where(used, source * KB + codes // KB, -1).reshape(POS)
    col_place, row_place = col_at.reshape(1, POS), row_at.reshape(1, POS)
    codes = codes.reshape(POS)

    left = lax.all_gather(project(rollout, projection), ("y", "c"))
    rights = ring_pieces(project(demo, projection), "z", NZ)

    cross, columns = first_pass(codes, col_place, left, rights)
    kernel, costed, rows, column_sum = second_pass(
        col_at, row_place, columns_to_row(columns), cross
    )
    rows = jnp.sum(swap(rows.reshape(NC, NY * KB, BLK), "c").astype(F32), axis=0)
    rows = jnp.sum(to_all(rows.astype(BF16), "y", NY).astype(F32), axis=0)
    rows = to_all(rows.astype(BF16), "c", NC).reshape(SOURCES * KB, BLK)
    columns = third_pass(row_at, col_place, rows, kernel)
    both, plan_sum = fourth_pass(
        col_at, row_place, columns_to_row(columns), column_sum, kernel, costed
    )
    both = jnp.sum(swap(both, ("y", "c")), axis=0)
    total = FLOOR + both[:KB]
    reward = -(both[KB:] + UNMATCHED * FLOOR) / total
    roll_pot = EPSILON * (SHIFT - jnp.log(total))
    reached = FLOOR + (FLOOR + own_columns(column_sum)) * own_columns(plan_sum)
    demo_pot = EPSILON * (SHIFT - jnp.log(reached))
    return reward.reshape(-1), roll_pot.reshape(-1), demo_pot.reshape(-1)


def solution(mesh):
    grid = Mesh(mesh.devices.reshape(NY, NZ, NC, NX), ("y", "z", "c", "x"))
    every, roll = ("y", "z", "c", "x"), ("y", "z", "c")
    return jax.shard_map(
        body,
        mesh=grid,
        in_specs=(P(every, None), P(roll, None), P(), P(), P(every, None), P(every)),
        out_specs=(P(every), P(every), P(roll)),
        check_vma=False,
    )
```

```python
import math

import jax
import jax.numpy as jnp
from jax import lax
from jax.experimental import pallas as pl
from jax.experimental.pallas import tpu as pltpu
from jax.sharding import Mesh
from jax.sharding import PartitionSpec as P

EPSILON = 0.02
UNMATCHED = 2.0
SLACK = 100.0
SHIFT = 46.0
LOG2E = 1.4426950408889634
SHIFT2 = SHIFT * LOG2E
FLOOR = math.exp(SHIFT - SLACK)
OFF = -1.0e30

BLK = 128
E = 256
NY, NZ, NC, NX = 8, 8, 2, 4
KB = 16
HB = KB // 2
HALF = HB * BLK + 2 * HB
SOURCES = NY * NC
POS = SOURCES * NZ
ROWS = KB * BLK
PART = 512
BETA = LOG2E * 2.0 / (E * EPSILON)
MIB = 2**20

F32, BF16 = jnp.float32, jnp.bfloat16
NT = (((1,), (1,)), ((), ()))
NN = (((1,), (0,)), ((), ()))
VMEM_WHOLE = pl.BlockSpec(memory_space=pltpu.VMEM)
SMEM_WHOLE = pl.BlockSpec(memory_space=pltpu.SMEM)
ANYWHERE = pl.BlockSpec(memory_space=pl.ANY)
IN_HBM = pl.BlockSpec(memory_space=pltpu.HBM)
GRANT = 40 * MIB


def dot(left, right, dims):
    return lax.dot_general(left, right, dims, preferred_element_type=F32)


def exact_sum(onehot, values):
    return lax.dot_general(
        onehot, values, NN, precision=lax.Precision.HIGHEST, preferred_element_type=F32
    )


def spread(places, count):
    rows = lax.broadcasted_iota(jnp.int32, (count, POS), 0)
    return jnp.where(rows == places, 1.0, 0.0)


def project_kernel(frames, projection, out, here, made, norms, sems, out_sems):
    def inward(n):
        rows = pl.ds(n * PART, PART)
        return pltpu.make_async_copy(frames.at[rows], here.at[rows], sems.at[n])

    def outward(h):
        return pltpu.make_async_copy(made.at[h], out.at[h], out_sems.at[h])

    for n in range(ROWS // PART):
        inward(n).start()
    ones = jnp.ones((16, E), BF16)
    for h in range(2):
        for j in range(HB):
            k = h * HB + j
            if k * BLK % PART == 0:
                inward(k * BLK // PART).wait()
            codes = dot(here[pl.ds(k * BLK, BLK), :], projection[...], NN).astype(BF16)
            made[h, pl.ds(j * BLK, BLK), :] = codes
            wide = codes.astype(F32)
            square = wide * wide
            high = square.astype(BF16)
            low = (square - high.astype(F32)).astype(BF16)
            norms[j : j + 1, :] = (dot(ones, high, NT) + dot(ones, low, NT))[0:1, :]
        norm = norms[...]
        high = norm.astype(BF16).astype(F32)
        middle = (norm - high).astype(BF16).astype(F32)
        low = norm - high - middle
        left = jnp.concatenate([high, low], axis=0)
        right = jnp.concatenate([middle, jnp.zeros_like(low)], axis=0)
        made[h, HB * BLK : HALF, :] = jnp.concatenate([left, right], axis=1).astype(BF16)
        outward(h).start()
    for h in range(2):
        outward(h).wait()


def project(frames, projection):
    return pl.pallas_call(
        project_kernel,
        out_shape=pltpu.HBM((2, HALF, E), BF16),
        in_specs=[IN_HBM, VMEM_WHOLE],
        out_specs=IN_HBM,
        scratch_shapes=[
            pltpu.VMEM((ROWS, E), BF16),
            pltpu.VMEM((2, HALF, E), BF16),
            pltpu.VMEM((HB, BLK), F32),
            pltpu.SemaphoreType.DMA((ROWS // PART,)),
            pltpu.SemaphoreType.DMA((2,)),
        ],
        compiler_params=pltpu.CompilerParams(vmem_limit_bytes=GRANT),
    )(in_hbm(frames), projection)


def in_hbm(value):
    return pltpu.with_memory_space_constraint(value, pltpu.HBM)


AHEAD = 2
SLOTS = AHEAD + 1
CHUNK = 32
CHUNKS = POS // CHUNK


def first_kernel(code, col_at, row_at, col_place, row_place, left, *rest):
    rights = rest[: 2 * NZ]
    (
        cross, columns, sums, taken, tails, held, picks, parts, norms, made,
        sems, tail_sem, right_sem, out_sem,
    ) = rest[2 * NZ :]

    def moves(z):
        slot = z % SLOTS
        copies = []
        for n in range(SOURCES):
            k = jnp.maximum(code[z * SOURCES + n], 0) // KB
            start = pl.multiple_of(k % HB * BLK, BLK)
            copies.append(
                pltpu.make_async_copy(
                    left.at[n, k // HB, pl.ds(start, BLK)], taken.at[slot, n], sems.at[slot, n]
                )
            )
        return copies

    def away(z):
        slot = z % SLOTS
        to = cross.at[pl.ds(z * SOURCES, SOURCES)]
        return pltpu.make_async_copy(made.at[slot], to, out_sem.at[slot])

    into = [
        pltpu.make_async_copy(rights[i], held.at[i // 2, i % 2], right_sem.at[i])
        for i in range(2 * NZ)
    ]
    tail_copy = pltpu.make_async_copy(
        left.at[:, :, pl.ds(HB * BLK, 2 * HB)], tails, tail_sem
    )
    tail_copy.start()
    for z in range(AHEAD):
        for copy in into[2 * z : 2 * z + 2] + moves(z):
            copy.start()
    for copy in into[2 * AHEAD :]:
        copy.start()
    row = lax.broadcasted_iota(jnp.int32, (4 * KB, BLK), 0)
    for k in range(KB):
        ours = (row // (2 * KB) == k // HB) & (row % HB == k % HB)
        picks[k] = jnp.where(ours, -0.5, 0.0).astype(BF16)
    tail_copy.wait()
    for n in range(SOURCES):
        stacked = []
        for h in range(2):
            tail = tails[n, h].astype(F32)
            stacked += [tail[:, 0:BLK], tail[:, BLK:E]]
        parts[n] = jnp.concatenate(stacked, axis=0).T.astype(BF16)

    @pl.loop(0, NZ)
    def _(z):
        slot = z % SLOTS

        @pl.when(z + AHEAD < NZ)
        def _():
            for copy in moves(z + AHEAD):
                copy.start()

        @pl.when(z >= SLOTS)
        def _():
            away(z - SLOTS).wait()

        for h in range(2):
            pltpu.make_async_copy(rights[h], held.at[z, h], right_sem.at[2 * z + h]).wait()
            tail = held[z, h, HB * BLK : HALF, :].astype(F32)
            norm = tail[0:HB, 0:BLK] + tail[0:HB, BLK:E] + tail[HB : 2 * HB, 0:BLK]
            norms[h * HB : (h + 1) * HB, :] = 0.5 * norm
        for copy in moves(z):
            copy.wait()
        rows = []
        for n in range(SOURCES):
            value = code[z * SOURCES + n]
            off = jnp.where(value >= 0, SHIFT2, OFF)
            value = jnp.maximum(value, 0)
            k, t = value // KB, value % KB
            v = held[z, t // HB, pl.ds(pl.multiple_of(t % HB * BLK, BLK), BLK), :]
            w = dot(taken[slot, n], v, NT) + dot(parts[n], picks[k], NN)
            w = w - norms[pl.ds(t, 1), :]
            made[slot, n] = w
            rows.append(jnp.sum(jnp.exp2(w * BETA + off), axis=0, keepdims=True))
        away(z).start()
        place = pl.ds(pl.multiple_of(z * SOURCES, SOURCES), SOURCES)
        sums[place, :] = jnp.concatenate(rows, axis=0)

    columns[...] = exact_sum(spread(col_place[...], NZ * KB), sums[...]).astype(BF16)
    for z in range(NZ - SLOTS, NZ):
        away(z).wait()


def first_pass(code, col_at, row_at, col_place, row_place, left, rights):
    return pl.pallas_call(
        first_kernel,
        in_specs=[SMEM_WHOLE] * 3 + [VMEM_WHOLE] * 2 + [ANYWHERE] * (2 * NZ + 1),
        out_specs=[IN_HBM, VMEM_WHOLE],
        scratch_shapes=[
            pltpu.VMEM((POS, BLK), F32),
            pltpu.VMEM((SLOTS, SOURCES, BLK, E), BF16),
            pltpu.VMEM((SOURCES, 2, 2 * HB, E), BF16),
            pltpu.VMEM((NZ, 2, HALF, E), BF16),
            pltpu.VMEM((KB, 4 * KB, BLK), BF16),
            pltpu.VMEM((SOURCES, BLK, 4 * KB), BF16),
            pltpu.VMEM((KB, BLK), F32),
            pltpu.VMEM((SLOTS, SOURCES, BLK, BLK), F32),
            pltpu.SemaphoreType.DMA((SLOTS, SOURCES)),
            pltpu.SemaphoreType.DMA,
            pltpu.SemaphoreType.DMA((2 * NZ,)),
            pltpu.SemaphoreType.DMA((SLOTS,)),
        ],
        out_shape=[
            pltpu.HBM((POS, BLK, BLK), F32),
            jax.ShapeDtypeStruct((NZ * KB, BLK), BF16),
        ],
        compiler_params=pltpu.CompilerParams(vmem_limit_bytes=GRANT),
    )(code, col_at, row_at, col_place, row_place, left, *rights)


def total_of(received):
    total = received[0].astype(F32)
    for n in range(1, received.shape[0]):
        total += received[n].astype(F32)
    return total


def one_chunk(source, target, sems, n):
    part = pl.ds(n * CHUNK, CHUNK)
    return pltpu.make_async_copy(source.at[part], target.at[part], sems.at[n])


def start_all(source, target, sems):
    for n in range(CHUNKS):
        one_chunk(source, target, sems, n).start()


def second_kernel(
    col_at, row_place, received, cross, kernel, rows_out, column_sum,
    cross_here, kernel_here, potential, sums, in_sem, kernel_sem,
):
    start_all(cross, cross_here, in_sem)
    column_sum[...] = total_of(received)
    potential[...] = 2.0 * SHIFT2 - jnp.log2(FLOOR + column_sum[...])
    ones = jnp.ones((16, BLK), BF16)

    @pl.loop(0, CHUNKS)
    def _(step):
        one_chunk(cross, cross_here, in_sem, step).wait()
        rows = []
        for n in range(CHUNK):
            tile = step * CHUNK + n
            at = col_at[tile]
            pot = potential[pl.ds(jnp.maximum(at, 0), 1), :] + jnp.where(at >= 0, 0.0, OFF)
            w = cross_here[tile]
            rounded = jnp.exp2(w * BETA + pot).astype(BF16)
            kernel_here[tile, 0:BLK, :] = rounded
            kernel_here[tile, BLK : 2 * BLK, :] = (
                rounded.astype(F32) * (w * (-2.0 / E))
            ).astype(BF16)
            rows.append(dot(ones, rounded, NT)[0:1, :])
        one_chunk(kernel_here, kernel, kernel_sem, step).start()
        sums[pl.ds(pl.multiple_of(step * CHUNK, CHUNK), CHUNK), :] = jnp.concatenate(rows, axis=0)

    rows_out[...] = exact_sum(spread(row_place[...], SOURCES * KB), sums[...]).astype(BF16)

    @pl.loop(0, CHUNKS)
    def _(step):
        one_chunk(kernel_here, kernel, kernel_sem, step).wait()


def second_pass(col_at, row_place, received, cross):
    return pl.pallas_call(
        second_kernel,
        in_specs=[SMEM_WHOLE, VMEM_WHOLE, VMEM_WHOLE, IN_HBM],
        out_specs=[IN_HBM, VMEM_WHOLE, VMEM_WHOLE],
        scratch_shapes=[
            pltpu.VMEM((POS, BLK, BLK), F32),
            pltpu.VMEM((POS, 2 * BLK, BLK), BF16),
            pltpu.VMEM((NZ * KB, BLK), F32),
            pltpu.VMEM((POS, BLK), F32),
            pltpu.SemaphoreType.DMA((CHUNKS,)),
            pltpu.SemaphoreType.DMA((CHUNKS,)),
        ],
        out_shape=[
            pltpu.HBM((POS, 2 * BLK, BLK), BF16),
            jax.ShapeDtypeStruct((SOURCES * KB, BLK), BF16),
            jax.ShapeDtypeStruct((NZ * KB, BLK), F32),
        ],
        compiler_params=pltpu.CompilerParams(vmem_limit_bytes=GRANT),
    )(col_at, row_place, received, in_hbm(cross))


def two_parts(row):
    high = row.astype(BF16).astype(F32)
    at = lax.broadcasted_iota(jnp.int32, (16, BLK), 0)
    return jnp.where(at == 0, high, jnp.where(at == 1, row - high, 0.0)).astype(BF16)


def third_kernel(row_at, col_place, received, kernel, columns, kernel_here, scale, sums, in_sem):
    upper = kernel.at[:, pl.ds(0, BLK)]
    start_all(upper, kernel_here, in_sem)
    scale[...] = 1.0 / (FLOOR + received[...].astype(F32))

    @pl.loop(0, CHUNKS)
    def _(step):
        one_chunk(upper, kernel_here, in_sem, step).wait()
        rows = []
        for n in range(CHUNK):
            tile = step * CHUNK + n
            at = jnp.maximum(row_at[tile], 0)
            both = dot(two_parts(scale[pl.ds(at, 1), :]), kernel_here[tile], NN)
            rows.append(both[0:1, :] + both[1:2, :])
        sums[pl.ds(pl.multiple_of(step * CHUNK, CHUNK), CHUNK), :] = jnp.concatenate(rows, axis=0)

    columns[...] = exact_sum(spread(col_place[...], NZ * KB), sums[...]).astype(BF16)


def third_pass(row_at, col_place, received, kernel):
    return pl.pallas_call(
        third_kernel,
        in_specs=[SMEM_WHOLE, VMEM_WHOLE, VMEM_WHOLE, IN_HBM],
        out_specs=VMEM_WHOLE,
        scratch_shapes=[
            pltpu.VMEM((POS, BLK, BLK), BF16),
            pltpu.VMEM((SOURCES * KB, BLK), F32),
            pltpu.VMEM((POS, BLK), F32),
            pltpu.SemaphoreType.DMA((CHUNKS,)),
        ],
        out_shape=jax.ShapeDtypeStruct((NZ * KB, BLK), BF16),
        compiler_params=pltpu.CompilerParams(vmem_limit_bytes=GRANT),
    )(row_at, col_place, received, in_hbm(kernel))


def fourth_kernel(
    col_at, row_place, received, column_sum, kernel, rows_out, plan_out,
    kernel_here, scale, sums, weighed, kernel_sem,
):
    start_all(kernel, kernel_here, kernel_sem)
    plan_sum = total_of(received)
    plan_out[...] = plan_sum
    scale[...] = 1.0 / (FLOOR / (FLOOR + column_sum[...]) + plan_sum)

    @pl.loop(0, CHUNKS)
    def _(step):
        one_chunk(kernel, kernel_here, kernel_sem, step).wait()
        rows, heavy = [], []
        for n in range(CHUNK):
            tile = step * CHUNK + n
            pair = two_parts(scale[pl.ds(jnp.maximum(col_at[tile], 0), 1), :])
            both = dot(pair, kernel_here[tile], NT)
            both = both[0:1, :] + both[1:2, :]
            rows.append(both[:, 0:BLK])
            heavy.append(both[:, BLK : 2 * BLK])
        place = pl.ds(pl.multiple_of(step * CHUNK, CHUNK), CHUNK)
        sums[place, :] = jnp.concatenate(rows, axis=0)
        weighed[place, :] = jnp.concatenate(heavy, axis=0)

    which = spread(row_place[...], SOURCES * KB)
    total = exact_sum(which, sums[...])
    heavy_total = exact_sum(which, weighed[...])
    for s in range(SOURCES):
        c, y = s // NY, s % NY
        rows_out[y * NC + c, 0:KB, :] = total[s * KB : (s + 1) * KB, :]
        rows_out[y * NC + c, KB : 2 * KB, :] = heavy_total[s * KB : (s + 1) * KB, :]


def fourth_pass(col_at, row_place, received, column_sum, kernel):
    return pl.pallas_call(
        fourth_kernel,
        in_specs=[SMEM_WHOLE] + [VMEM_WHOLE] * 3 + [IN_HBM],
        out_specs=[VMEM_WHOLE] * 2,
        scratch_shapes=[
            pltpu.VMEM((POS, 2 * BLK, BLK), BF16),
            pltpu.VMEM((NZ * KB, BLK), F32),
            pltpu.VMEM((POS, BLK), F32),
            pltpu.VMEM((POS, BLK), F32),
            pltpu.SemaphoreType.DMA((CHUNKS,)),
        ],
        out_shape=[
            jax.ShapeDtypeStruct((SOURCES, 2 * KB, BLK), F32),
            jax.ShapeDtypeStruct((NZ * KB, BLK), F32),
        ],
        compiler_params=pltpu.CompilerParams(vmem_limit_bytes=GRANT),
    )(col_at, row_place, received, column_sum, in_hbm(kernel))


def ring_pieces(block, axis, n):
    up = [(i, (i + 1) % n) for i in range(n)]
    down = [(i, (i - 1) % n) for i in range(n)]
    top, low = block[0], block[1]
    held = [[top, low]] + [[None, None] for _ in range(n - 1)]
    right, left = [top, low], [low, top]
    for k in range(1, n // 2 + 1):
        for i in range(2 if k < n // 2 else 1):
            right[i] = lax.ppermute(right[i], axis, up)
            left[i] = lax.ppermute(left[i], axis, down)
            held[n - k][i] = right[i]
            held[k][1 - i] = left[i]
    return [half for pair in held for half in pair]


def swap(value, axes):
    return lax.all_to_all(value, axes, split_axis=0, concat_axis=0, tiled=True)


def to_all(value, axes, n):
    return swap(jnp.broadcast_to(value[None], (n,) + value.shape), axes)


def columns_to_row(columns):
    over_rep = jnp.sum(to_all(columns, "x", NX).astype(F32), axis=0)
    return to_all(over_rep.astype(BF16), "z", NZ)


def own_columns(columns):
    at = lax.axis_index("z") * KB
    return lax.dynamic_slice_in_dim(columns, at, KB, 0)


def slot_codes(location, pair_block, pair_count):
    slots = pair_block.shape[1]
    stored = location[pair_block.reshape(-1)]
    used = (
        jnp.arange(slots, dtype=jnp.int32)[None, :] < pair_count[:, None]
    ).reshape(-1)
    block = jnp.arange(KB * slots, dtype=jnp.int32) // slots
    owner, local = stored // KB, stored % KB
    holders = jnp.arange(NY * NZ * NC, dtype=jnp.int32)
    match = (owner[None, :] == holders[:, None]) & used[None, :]
    return jnp.max(jnp.where(match, (block * KB + local)[None, :], -1), axis=1)


def body(rollout, demo, projection, location, pair_block, pair_count):
    codes = slot_codes(location, pair_block, pair_count)
    codes = codes.reshape(NY, NZ, NC).transpose(0, 2, 1).reshape(SOURCES, NZ)
    codes = swap(codes[:, None, :], ("y", "c")).reshape(SOURCES, NZ)
    turned = (lax.axis_index("z") + jnp.arange(NZ, dtype=jnp.int32)) % NZ
    pick = turned[:, None] == jnp.arange(NZ, dtype=jnp.int32)[None, :]
    codes = jnp.max(jnp.where(pick[:, None, :], codes[None], -1), axis=2)
    used = codes >= 0
    col_at = jnp.where(used, turned[:, None] * KB + codes % KB, -1).reshape(POS)
    source = jnp.arange(SOURCES, dtype=jnp.int32)
    source = (source % NC * NY + source // NC)[None, :]
    row_at = jnp.where(used, source * KB + codes // KB, -1).reshape(POS)
    col_place, row_place = col_at.reshape(1, POS), row_at.reshape(1, POS)
    codes = codes.reshape(POS)

    left = lax.all_gather(project(rollout, projection), ("y", "c"))
    rights = ring_pieces(project(demo, projection), "z", NZ)

    cross, columns = first_pass(codes, col_at, row_at, col_place, row_place, left, rights)
    kernel, rows, column_sum = second_pass(
        col_at, row_place, columns_to_row(columns), cross
    )
    rows = jnp.sum(swap(rows.reshape(NC, NY * KB, BLK), "c").astype(F32), axis=0)
    rows = jnp.sum(to_all(rows.astype(BF16), "y", NY).astype(F32), axis=0)
    rows = to_all(rows.astype(BF16), "c", NC).reshape(SOURCES * KB, BLK)
    columns = third_pass(row_at, col_place, rows, kernel)
    both, plan_sum = fourth_pass(
        col_at, row_place, columns_to_row(columns), column_sum, kernel
    )
    both = jnp.sum(swap(both, ("y", "c")), axis=0)
    total = FLOOR + both[:KB]
    reward = -(both[KB:] + UNMATCHED * FLOOR) / total
    roll_pot = EPSILON * (SHIFT - jnp.log(total))
    reached = FLOOR + (FLOOR + own_columns(column_sum)) * own_columns(plan_sum)
    demo_pot = EPSILON * (SHIFT - jnp.log(reached))
    return reward.reshape(-1), roll_pot.reshape(-1), demo_pot.reshape(-1)


def solution(mesh):
    grid = Mesh(mesh.devices.reshape(NY, NZ, NC, NX), ("y", "z", "c", "x"))
    every, roll = ("y", "z", "c", "x"), ("y", "z", "c")
    return jax.shard_map(
        body,
        mesh=grid,
        in_specs=(P(every, None), P(roll, None), P(), P(), P(every, None), P(every)),
        out_specs=(P(every), P(every), P(roll)),
        check_vma=False,
    )
```

```python
import math

import jax
import jax.numpy as jnp
from jax import lax
from jax.experimental import pallas as pl
from jax.experimental.pallas import tpu as pltpu
from jax.sharding import Mesh
from jax.sharding import PartitionSpec as P

EPSILON = 0.02
UNMATCHED = 2.0
SLACK = 100.0
SHIFT = 46.0
LOG2E = 1.4426950408889634
SHIFT2 = SHIFT * LOG2E
FLOOR = math.exp(SHIFT - SLACK)
OFF = -1.0e30

BLK = 128
E = 256
NY, NZ, NC, NX = 8, 8, 2, 4
KB = 16
HB = KB // 2
HALF = HB * BLK + 2 * HB
SOURCES = NY * NC
POS = SOURCES * NZ
ROWS = KB * BLK
PART = 512
BETA = LOG2E * 2.0 / (E * EPSILON)
MIB = 2**20

F32, BF16 = jnp.float32, jnp.bfloat16
NT = (((1,), (1,)), ((), ()))
NN = (((1,), (0,)), ((), ()))
VMEM_WHOLE = pl.BlockSpec(memory_space=pltpu.VMEM)
SMEM_WHOLE = pl.BlockSpec(memory_space=pltpu.SMEM)
IN_HBM = pl.BlockSpec(memory_space=pltpu.HBM)
GRANT = 40 * MIB


def dot(left, right, dims):
    return lax.dot_general(left, right, dims, preferred_element_type=F32)


def exact_sum(onehot, values):
    return lax.dot_general(
        onehot, values, NN, precision=lax.Precision.HIGHEST, preferred_element_type=F32
    )


def spread(places, count):
    rows = lax.broadcasted_iota(jnp.int32, (count, POS), 0)
    return jnp.where(rows == places, 1.0, 0.0)


def project_kernel(frames, head, out, here, projection, made, norms, sems, head_sem, out_sems):
    def inward(n):
        rows = pl.ds(n * PART, PART)
        return pltpu.make_async_copy(frames.at[rows], here.at[rows], sems.at[n])

    def outward(h):
        return pltpu.make_async_copy(made.at[h], out.at[h], out_sems.at[h])

    head_copy = pltpu.make_async_copy(head, projection, head_sem)
    inward(0).start()
    head_copy.start()
    for n in range(1, ROWS // PART):
        inward(n).start()
    ones = jnp.ones((16, E), BF16)
    head_copy.wait()
    for h in range(2):
        for j in range(HB):
            k = h * HB + j
            if k * BLK % PART == 0:
                inward(k * BLK // PART).wait()
            codes = dot(here[pl.ds(k * BLK, BLK), :], projection[...], NN).astype(BF16)
            made[h, pl.ds(j * BLK, BLK), :] = codes
            wide = codes.astype(F32)
            square = wide * wide
            high = square.astype(BF16)
            low = (square - high.astype(F32)).astype(BF16)
            norms[j : j + 1, :] = (dot(ones, high, NT) + dot(ones, low, NT))[0:1, :]
        norm = norms[...]
        high = norm.astype(BF16).astype(F32)
        middle = (norm - high).astype(BF16).astype(F32)
        low = norm - high - middle
        left = jnp.concatenate([high, low], axis=0)
        right = jnp.concatenate([middle, jnp.zeros_like(low)], axis=0)
        made[h, HB * BLK : HALF, :] = jnp.concatenate([left, right], axis=1).astype(BF16)
        outward(h).start()
    for h in range(2):
        outward(h).wait()


def project(frames, projection):
    return pl.pallas_call(
        project_kernel,
        out_shape=pltpu.HBM((2, HALF, E), BF16),
        in_specs=[IN_HBM, IN_HBM],
        out_specs=IN_HBM,
        scratch_shapes=[
            pltpu.VMEM((ROWS, E), BF16),
            pltpu.VMEM((E, E), BF16),
            pltpu.VMEM((2, HALF, E), BF16),
            pltpu.VMEM((HB, BLK), F32),
            pltpu.SemaphoreType.DMA((ROWS // PART,)),
            pltpu.SemaphoreType.DMA,
            pltpu.SemaphoreType.DMA((2,)),
        ],
        compiler_params=pltpu.CompilerParams(vmem_limit_bytes=GRANT),
    )(in_hbm(frames), in_hbm(projection))


def in_hbm(value):
    return pltpu.with_memory_space_constraint(value, pltpu.HBM)


AHEAD = 2
SLOTS = AHEAD + 1
CHUNK = 16
CHUNKS = POS // CHUNK


def chunks_of(count):
    return (count[0] + CHUNK - 1) // CHUNK


def first_kernel(count, place, col_at, row_at, col_place, row_place, left, *rest):
    rights = rest[: 2 * NZ]
    (
        cross, columns, sums, taken, tails, held, picks, parts, norms, made,
        sems, tail_sem, right_sem, out_sem,
    ) = rest[2 * NZ :]
    chunks = chunks_of(count)

    def taken_apart(at):
        value = place[at]
        return value // (256 * SOURCES), value // 256 % SOURCES, value // KB % KB, value % KB

    def moves(i):
        slot = i % SLOTS
        copies = []
        for n in range(CHUNK):
            _, source, k, _ = taken_apart(i * CHUNK + n)
            start = pl.multiple_of(k % HB * BLK, BLK)
            copies.append(
                pltpu.make_async_copy(
                    left.at[source, k // HB, pl.ds(start, BLK)],
                    taken.at[slot, n],
                    sems.at[slot, n],
                )
            )
        return copies

    def away(i):
        slot = i % SLOTS
        to = cross.at[pl.ds(i * CHUNK, CHUNK)]
        return pltpu.make_async_copy(made.at[slot], to, out_sem.at[slot])

    into = [
        pltpu.make_async_copy(rights[i], held.at[i // 2, i % 2], right_sem.at[i])
        for i in range(2 * NZ)
    ]
    tail_copy = pltpu.make_async_copy(
        left.at[:, :, pl.ds(HB * BLK, 2 * HB)], tails, tail_sem
    )
    tail_copy.start()
    for i in range(AHEAD):
        for copy in into[2 * i : 2 * i + 2]:
            copy.start()

        @pl.when(i < chunks)
        def _():
            for copy in moves(i):
                copy.start()

    for copy in into[2 * AHEAD :]:
        copy.start()
    sums[...] = jnp.zeros_like(sums)
    row = lax.broadcasted_iota(jnp.int32, (4 * KB, BLK), 0)
    for k in range(KB):
        ours = (row // (2 * KB) == k // HB) & (row % HB == k % HB)
        picks[k] = jnp.where(ours, -0.5, 0.0).astype(BF16)
    tail_copy.wait()
    for n in range(SOURCES):
        stacked = []
        for h in range(2):
            tail = tails[n, h].astype(F32)
            stacked += [tail[:, 0:BLK], tail[:, BLK:E]]
        parts[n] = jnp.concatenate(stacked, axis=0).T.astype(BF16)

    def last_piece(i):
        return place[i * CHUNK + CHUNK - 1] // (256 * SOURCES)

    def one(i, seen):
        slot = i % SLOTS

        @pl.when(i + AHEAD < chunks)
        def _():
            for copy in moves(i + AHEAD):
                copy.start()

        @pl.when(i >= SLOTS)
        def _():
            away(i - SLOTS).wait()

        needed = last_piece(i)
        for z in range(NZ):

            @pl.when((z > seen) & (z <= needed))
            def _():
                for h in range(2):
                    into[2 * z + h].wait()
                    tail = held[z, h, HB * BLK : HALF, :].astype(F32)
                    norm = tail[0:HB, 0:BLK] + tail[0:HB, BLK:E] + tail[HB : 2 * HB, 0:BLK]
                    norms[z * KB + h * HB : z * KB + (h + 1) * HB, :] = 0.5 * norm

        for copy in moves(i):
            copy.wait()
        rows = []
        for n in range(CHUNK):
            z, source, k, t = taken_apart(i * CHUNK + n)
            off = jnp.where(i * CHUNK + n < count[0], SHIFT2, OFF)
            v = held[z, t // HB, pl.ds(pl.multiple_of(t % HB * BLK, BLK), BLK), :]
            w = dot(taken[slot, n], v, NT) + dot(parts[source], picks[k], NN)
            w = w - norms[pl.ds(z * KB + t, 1), :]
            made[slot, n] = w
            rows.append(jnp.sum(jnp.exp2(w * BETA + off), axis=0, keepdims=True))
        away(i).start()
        sums[pl.ds(pl.multiple_of(i * CHUNK, CHUNK), CHUNK), :] = jnp.concatenate(rows, axis=0)
        return needed

    seen = lax.fori_loop(0, chunks, one, -1)
    columns[...] = exact_sum(spread(col_place[...], NZ * KB), sums[...]).astype(BF16)
    for z in range(NZ):

        @pl.when(z > seen)
        def _():
            for h in range(2):
                into[2 * z + h].wait()

    for n in range(SLOTS):
        i = chunks - 1 - n

        @pl.when(i >= 0)
        def _():
            away(i).wait()


def first_pass(count, place, col_at, row_at, col_place, row_place, left, rights):
    return pl.pallas_call(
        first_kernel,
        in_specs=[SMEM_WHOLE] * 4 + [VMEM_WHOLE] * 2 + [IN_HBM] * (2 * NZ + 1),
        out_specs=[IN_HBM, VMEM_WHOLE],
        scratch_shapes=[
            pltpu.VMEM((POS, BLK), F32),
            pltpu.VMEM((SLOTS, CHUNK, BLK, E), BF16),
            pltpu.VMEM((SOURCES, 2, 2 * HB, E), BF16),
            pltpu.VMEM((NZ, 2, HALF, E), BF16),
            pltpu.VMEM((KB, 4 * KB, BLK), BF16),
            pltpu.VMEM((SOURCES, BLK, 4 * KB), BF16),
            pltpu.VMEM((NZ * KB, BLK), F32),
            pltpu.VMEM((SLOTS, CHUNK, BLK, BLK), F32),
            pltpu.SemaphoreType.DMA((SLOTS, CHUNK)),
            pltpu.SemaphoreType.DMA,
            pltpu.SemaphoreType.DMA((2 * NZ,)),
            pltpu.SemaphoreType.DMA((SLOTS,)),
        ],
        out_shape=[
            pltpu.HBM((POS, BLK, BLK), F32),
            jax.ShapeDtypeStruct((NZ * KB, BLK), BF16),
        ],
        compiler_params=pltpu.CompilerParams(vmem_limit_bytes=GRANT),
    )(count, place, col_at, row_at, col_place, row_place, in_hbm(left), *map(in_hbm, rights))


def total_of(received):
    total = received[0].astype(F32)
    for n in range(1, received.shape[0]):
        total += received[n].astype(F32)
    return total


def one_chunk(source, target, sems, n):
    part = pl.ds(n * CHUNK, CHUNK)
    return pltpu.make_async_copy(source.at[part], target.at[part], sems.at[n])


def start_all(source, target, sems, chunks):
    for n in range(CHUNKS):

        @pl.when(n < chunks)
        def _():
            one_chunk(source, target, sems, n).start()


def second_kernel(
    count, col_at, row_place, received, cross, kernel, rows_out, column_sum,
    cross_here, kernel_here, potential, sums, in_sem, kernel_sem,
):
    chunks = chunks_of(count)
    start_all(cross, cross_here, in_sem, chunks)
    sums[...] = jnp.zeros_like(sums)
    column_sum[...] = total_of(received)
    potential[...] = 2.0 * SHIFT2 - jnp.log2(FLOOR + column_sum[...])
    ones = jnp.ones((16, BLK), BF16)

    @pl.loop(0, chunks)
    def _(step):
        one_chunk(cross, cross_here, in_sem, step).wait()
        rows = []
        for n in range(CHUNK):
            tile = step * CHUNK + n
            off = jnp.where(tile < count[0], 0.0, OFF)
            pot = potential[pl.ds(col_at[tile], 1), :] + off
            w = cross_here[tile]
            rounded = jnp.exp2(w * BETA + pot).astype(BF16)
            kernel_here[tile, 0:BLK, :] = rounded
            kernel_here[tile, BLK : 2 * BLK, :] = (
                rounded.astype(F32) * (w * (-2.0 / E))
            ).astype(BF16)
            rows.append(dot(ones, rounded, NT)[0:1, :])
        one_chunk(kernel_here, kernel, kernel_sem, step).start()
        sums[pl.ds(pl.multiple_of(step * CHUNK, CHUNK), CHUNK), :] = jnp.concatenate(rows, axis=0)

    rows_out[...] = exact_sum(spread(row_place[...], SOURCES * KB), sums[...]).astype(BF16)

    @pl.loop(0, chunks)
    def _(step):
        one_chunk(kernel_here, kernel, kernel_sem, step).wait()


def second_pass(count, col_at, row_place, received, cross):
    return pl.pallas_call(
        second_kernel,
        in_specs=[SMEM_WHOLE, SMEM_WHOLE, VMEM_WHOLE, VMEM_WHOLE, IN_HBM],
        out_specs=[IN_HBM, VMEM_WHOLE, VMEM_WHOLE],
        scratch_shapes=[
            pltpu.VMEM((POS, BLK, BLK), F32),
            pltpu.VMEM((POS, 2 * BLK, BLK), BF16),
            pltpu.VMEM((NZ * KB, BLK), F32),
            pltpu.VMEM((POS, BLK), F32),
            pltpu.SemaphoreType.DMA((CHUNKS,)),
            pltpu.SemaphoreType.DMA((CHUNKS,)),
        ],
        out_shape=[
            pltpu.HBM((POS, 2 * BLK, BLK), BF16),
            jax.ShapeDtypeStruct((SOURCES * KB, BLK), BF16),
            jax.ShapeDtypeStruct((NZ * KB, BLK), F32),
        ],
        compiler_params=pltpu.CompilerParams(vmem_limit_bytes=GRANT),
    )(count, col_at, row_place, received, in_hbm(cross))


def two_parts(row):
    high = row.astype(BF16).astype(F32)
    at = lax.broadcasted_iota(jnp.int32, (16, BLK), 0)
    return jnp.where(at == 0, high, jnp.where(at == 1, row - high, 0.0)).astype(BF16)


def third_kernel(
    count, row_at, col_place, received, kernel, columns, kernel_here, scale, sums, in_sem
):
    chunks = chunks_of(count)
    sums[...] = jnp.zeros_like(sums)
    upper = kernel.at[:, pl.ds(0, BLK)]
    start_all(upper, kernel_here, in_sem, chunks)
    scale[...] = 1.0 / (FLOOR + received[...].astype(F32))

    @pl.loop(0, chunks)
    def _(step):
        one_chunk(upper, kernel_here, in_sem, step).wait()
        rows = []
        for n in range(CHUNK):
            tile = step * CHUNK + n
            both = dot(two_parts(scale[pl.ds(row_at[tile], 1), :]), kernel_here[tile], NN)
            rows.append(both[0:1, :] + both[1:2, :])
        sums[pl.ds(pl.multiple_of(step * CHUNK, CHUNK), CHUNK), :] = jnp.concatenate(rows, axis=0)

    columns[...] = exact_sum(spread(col_place[...], NZ * KB), sums[...]).astype(BF16)


def third_pass(count, row_at, col_place, received, kernel):
    return pl.pallas_call(
        third_kernel,
        in_specs=[SMEM_WHOLE, SMEM_WHOLE, VMEM_WHOLE, VMEM_WHOLE, IN_HBM],
        out_specs=VMEM_WHOLE,
        scratch_shapes=[
            pltpu.VMEM((POS, BLK, BLK), BF16),
            pltpu.VMEM((SOURCES * KB, BLK), F32),
            pltpu.VMEM((POS, BLK), F32),
            pltpu.SemaphoreType.DMA((CHUNKS,)),
        ],
        out_shape=jax.ShapeDtypeStruct((NZ * KB, BLK), BF16),
        compiler_params=pltpu.CompilerParams(vmem_limit_bytes=GRANT),
    )(count, row_at, col_place, received, in_hbm(kernel))


def fourth_kernel(
    count, col_at, row_place, received, column_sum, kernel, rows_out, plan_out,
    kernel_here, scale, sums, weighed, kernel_sem,
):
    chunks = chunks_of(count)
    start_all(kernel, kernel_here, kernel_sem, chunks)
    sums[...] = jnp.zeros_like(sums)
    weighed[...] = jnp.zeros_like(weighed)
    plan_sum = total_of(received)
    plan_out[...] = plan_sum
    scale[...] = 1.0 / (FLOOR / (FLOOR + column_sum[...]) + plan_sum)

    @pl.loop(0, chunks)
    def _(step):
        one_chunk(kernel, kernel_here, kernel_sem, step).wait()
        rows, heavy = [], []
        for n in range(CHUNK):
            tile = step * CHUNK + n
            pair = two_parts(scale[pl.ds(col_at[tile], 1), :])
            both = dot(pair, kernel_here[tile], NT)
            both = both[0:1, :] + both[1:2, :]
            rows.append(both[:, 0:BLK])
            heavy.append(both[:, BLK : 2 * BLK])
        place = pl.ds(pl.multiple_of(step * CHUNK, CHUNK), CHUNK)
        sums[place, :] = jnp.concatenate(rows, axis=0)
        weighed[place, :] = jnp.concatenate(heavy, axis=0)

    which = spread(row_place[...], SOURCES * KB)
    total = exact_sum(which, sums[...])
    heavy_total = exact_sum(which, weighed[...])
    for s in range(SOURCES):
        c, y = s // NY, s % NY
        rows_out[y * NC + c, 0:KB, :] = total[s * KB : (s + 1) * KB, :]
        rows_out[y * NC + c, KB : 2 * KB, :] = heavy_total[s * KB : (s + 1) * KB, :]


def fourth_pass(count, col_at, row_place, received, column_sum, kernel):
    return pl.pallas_call(
        fourth_kernel,
        in_specs=[SMEM_WHOLE] * 2 + [VMEM_WHOLE] * 3 + [IN_HBM],
        out_specs=[VMEM_WHOLE] * 2,
        scratch_shapes=[
            pltpu.VMEM((POS, 2 * BLK, BLK), BF16),
            pltpu.VMEM((NZ * KB, BLK), F32),
            pltpu.VMEM((POS, BLK), F32),
            pltpu.VMEM((POS, BLK), F32),
            pltpu.SemaphoreType.DMA((CHUNKS,)),
        ],
        out_shape=[
            jax.ShapeDtypeStruct((SOURCES, 2 * KB, BLK), F32),
            jax.ShapeDtypeStruct((NZ * KB, BLK), F32),
        ],
        compiler_params=pltpu.CompilerParams(vmem_limit_bytes=GRANT),
    )(count, col_at, row_place, received, column_sum, in_hbm(kernel))


def ring_pieces(block, axis, n):
    up = [(i, (i + 1) % n) for i in range(n)]
    down = [(i, (i - 1) % n) for i in range(n)]
    top, low = block[0], block[1]
    held = [[top, low]] + [[None, None] for _ in range(n - 1)]
    right, left = [top, low], [low, top]
    for k in range(1, n // 2 + 1):
        for i in range(2 if k < n // 2 else 1):
            right[i] = lax.ppermute(right[i], axis, up)
            left[i] = lax.ppermute(left[i], axis, down)
            held[n - k][i] = right[i]
            held[k][1 - i] = left[i]
    return [half for pair in held for half in pair]


def swap(value, axes):
    return lax.all_to_all(value, axes, split_axis=0, concat_axis=0, tiled=True)


def to_all(value, axes, n):
    return swap(jnp.broadcast_to(value[None], (n,) + value.shape), axes)


def columns_to_row(columns):
    over_rep = jnp.sum(to_all(columns, "x", NX).astype(F32), axis=0)
    return to_all(over_rep.astype(BF16), "z", NZ)


def own_columns(columns):
    at = lax.axis_index("z") * KB
    return lax.dynamic_slice_in_dim(columns, at, KB, 0)


def slot_codes(location, pair_block, pair_count):
    slots = pair_block.shape[1]
    stored = location[pair_block.reshape(-1)]
    used = (
        jnp.arange(slots, dtype=jnp.int32)[None, :] < pair_count[:, None]
    ).reshape(-1)
    block = jnp.arange(KB * slots, dtype=jnp.int32) // slots
    owner, local = stored // KB, stored % KB
    holders = jnp.arange(NY * NZ * NC, dtype=jnp.int32)
    match = (owner[None, :] == holders[:, None]) & used[None, :]
    return jnp.max(jnp.where(match, (block * KB + local)[None, :], -1), axis=1)


def in_use(codes):
    at = jnp.arange(POS, dtype=jnp.int32)
    active = codes >= 0
    rank = jnp.sum((active[None, :] & (at[None, :] < at[:, None])).astype(jnp.int32), axis=1)
    count = jnp.sum(active.astype(jnp.int32))
    place = jnp.where(active, at * 256 + codes, 0)
    lands = active[None, :] & (rank[None, :] == at[:, None])
    sorted_ = jnp.max(jnp.where(lands, place[None, :], 0), axis=1)
    used = at < count
    return count.reshape(1), jnp.where(used, sorted_, jnp.max(place)), used


def body(rollout, demo, projection, location, pair_block, pair_count):
    codes = slot_codes(location, pair_block, pair_count)
    codes = codes.reshape(NY, NZ, NC).transpose(0, 2, 1).reshape(SOURCES, NZ)
    codes = swap(codes[:, None, :], ("y", "c")).reshape(SOURCES, NZ)
    turned = (lax.axis_index("z") + jnp.arange(NZ, dtype=jnp.int32)) % NZ
    pick = turned[:, None] == jnp.arange(NZ, dtype=jnp.int32)[None, :]
    codes = jnp.max(jnp.where(pick[:, None, :], codes[None], -1), axis=2)
    count, place, used = in_use(codes.reshape(POS))
    piece, source = place // (256 * SOURCES), place // 256 % SOURCES
    col_at = (lax.axis_index("z") + piece) % NZ * KB + place % KB
    row_at = (source % NC * NY + source // NC) * KB + place // KB % KB
    col_place = jnp.where(used, col_at, -1).reshape(1, POS)
    row_place = jnp.where(used, row_at, -1).reshape(1, POS)

    left = lax.all_gather(project(rollout, projection), ("y", "c"))
    rights = ring_pieces(project(demo, projection), "z", NZ)

    cross, columns = first_pass(
        count, place, col_at, row_at, col_place, row_place, left, rights
    )
    kernel, rows, column_sum = second_pass(
        count, col_at, row_place, columns_to_row(columns), cross
    )
    rows = jnp.sum(swap(rows.reshape(NC, NY * KB, BLK), "c").astype(F32), axis=0)
    rows = jnp.sum(to_all(rows.astype(BF16), "y", NY).astype(F32), axis=0)
    rows = to_all(rows.astype(BF16), "c", NC).reshape(SOURCES * KB, BLK)
    columns = third_pass(count, row_at, col_place, rows, kernel)
    both, plan_sum = fourth_pass(
        count, col_at, row_place, columns_to_row(columns), column_sum, kernel
    )
    both = jnp.sum(swap(both, ("y", "c")), axis=0)
    total = FLOOR + both[:KB]
    reward = -(both[KB:] + UNMATCHED * FLOOR) / total
    roll_pot = EPSILON * (SHIFT - jnp.log(total))
    reached = FLOOR + (FLOOR + own_columns(column_sum)) * own_columns(plan_sum)
    demo_pot = EPSILON * (SHIFT - jnp.log(reached))
    return reward.reshape(-1), roll_pot.reshape(-1), demo_pot.reshape(-1)


def solution(mesh):
    grid = Mesh(mesh.devices.reshape(NY, NZ, NC, NX), ("y", "z", "c", "x"))
    every, roll = ("y", "z", "c", "x"), ("y", "z", "c")
    return jax.shard_map(
        body,
        mesh=grid,
        in_specs=(P(every, None), P(roll, None), P(), P(), P(every, None), P(every)),
        out_specs=(P(every), P(every), P(roll)),
        check_vma=False,
    )
```

```python
import math

import jax
import jax.numpy as jnp
from jax import lax
from jax.experimental import pallas as pl
from jax.experimental.pallas import tpu as pltpu
from jax.sharding import Mesh
from jax.sharding import PartitionSpec as P

EPSILON = 0.02
UNMATCHED = 2.0
SLACK = 100.0
SHIFT = 46.0
LOG2E = 1.4426950408889634
SHIFT2 = SHIFT * LOG2E
FLOOR = math.exp(SHIFT - SLACK)
OFF = -1.0e30

BLK = 128
E = 256
NY, NZ, NC, NX = 8, 8, 2, 4
KB = 16
HB = KB // 2
HALF = HB * BLK + 2 * HB
SOURCES = NY * NC
POS = SOURCES * NZ
ROWS = KB * BLK
PART = 512
BETA = LOG2E * 2.0 / (E * EPSILON)
MIB = 2**20

F32, BF16 = jnp.float32, jnp.bfloat16
NT = (((1,), (1,)), ((), ()))
NN = (((1,), (0,)), ((), ()))
VMEM_WHOLE = pl.BlockSpec(memory_space=pltpu.VMEM)
SMEM_WHOLE = pl.BlockSpec(memory_space=pltpu.SMEM)
IN_HBM = pl.BlockSpec(memory_space=pltpu.HBM)
GRANT = 40 * MIB


def dot(left, right, dims):
    return lax.dot_general(left, right, dims, preferred_element_type=F32)


def exact_sum(onehot, values):
    return lax.dot_general(
        onehot, values, NN, precision=lax.Precision.HIGHEST, preferred_element_type=F32
    )


def spread(places, count):
    rows = lax.broadcasted_iota(jnp.int32, (count, POS), 0)
    return jnp.where(rows == places, 1.0, 0.0)


def norms_of(codes):
    wide = codes.astype(F32)
    square = wide * wide
    high = square.astype(BF16)
    low = (square - high.astype(F32)).astype(BF16)
    ones = jnp.ones((16, E), BF16)
    return (dot(ones, high, NT) + dot(ones, low, NT))[0:1, :]


def three_parts(norm):
    high = norm.astype(BF16).astype(F32)
    middle = (norm - high).astype(BF16).astype(F32)
    return high, middle, norm - high - middle


def codes_kernel(frames, head, out, here, projection, made, sems, head_sem, out_sems):
    def inward(n):
        rows = pl.ds(n * PART, PART)
        return pltpu.make_async_copy(frames.at[rows], here.at[rows], sems.at[n])

    def outward(n):
        rows = pl.ds(n * PART, PART)
        return pltpu.make_async_copy(made.at[rows], out.at[rows], out_sems.at[n])

    head_copy = pltpu.make_async_copy(head, projection, head_sem)
    inward(0).start()
    head_copy.start()
    for n in range(1, ROWS // PART):
        inward(n).start()
    head_copy.wait()
    for n in range(ROWS // PART):
        rows = pl.ds(n * PART, PART)
        inward(n).wait()
        made[rows, :] = dot(here[rows, :], projection[...], NN).astype(BF16)
        outward(n).start()
    for n in range(ROWS // PART):
        outward(n).wait()


def project_codes(frames, projection):
    return pl.pallas_call(
        codes_kernel,
        out_shape=pltpu.HBM((ROWS, E), BF16),
        in_specs=[IN_HBM, IN_HBM],
        out_specs=IN_HBM,
        scratch_shapes=[
            pltpu.VMEM((ROWS, E), BF16),
            pltpu.VMEM((E, E), BF16),
            pltpu.VMEM((ROWS, E), BF16),
            pltpu.SemaphoreType.DMA((ROWS // PART,)),
            pltpu.SemaphoreType.DMA,
            pltpu.SemaphoreType.DMA((ROWS // PART,)),
        ],
        compiler_params=pltpu.CompilerParams(vmem_limit_bytes=GRANT),
    )(in_hbm(frames), in_hbm(projection))


def norms_kernel(codes, after, out):
    for k in range(KB):
        out[k : k + 1, :] = norms_of(codes[pl.ds(k * BLK, BLK), :])


def block_norms(codes, after):
    return pl.pallas_call(
        norms_kernel,
        out_shape=jax.ShapeDtypeStruct((KB, BLK), F32),
        in_specs=[VMEM_WHOLE, IN_HBM],
        out_specs=VMEM_WHOLE,
        compiler_params=pltpu.CompilerParams(vmem_limit_bytes=GRANT),
    )(codes, in_hbm(after))


def parts_kernel(received, parts, picks):
    for n in range(SOURCES):
        stacked = [*three_parts(received[n, 0:KB, :]), jnp.zeros((KB, BLK), F32)]
        parts[n] = jnp.concatenate(stacked, axis=0).T.astype(BF16)
    row = lax.broadcasted_iota(jnp.int32, (4 * KB, BLK), 0)
    for k in range(KB):
        ours = (row % KB == k) & (row < 3 * KB)
        picks[k] = jnp.where(ours, -0.5, 0.0).astype(BF16)


def norm_parts(received):
    return pl.pallas_call(
        parts_kernel,
        out_shape=[
            jax.ShapeDtypeStruct((SOURCES, BLK, 4 * KB), BF16),
            jax.ShapeDtypeStruct((KB, 4 * KB, BLK), BF16),
        ],
        in_specs=[VMEM_WHOLE],
        out_specs=[VMEM_WHOLE] * 2,
        compiler_params=pltpu.CompilerParams(vmem_limit_bytes=GRANT),
    )(received)


def project_kernel(frames, head, out, here, projection, made, norms, sems, head_sem, out_sems):
    def inward(n):
        rows = pl.ds(n * PART, PART)
        return pltpu.make_async_copy(frames.at[rows], here.at[rows], sems.at[n])

    def outward(h):
        return pltpu.make_async_copy(made.at[h], out.at[h], out_sems.at[h])

    head_copy = pltpu.make_async_copy(head, projection, head_sem)
    inward(0).start()
    head_copy.start()
    for n in range(1, ROWS // PART):
        inward(n).start()
    head_copy.wait()
    for h in range(2):
        for j in range(HB):
            k = h * HB + j
            if k * BLK % PART == 0:
                inward(k * BLK // PART).wait()
            codes = dot(here[pl.ds(k * BLK, BLK), :], projection[...], NN).astype(BF16)
            made[h, pl.ds(j * BLK, BLK), :] = codes
            norms[j : j + 1, :] = norms_of(codes)
        high, middle, low = three_parts(norms[...])
        left = jnp.concatenate([high, low], axis=0)
        right = jnp.concatenate([middle, jnp.zeros_like(low)], axis=0)
        made[h, HB * BLK : HALF, :] = jnp.concatenate([left, right], axis=1).astype(BF16)
        outward(h).start()
    for h in range(2):
        outward(h).wait()


def project(frames, projection):
    return pl.pallas_call(
        project_kernel,
        out_shape=pltpu.HBM((2, HALF, E), BF16),
        in_specs=[IN_HBM, IN_HBM],
        out_specs=IN_HBM,
        scratch_shapes=[
            pltpu.VMEM((ROWS, E), BF16),
            pltpu.VMEM((E, E), BF16),
            pltpu.VMEM((2, HALF, E), BF16),
            pltpu.VMEM((HB, BLK), F32),
            pltpu.SemaphoreType.DMA((ROWS // PART,)),
            pltpu.SemaphoreType.DMA,
            pltpu.SemaphoreType.DMA((2,)),
        ],
        compiler_params=pltpu.CompilerParams(vmem_limit_bytes=GRANT),
    )(in_hbm(frames), in_hbm(projection))


def in_hbm(value):
    return pltpu.with_memory_space_constraint(value, pltpu.HBM)


AHEAD = 3
SLOTS = AHEAD + 1
CHUNK = 16
CHUNKS = POS // CHUNK


def chunks_of(count):
    return (count[0] + CHUNK - 1) // CHUNK


def first_kernel(count, place, col_at, row_at, col_place, row_place, parts, picks, left, *rest):
    rights = rest[: 2 * NZ]
    (
        cross, columns, sums, taken, held, norms, made, sems, right_sem, out_sem,
    ) = rest[2 * NZ :]
    chunks = chunks_of(count)

    def taken_apart(at):
        value = place[at]
        return value // (256 * SOURCES), value // 256 % SOURCES, value // KB % KB, value % KB

    def moves(i):
        slot = i % SLOTS
        copies = []
        for n in range(CHUNK):
            _, source, k, _ = taken_apart(i * CHUNK + n)
            start = pl.multiple_of(k * BLK, BLK)
            copies.append(
                pltpu.make_async_copy(
                    left.at[source, pl.ds(start, BLK)],
                    taken.at[slot, n],
                    sems.at[slot, n],
                )
            )
        return copies

    def away(i):
        slot = i % SLOTS
        to = cross.at[pl.ds(i * CHUNK, CHUNK)]
        return pltpu.make_async_copy(made.at[slot], to, out_sem.at[slot])

    into = [
        pltpu.make_async_copy(rights[i], held.at[i // 2, i % 2], right_sem.at[i])
        for i in range(2 * NZ)
    ]
    for i in range(AHEAD):
        for copy in into[2 * i : 2 * i + 2]:
            copy.start()

        @pl.when(i < chunks)
        def _():
            for copy in moves(i):
                copy.start()

    for copy in into[2 * AHEAD :]:
        copy.start()
    sums[...] = jnp.zeros_like(sums)

    def last_piece(i):
        return place[i * CHUNK + CHUNK - 1] // (256 * SOURCES)

    def one(i, seen):
        slot = i % SLOTS

        @pl.when(i + AHEAD < chunks)
        def _():
            for copy in moves(i + AHEAD):
                copy.start()

        @pl.when(i >= SLOTS)
        def _():
            away(i - SLOTS).wait()

        needed = last_piece(i)
        for z in range(NZ):

            @pl.when((z > seen) & (z <= needed))
            def _():
                for h in range(2):
                    into[2 * z + h].wait()
                    tail = held[z, h, HB * BLK : HALF, :].astype(F32)
                    norm = tail[0:HB, 0:BLK] + tail[0:HB, BLK:E] + tail[HB : 2 * HB, 0:BLK]
                    norms[z * KB + h * HB : z * KB + (h + 1) * HB, :] = 0.5 * norm

        for copy in moves(i):
            copy.wait()
        rows = []
        for n in range(CHUNK):
            z, source, k, t = taken_apart(i * CHUNK + n)
            off = jnp.where(i * CHUNK + n < count[0], SHIFT2, OFF)
            v = held[z, t // HB, pl.ds(pl.multiple_of(t % HB * BLK, BLK), BLK), :]
            w = dot(taken[slot, n], v, NT) + dot(parts[source], picks[k], NN)
            w = w - norms[pl.ds(z * KB + t, 1), :]
            made[slot, n] = w
            rows.append(jnp.sum(jnp.exp2(w * BETA + off), axis=0, keepdims=True))
        away(i).start()
        sums[pl.ds(pl.multiple_of(i * CHUNK, CHUNK), CHUNK), :] = jnp.concatenate(rows, axis=0)
        return needed

    seen = lax.fori_loop(0, chunks, one, -1)
    columns[...] = exact_sum(spread(col_place[...], NZ * KB), sums[...]).astype(BF16)
    for z in range(NZ):

        @pl.when(z > seen)
        def _():
            for h in range(2):
                into[2 * z + h].wait()

    for n in range(SLOTS):
        i = chunks - 1 - n

        @pl.when(i >= 0)
        def _():
            away(i).wait()


def first_pass(count, place, col_at, row_at, col_place, row_place, parts, picks, left, rights):
    return pl.pallas_call(
        first_kernel,
        in_specs=[SMEM_WHOLE] * 4 + [VMEM_WHOLE] * 4 + [IN_HBM] * (2 * NZ + 1),
        out_specs=[IN_HBM, VMEM_WHOLE],
        scratch_shapes=[
            pltpu.VMEM((POS, BLK), F32),
            pltpu.VMEM((SLOTS, CHUNK, BLK, E), BF16),
            pltpu.VMEM((NZ, 2, HALF, E), BF16),
            pltpu.VMEM((NZ * KB, BLK), F32),
            pltpu.VMEM((SLOTS, CHUNK, BLK, BLK), F32),
            pltpu.SemaphoreType.DMA((SLOTS, CHUNK)),
            pltpu.SemaphoreType.DMA((2 * NZ,)),
            pltpu.SemaphoreType.DMA((SLOTS,)),
        ],
        out_shape=[
            pltpu.HBM((POS, BLK, BLK), F32),
            jax.ShapeDtypeStruct((NZ * KB, BLK), BF16),
        ],
        compiler_params=pltpu.CompilerParams(vmem_limit_bytes=GRANT),
    )(
        count, place, col_at, row_at, col_place, row_place, parts, picks,
        in_hbm(left), *map(in_hbm, rights),
    )


def total_of(received):
    total = received[0].astype(F32)
    for n in range(1, received.shape[0]):
        total += received[n].astype(F32)
    return total


def one_chunk(source, target, sems, n):
    part = pl.ds(n * CHUNK, CHUNK)
    return pltpu.make_async_copy(source.at[part], target.at[part], sems.at[n])


def start_all(source, target, sems, chunks):
    for n in range(CHUNKS):

        @pl.when(n < chunks)
        def _():
            one_chunk(source, target, sems, n).start()


def second_kernel(
    count, col_at, row_place, received, cross, kernel, rows_out, column_sum,
    cross_here, kernel_here, potential, sums, in_sem, kernel_sem,
):
    chunks = chunks_of(count)
    start_all(cross, cross_here, in_sem, chunks)
    sums[...] = jnp.zeros_like(sums)
    column_sum[...] = total_of(received)
    potential[...] = 2.0 * SHIFT2 - jnp.log2(FLOOR + column_sum[...])
    ones = jnp.ones((16, BLK), BF16)

    @pl.loop(0, chunks)
    def _(step):
        one_chunk(cross, cross_here, in_sem, step).wait()
        rows = []
        for n in range(CHUNK):
            tile = step * CHUNK + n
            off = jnp.where(tile < count[0], 0.0, OFF)
            pot = potential[pl.ds(col_at[tile], 1), :] + off
            w = cross_here[tile]
            rounded = jnp.exp2(w * BETA + pot).astype(BF16)
            kernel_here[tile, 0:BLK, :] = rounded
            kernel_here[tile, BLK : 2 * BLK, :] = (
                rounded.astype(F32) * (w * (-2.0 / E))
            ).astype(BF16)
            rows.append(dot(ones, rounded, NT)[0:1, :])
        one_chunk(kernel_here, kernel, kernel_sem, step).start()
        sums[pl.ds(pl.multiple_of(step * CHUNK, CHUNK), CHUNK), :] = jnp.concatenate(rows, axis=0)

    rows_out[...] = exact_sum(spread(row_place[...], SOURCES * KB), sums[...]).astype(BF16)

    @pl.loop(0, chunks)
    def _(step):
        one_chunk(kernel_here, kernel, kernel_sem, step).wait()


def second_pass(count, col_at, row_place, received, cross):
    return pl.pallas_call(
        second_kernel,
        in_specs=[SMEM_WHOLE, SMEM_WHOLE, VMEM_WHOLE, VMEM_WHOLE, IN_HBM],
        out_specs=[IN_HBM, VMEM_WHOLE, VMEM_WHOLE],
        scratch_shapes=[
            pltpu.VMEM((POS, BLK, BLK), F32),
            pltpu.VMEM((POS, 2 * BLK, BLK), BF16),
            pltpu.VMEM((NZ * KB, BLK), F32),
            pltpu.VMEM((POS, BLK), F32),
            pltpu.SemaphoreType.DMA((CHUNKS,)),
            pltpu.SemaphoreType.DMA((CHUNKS,)),
        ],
        out_shape=[
            pltpu.HBM((POS, 2 * BLK, BLK), BF16),
            jax.ShapeDtypeStruct((SOURCES * KB, BLK), BF16),
            jax.ShapeDtypeStruct((NZ * KB, BLK), F32),
        ],
        compiler_params=pltpu.CompilerParams(vmem_limit_bytes=GRANT),
    )(count, col_at, row_place, received, in_hbm(cross))


def two_parts(row):
    high = row.astype(BF16).astype(F32)
    at = lax.broadcasted_iota(jnp.int32, (16, BLK), 0)
    return jnp.where(at == 0, high, jnp.where(at == 1, row - high, 0.0)).astype(BF16)


def third_kernel(
    count, row_at, col_place, received, kernel, columns, kernel_here, scale, sums, in_sem
):
    chunks = chunks_of(count)
    sums[...] = jnp.zeros_like(sums)
    upper = kernel.at[:, pl.ds(0, BLK)]
    start_all(upper, kernel_here, in_sem, chunks)
    scale[...] = 1.0 / (FLOOR + received[...].astype(F32))

    @pl.loop(0, chunks)
    def _(step):
        one_chunk(upper, kernel_here, in_sem, step).wait()
        rows = []
        for n in range(CHUNK):
            tile = step * CHUNK + n
            both = dot(two_parts(scale[pl.ds(row_at[tile], 1), :]), kernel_here[tile], NN)
            rows.append(both[0:1, :] + both[1:2, :])
        sums[pl.ds(pl.multiple_of(step * CHUNK, CHUNK), CHUNK), :] = jnp.concatenate(rows, axis=0)

    columns[...] = exact_sum(spread(col_place[...], NZ * KB), sums[...]).astype(BF16)


def third_pass(count, row_at, col_place, received, kernel):
    return pl.pallas_call(
        third_kernel,
        in_specs=[SMEM_WHOLE, SMEM_WHOLE, VMEM_WHOLE, VMEM_WHOLE, IN_HBM],
        out_specs=VMEM_WHOLE,
        scratch_shapes=[
            pltpu.VMEM((POS, BLK, BLK), BF16),
            pltpu.VMEM((SOURCES * KB, BLK), F32),
            pltpu.VMEM((POS, BLK), F32),
            pltpu.SemaphoreType.DMA((CHUNKS,)),
        ],
        out_shape=jax.ShapeDtypeStruct((NZ * KB, BLK), BF16),
        compiler_params=pltpu.CompilerParams(vmem_limit_bytes=GRANT),
    )(count, row_at, col_place, received, in_hbm(kernel))


def fourth_kernel(
    count, col_at, row_place, received, column_sum, kernel, rows_out, potential,
    kernel_here, scale, sums, weighed, kernel_sem,
):
    chunks = chunks_of(count)
    start_all(kernel, kernel_here, kernel_sem, chunks)
    sums[...] = jnp.zeros_like(sums)
    weighed[...] = jnp.zeros_like(weighed)
    plan_sum = total_of(received)
    scale[...] = EPSILON * (SHIFT - jnp.log(FLOOR + (FLOOR + column_sum[...]) * plan_sum))
    potential[...] = scale[pl.ds(pl.multiple_of(count[1] * KB, KB), KB), :]
    scale[...] = 1.0 / (FLOOR / (FLOOR + column_sum[...]) + plan_sum)

    @pl.loop(0, chunks)
    def _(step):
        one_chunk(kernel, kernel_here, kernel_sem, step).wait()
        rows, heavy = [], []
        for n in range(CHUNK):
            tile = step * CHUNK + n
            pair = two_parts(scale[pl.ds(col_at[tile], 1), :])
            both = dot(pair, kernel_here[tile], NT)
            both = both[0:1, :] + both[1:2, :]
            rows.append(both[:, 0:BLK])
            heavy.append(both[:, BLK : 2 * BLK])
        place = pl.ds(pl.multiple_of(step * CHUNK, CHUNK), CHUNK)
        sums[place, :] = jnp.concatenate(rows, axis=0)
        weighed[place, :] = jnp.concatenate(heavy, axis=0)

    which = spread(row_place[...], SOURCES * KB)
    total = exact_sum(which, sums[...])
    heavy_total = exact_sum(which, weighed[...])
    for s in range(SOURCES):
        c, y = s // NY, s % NY
        rows_out[y * NC + c, 0:KB, :] = total[s * KB : (s + 1) * KB, :]
        rows_out[y * NC + c, KB : 2 * KB, :] = heavy_total[s * KB : (s + 1) * KB, :]


def fourth_pass(count, col_at, row_place, received, column_sum, kernel):
    return pl.pallas_call(
        fourth_kernel,
        in_specs=[SMEM_WHOLE] * 2 + [VMEM_WHOLE] * 3 + [IN_HBM],
        out_specs=[VMEM_WHOLE] * 2,
        scratch_shapes=[
            pltpu.VMEM((POS, 2 * BLK, BLK), BF16),
            pltpu.VMEM((NZ * KB, BLK), F32),
            pltpu.VMEM((POS, BLK), F32),
            pltpu.VMEM((POS, BLK), F32),
            pltpu.SemaphoreType.DMA((CHUNKS,)),
        ],
        out_shape=[
            jax.ShapeDtypeStruct((SOURCES, 2 * KB, BLK), F32),
            jax.ShapeDtypeStruct((KB, BLK), F32),
        ],
        compiler_params=pltpu.CompilerParams(vmem_limit_bytes=GRANT),
    )(count, col_at, row_place, received, column_sum, in_hbm(kernel))


def ring_pieces(block, axis, n):
    up = [(i, (i + 1) % n) for i in range(n)]
    down = [(i, (i - 1) % n) for i in range(n)]
    top, low = block[0], block[1]
    held = [[top, low]] + [[None, None] for _ in range(n - 1)]
    right, left = [top, low], [low, top]
    for k in range(1, n // 2 + 1):
        for i in range(2 if k < n // 2 else 1):
            right[i] = lax.ppermute(right[i], axis, up)
            left[i] = lax.ppermute(left[i], axis, down)
            held[n - k][i] = right[i]
            held[k][1 - i] = left[i]
    return [half for pair in held for half in pair]


def swap(value, axes):
    return lax.all_to_all(value, axes, split_axis=0, concat_axis=0, tiled=True)


def to_all(value, axes, n):
    return swap(jnp.broadcast_to(value[None], (n,) + value.shape), axes)


def columns_to_row(columns):
    over_rep = jnp.sum(to_all(columns, "x", NX).astype(F32), axis=0)
    return to_all(over_rep.astype(BF16), "z", NZ)


def slot_codes(location, pair_block, pair_count):
    slots = pair_block.shape[1]
    stored = location[pair_block.reshape(-1)]
    used = (
        jnp.arange(slots, dtype=jnp.int32)[None, :] < pair_count[:, None]
    ).reshape(-1)
    block = jnp.arange(KB * slots, dtype=jnp.int32) // slots
    owner, local = stored // KB, stored % KB
    holders = jnp.arange(NY * NZ * NC, dtype=jnp.int32)
    match = (owner[None, :] == holders[:, None]) & used[None, :]
    return jnp.max(jnp.where(match, (block * KB + local)[None, :], -1), axis=1)


def in_use(codes):
    at = jnp.arange(POS, dtype=jnp.int32)
    active = codes >= 0
    rank = jnp.sum((active[None, :] & (at[None, :] < at[:, None])).astype(jnp.int32), axis=1)
    count = jnp.sum(active.astype(jnp.int32))
    place = jnp.where(active, at * 256 + codes, 0)
    lands = active[None, :] & (rank[None, :] == at[:, None])
    sorted_ = jnp.max(jnp.where(lands, place[None, :], 0), axis=1)
    used = at < count
    return count, jnp.where(used, sorted_, jnp.max(place)), used


def body(rollout, demo, projection, location, pair_block, pair_count):
    codes = slot_codes(location, pair_block, pair_count)
    codes = codes.reshape(NY, NZ, NC).transpose(0, 2, 1).reshape(SOURCES, 1, NZ)
    own_codes = project_codes(rollout, projection)
    left = lax.all_gather(own_codes, ("y", "c"))
    rights = ring_pieces(project(demo, projection), "z", NZ)
    norms = jnp.broadcast_to(block_norms(own_codes, rights[-1])[None], (SOURCES, KB, BLK))
    wide = jnp.pad(codes.astype(F32), ((0, 0), (0, 7), (0, BLK - NZ)))
    received = swap(jnp.concatenate([norms, wide], axis=1), ("y", "c"))
    parts, picks = norm_parts(received)
    codes = received[:, KB, :NZ].astype(jnp.int32)
    turned = (lax.axis_index("z") + jnp.arange(NZ, dtype=jnp.int32)) % NZ
    pick = turned[:, None] == jnp.arange(NZ, dtype=jnp.int32)[None, :]
    codes = jnp.max(jnp.where(pick[:, None, :], codes[None], -1), axis=2)
    count, place, used = in_use(codes.reshape(POS))
    count = jnp.stack([count, lax.axis_index("z").astype(jnp.int32)])
    piece, source = place // (256 * SOURCES), place // 256 % SOURCES
    col_at = (lax.axis_index("z") + piece) % NZ * KB + place % KB
    row_at = (source % NC * NY + source // NC) * KB + place // KB % KB
    col_place = jnp.where(used, col_at, -1).reshape(1, POS)
    row_place = jnp.where(used, row_at, -1).reshape(1, POS)


    cross, columns = first_pass(
        count, place, col_at, row_at, col_place, row_place, parts, picks, left, rights
    )
    kernel, rows, column_sum = second_pass(
        count, col_at, row_place, columns_to_row(columns), cross
    )
    rows = jnp.sum(swap(rows.reshape(NC, NY * KB, BLK), "c").astype(F32), axis=0)
    rows = jnp.sum(to_all(rows.astype(BF16), "y", NY).astype(F32), axis=0)
    rows = to_all(rows.astype(BF16), "c", NC).reshape(SOURCES * KB, BLK)
    columns = third_pass(count, row_at, col_place, rows, kernel)
    both, demo_pot = fourth_pass(
        count, col_at, row_place, columns_to_row(columns), column_sum, kernel
    )
    both = jnp.sum(swap(both, ("y", "c")), axis=0)
    total = FLOOR + both[:KB]
    reward = -(both[KB:] + UNMATCHED * FLOOR) / total
    roll_pot = EPSILON * (SHIFT - jnp.log(total))
    return reward.reshape(-1), roll_pot.reshape(-1), demo_pot.reshape(-1)


def solution(mesh):
    grid = Mesh(mesh.devices.reshape(NY, NZ, NC, NX), ("y", "z", "c", "x"))
    every, roll = ("y", "z", "c", "x"), ("y", "z", "c")
    return jax.shard_map(
        body,
        mesh=grid,
        in_specs=(P(every, None), P(roll, None), P(), P(), P(every, None), P(every)),
        out_specs=(P(every), P(every), P(roll)),
        check_vma=False,
    )
```

```python
import math

import jax
import jax.numpy as jnp
from jax import lax
from jax.experimental import pallas as pl
from jax.experimental.pallas import tpu as pltpu
from jax.sharding import Mesh
from jax.sharding import PartitionSpec as P

EPSILON = 0.02
UNMATCHED = 2.0
SLACK = 100.0
SHIFT = 46.0
LOG2E = 1.4426950408889634
SHIFT2 = SHIFT * LOG2E
FLOOR = math.exp(SHIFT - SLACK)
OFF = -1.0e30

BLK = 128
E = 256
NY, NZ, NC, NX = 8, 8, 2, 4
KB = 16
HB = KB // 2
HALF = HB * BLK + 2 * HB
SOURCES = NY * NC
POS = SOURCES * NZ
ROWS = KB * BLK
PART = 512
BETA = LOG2E * 2.0 / (E * EPSILON)
MIB = 2**20

F32, BF16 = jnp.float32, jnp.bfloat16
NT = (((1,), (1,)), ((), ()))
NN = (((1,), (0,)), ((), ()))
VMEM_WHOLE = pl.BlockSpec(memory_space=pltpu.VMEM)
SMEM_WHOLE = pl.BlockSpec(memory_space=pltpu.SMEM)
IN_HBM = pl.BlockSpec(memory_space=pltpu.HBM)
GRANT = 40 * MIB


def dot(left, right, dims):
    return lax.dot_general(left, right, dims, preferred_element_type=F32)


def exact_sum(onehot, values):
    return lax.dot_general(
        onehot, values, NN, precision=lax.Precision.HIGHEST, preferred_element_type=F32
    )


def spread(places, count):
    rows = lax.broadcasted_iota(jnp.int32, (count, POS), 0)
    return jnp.where(rows == places, 1.0, 0.0)


def norms_of(codes):
    wide = codes.astype(F32)
    square = wide * wide
    high = square.astype(BF16)
    low = (square - high.astype(F32)).astype(BF16)
    ones = jnp.ones((16, E), BF16)
    return (dot(ones, high, NT) + dot(ones, low, NT))[0:1, :]


def three_parts(norm):
    high = norm.astype(BF16).astype(F32)
    middle = (norm - high).astype(BF16).astype(F32)
    return high, middle, norm - high - middle


def codes_kernel(frames, head, out, here, projection, made, sems, head_sem, out_sems):
    def inward(n):
        rows = pl.ds(n * PART, PART)
        return pltpu.make_async_copy(frames.at[rows], here.at[rows], sems.at[n])

    def outward(n):
        rows = pl.ds(n * PART, PART)
        return pltpu.make_async_copy(made.at[rows], out.at[rows], out_sems.at[n])

    head_copy = pltpu.make_async_copy(head, projection, head_sem)
    inward(0).start()
    head_copy.start()
    for n in range(1, ROWS // PART):
        inward(n).start()
    head_copy.wait()
    for n in range(ROWS // PART):
        rows = pl.ds(n * PART, PART)
        inward(n).wait()
        made[rows, :] = dot(here[rows, :], projection[...], NN).astype(BF16)
        outward(n).start()
    for n in range(ROWS // PART):
        outward(n).wait()


def project_codes(frames, projection):
    return pl.pallas_call(
        codes_kernel,
        out_shape=pltpu.HBM((ROWS, E), BF16),
        in_specs=[IN_HBM, IN_HBM],
        out_specs=IN_HBM,
        scratch_shapes=[
            pltpu.VMEM((ROWS, E), BF16),
            pltpu.VMEM((E, E), BF16),
            pltpu.VMEM((ROWS, E), BF16),
            pltpu.SemaphoreType.DMA((ROWS // PART,)),
            pltpu.SemaphoreType.DMA,
            pltpu.SemaphoreType.DMA((ROWS // PART,)),
        ],
        compiler_params=pltpu.CompilerParams(vmem_limit_bytes=GRANT),
    )(in_hbm(frames), in_hbm(projection))


def norms_kernel(codes, after, out):
    for k in range(KB):
        out[k : k + 1, :] = norms_of(codes[pl.ds(k * BLK, BLK), :])


def block_norms(codes, after):
    return pl.pallas_call(
        norms_kernel,
        out_shape=jax.ShapeDtypeStruct((KB, BLK), F32),
        in_specs=[VMEM_WHOLE, IN_HBM],
        out_specs=VMEM_WHOLE,
        compiler_params=pltpu.CompilerParams(vmem_limit_bytes=GRANT),
    )(codes, in_hbm(after))


def parts_kernel(received, parts, picks):
    for n in range(SOURCES):
        stacked = [*three_parts(received[n, 0:KB, :]), jnp.zeros((KB, BLK), F32)]
        parts[n] = jnp.concatenate(stacked, axis=0).T.astype(BF16)
    row = lax.broadcasted_iota(jnp.int32, (4 * KB, BLK), 0)
    for k in range(KB):
        ours = (row % KB == k) & (row < 3 * KB)
        picks[k] = jnp.where(ours, -0.5, 0.0).astype(BF16)


def norm_parts(received):
    return pl.pallas_call(
        parts_kernel,
        out_shape=[
            jax.ShapeDtypeStruct((SOURCES, BLK, 4 * KB), BF16),
            jax.ShapeDtypeStruct((KB, 4 * KB, BLK), BF16),
        ],
        in_specs=[VMEM_WHOLE],
        out_specs=[VMEM_WHOLE] * 2,
        compiler_params=pltpu.CompilerParams(vmem_limit_bytes=GRANT),
    )(received)


def project_kernel(frames, head, out, here, projection, made, norms, sems, head_sem, out_sems):
    def inward(n):
        rows = pl.ds(n * PART, PART)
        return pltpu.make_async_copy(frames.at[rows], here.at[rows], sems.at[n])

    def outward(h):
        return pltpu.make_async_copy(made.at[h], out.at[h], out_sems.at[h])

    head_copy = pltpu.make_async_copy(head, projection, head_sem)
    inward(0).start()
    head_copy.start()
    for n in range(1, ROWS // PART):
        inward(n).start()
    head_copy.wait()
    for h in range(2):
        for j in range(HB):
            k = h * HB + j
            if k * BLK % PART == 0:
                inward(k * BLK // PART).wait()
            codes = dot(here[pl.ds(k * BLK, BLK), :], projection[...], NN).astype(BF16)
            made[h, pl.ds(j * BLK, BLK), :] = codes
            norms[j : j + 1, :] = norms_of(codes)
        high, middle, low = three_parts(norms[...])
        left = jnp.concatenate([high, low], axis=0)
        right = jnp.concatenate([middle, jnp.zeros_like(low)], axis=0)
        made[h, HB * BLK : HALF, :] = jnp.concatenate([left, right], axis=1).astype(BF16)
        outward(h).start()
    for h in range(2):
        outward(h).wait()


def project(frames, projection):
    return pl.pallas_call(
        project_kernel,
        out_shape=pltpu.HBM((2, HALF, E), BF16),
        in_specs=[IN_HBM, IN_HBM],
        out_specs=IN_HBM,
        scratch_shapes=[
            pltpu.VMEM((ROWS, E), BF16),
            pltpu.VMEM((E, E), BF16),
            pltpu.VMEM((2, HALF, E), BF16),
            pltpu.VMEM((HB, BLK), F32),
            pltpu.SemaphoreType.DMA((ROWS // PART,)),
            pltpu.SemaphoreType.DMA,
            pltpu.SemaphoreType.DMA((2,)),
        ],
        compiler_params=pltpu.CompilerParams(vmem_limit_bytes=GRANT),
    )(in_hbm(frames), in_hbm(projection))


def in_hbm(value):
    return pltpu.with_memory_space_constraint(value, pltpu.HBM)


AHEAD = 3
SLOTS = AHEAD + 1
CHUNK = 16
CHUNKS = POS // CHUNK


def chunks_of(count):
    return (count[0] + CHUNK - 1) // CHUNK


def first_kernel(count, place, col_at, row_at, col_place, row_place, parts, picks, left, *rest):
    rights = rest[: 2 * NZ]
    (
        cross, columns, sums, taken, held, norms, made, sems, right_sem, out_sem,
    ) = rest[2 * NZ :]
    chunks = chunks_of(count)

    def taken_apart(at):
        value = place[at]
        return value // (256 * SOURCES), value // 256 % SOURCES, value // KB % KB, value % KB

    def moves(i):
        slot = i % SLOTS
        copies = []
        for n in range(CHUNK):
            _, source, k, _ = taken_apart(i * CHUNK + n)
            start = pl.multiple_of(k * BLK, BLK)
            copies.append(
                pltpu.make_async_copy(
                    left.at[source, pl.ds(start, BLK)],
                    taken.at[slot, n],
                    sems.at[slot, n],
                )
            )
        return copies

    def away(i):
        slot = i % SLOTS
        to = cross.at[pl.ds(i * CHUNK, CHUNK)]
        return pltpu.make_async_copy(made.at[slot], to, out_sem.at[slot])

    into = [
        pltpu.make_async_copy(rights[i], held.at[i // 2, i % 2], right_sem.at[i])
        for i in range(2 * NZ)
    ]
    for i in range(AHEAD):
        for copy in into[2 * i : 2 * i + 2]:
            copy.start()

        @pl.when(i < chunks)
        def _():
            for copy in moves(i):
                copy.start()

    for copy in into[2 * AHEAD :]:
        copy.start()
    sums[...] = jnp.zeros_like(sums)

    def last_piece(i):
        return place[i * CHUNK + CHUNK - 1] // (256 * SOURCES)

    def one(i, seen):
        slot = i % SLOTS

        @pl.when(i + AHEAD < chunks)
        def _():
            for copy in moves(i + AHEAD):
                copy.start()

        @pl.when(i >= SLOTS)
        def _():
            away(i - SLOTS).wait()

        needed = last_piece(i)
        for z in range(NZ):

            @pl.when((z > seen) & (z <= needed))
            def _():
                for h in range(2):
                    into[2 * z + h].wait()
                    tail = held[z, h, HB * BLK : HALF, :].astype(F32)
                    norm = tail[0:HB, 0:BLK] + tail[0:HB, BLK:E] + tail[HB : 2 * HB, 0:BLK]
                    norms[z * KB + h * HB : z * KB + (h + 1) * HB, :] = 0.5 * norm

        for copy in moves(i):
            copy.wait()
        rows = []
        for n in range(CHUNK):
            z, source, k, t = taken_apart(i * CHUNK + n)
            off = jnp.where(i * CHUNK + n < count[0], SHIFT2, OFF)
            v = held[z, t // HB, pl.ds(pl.multiple_of(t % HB * BLK, BLK), BLK), :]
            w = dot(taken[slot, n], v, NT) + dot(parts[source], picks[k], NN)
            w = w - norms[pl.ds(z * KB + t, 1), :]
            made[slot, n] = w
            rows.append(jnp.sum(jnp.exp2(w * BETA + off), axis=0, keepdims=True))
        away(i).start()
        sums[pl.ds(pl.multiple_of(i * CHUNK, CHUNK), CHUNK), :] = jnp.concatenate(rows, axis=0)
        return needed

    seen = lax.fori_loop(0, chunks, one, -1)
    columns[...] = exact_sum(spread(col_place[...], NZ * KB), sums[...]).astype(BF16)
    for z in range(NZ):

        @pl.when(z > seen)
        def _():
            for h in range(2):
                into[2 * z + h].wait()

    for n in range(SLOTS):
        i = chunks - 1 - n

        @pl.when(i >= 0)
        def _():
            away(i).wait()


def first_pass(count, place, col_at, row_at, col_place, row_place, parts, picks, left, rights):
    return pl.pallas_call(
        first_kernel,
        in_specs=[SMEM_WHOLE] * 4 + [VMEM_WHOLE] * 4 + [IN_HBM] * (2 * NZ + 1),
        out_specs=[IN_HBM, VMEM_WHOLE],
        scratch_shapes=[
            pltpu.VMEM((POS, BLK), F32),
            pltpu.VMEM((SLOTS, CHUNK, BLK, E), BF16),
            pltpu.VMEM((NZ, 2, HALF, E), BF16),
            pltpu.VMEM((NZ * KB, BLK), F32),
            pltpu.VMEM((SLOTS, CHUNK, BLK, BLK), F32),
            pltpu.SemaphoreType.DMA((SLOTS, CHUNK)),
            pltpu.SemaphoreType.DMA((2 * NZ,)),
            pltpu.SemaphoreType.DMA((SLOTS,)),
        ],
        out_shape=[
            pltpu.HBM((POS, BLK, BLK), F32),
            jax.ShapeDtypeStruct((NZ * KB, BLK), BF16),
        ],
        compiler_params=pltpu.CompilerParams(vmem_limit_bytes=GRANT),
    )(
        count, place, col_at, row_at, col_place, row_place, parts, picks,
        in_hbm(left), *map(in_hbm, rights),
    )


def total_of(received):
    total = received[0].astype(F32)
    for n in range(1, received.shape[0]):
        total += received[n].astype(F32)
    return total


def one_chunk(source, target, sems, n):
    part = pl.ds(n * CHUNK, CHUNK)
    return pltpu.make_async_copy(source.at[part], target.at[part], sems.at[n])


def start_all(source, target, sems, chunks):
    for n in range(CHUNKS):

        @pl.when(n < chunks)
        def _():
            one_chunk(source, target, sems, n).start()


def second_kernel(
    count, col_at, row_place, received, cross, kernel, rows_out, column_sum,
    cross_here, kernel_here, potential, sums, in_sem, kernel_sem,
):
    chunks = chunks_of(count)
    start_all(cross, cross_here, in_sem, chunks)
    sums[...] = jnp.zeros_like(sums)
    column_sum[...] = total_of(received)
    potential[...] = 2.0 * SHIFT2 - jnp.log2(FLOOR + column_sum[...])
    ones = jnp.ones((16, BLK), BF16)

    @pl.loop(0, chunks)
    def _(step):
        one_chunk(cross, cross_here, in_sem, step).wait()
        rows = []
        for n in range(CHUNK):
            tile = step * CHUNK + n
            off = jnp.where(tile < count[0], 0.0, OFF)
            pot = potential[pl.ds(col_at[tile], 1), :] + off
            w = cross_here[tile]
            rounded = jnp.exp2(w * BETA + pot).astype(BF16)
            kernel_here[tile, 0:BLK, :] = rounded
            kernel_here[tile, BLK : 2 * BLK, :] = (
                rounded.astype(F32) * (w * (-2.0 / E))
            ).astype(BF16)
            rows.append(dot(ones, rounded, NT)[0:1, :])
        one_chunk(kernel_here, kernel, kernel_sem, step).start()
        sums[pl.ds(pl.multiple_of(step * CHUNK, CHUNK), CHUNK), :] = jnp.concatenate(rows, axis=0)

    rows_out[...] = exact_sum(spread(row_place[...], SOURCES * KB), sums[...]).astype(BF16)

    @pl.loop(0, chunks)
    def _(step):
        one_chunk(kernel_here, kernel, kernel_sem, step).wait()


def second_pass(count, col_at, row_place, received, cross):
    return pl.pallas_call(
        second_kernel,
        in_specs=[SMEM_WHOLE, SMEM_WHOLE, VMEM_WHOLE, VMEM_WHOLE, IN_HBM],
        out_specs=[IN_HBM, VMEM_WHOLE, VMEM_WHOLE],
        scratch_shapes=[
            pltpu.VMEM((POS, BLK, BLK), F32),
            pltpu.VMEM((POS, 2 * BLK, BLK), BF16),
            pltpu.VMEM((NZ * KB, BLK), F32),
            pltpu.VMEM((POS, BLK), F32),
            pltpu.SemaphoreType.DMA((CHUNKS,)),
            pltpu.SemaphoreType.DMA((CHUNKS,)),
        ],
        out_shape=[
            pltpu.HBM((POS, 2 * BLK, BLK), BF16),
            jax.ShapeDtypeStruct((SOURCES * KB, BLK), BF16),
            jax.ShapeDtypeStruct((NZ * KB, BLK), F32),
        ],
        compiler_params=pltpu.CompilerParams(vmem_limit_bytes=GRANT),
    )(count, col_at, row_place, received, in_hbm(cross))


def two_parts(row):
    high = row.astype(BF16).astype(F32)
    at = lax.broadcasted_iota(jnp.int32, (16, BLK), 0)
    return jnp.where(at == 0, high, jnp.where(at == 1, row - high, 0.0)).astype(BF16)


def third_kernel(
    count, row_at, col_place, received, kernel, columns, kernel_here, scale, sums, in_sem
):
    chunks = chunks_of(count)
    sums[...] = jnp.zeros_like(sums)
    upper = kernel.at[:, pl.ds(0, BLK)]
    start_all(upper, kernel_here, in_sem, chunks)
    scale[...] = 1.0 / (FLOOR + received[...].astype(F32))

    @pl.loop(0, chunks)
    def _(step):
        one_chunk(upper, kernel_here, in_sem, step).wait()
        rows = []
        for n in range(CHUNK):
            tile = step * CHUNK + n
            both = dot(two_parts(scale[pl.ds(row_at[tile], 1), :]), kernel_here[tile], NN)
            rows.append(both[0:1, :] + both[1:2, :])
        sums[pl.ds(pl.multiple_of(step * CHUNK, CHUNK), CHUNK), :] = jnp.concatenate(rows, axis=0)

    columns[...] = exact_sum(spread(col_place[...], NZ * KB), sums[...]).astype(BF16)


def third_pass(count, row_at, col_place, received, kernel):
    return pl.pallas_call(
        third_kernel,
        in_specs=[SMEM_WHOLE, SMEM_WHOLE, VMEM_WHOLE, VMEM_WHOLE, IN_HBM],
        out_specs=VMEM_WHOLE,
        scratch_shapes=[
            pltpu.VMEM((POS, BLK, BLK), BF16),
            pltpu.VMEM((SOURCES * KB, BLK), F32),
            pltpu.VMEM((POS, BLK), F32),
            pltpu.SemaphoreType.DMA((CHUNKS,)),
        ],
        out_shape=jax.ShapeDtypeStruct((NZ * KB, BLK), BF16),
        compiler_params=pltpu.CompilerParams(vmem_limit_bytes=GRANT),
    )(count, row_at, col_place, received, in_hbm(kernel))


def fourth_kernel(
    count, col_at, row_place, received, column_sum, kernel, rows_out, potential,
    kernel_here, scale, sums, weighed, kernel_sem,
):
    chunks = chunks_of(count)
    start_all(kernel, kernel_here, kernel_sem, chunks)
    sums[...] = jnp.zeros_like(sums)
    weighed[...] = jnp.zeros_like(weighed)
    plan_sum = total_of(received)
    scale[...] = EPSILON * (SHIFT - jnp.log(FLOOR + (FLOOR + column_sum[...]) * plan_sum))
    potential[...] = scale[pl.ds(pl.multiple_of(count[1] * KB, KB), KB), :]
    scale[...] = 1.0 / (FLOOR / (FLOOR + column_sum[...]) + plan_sum)

    @pl.loop(0, chunks)
    def _(step):
        one_chunk(kernel, kernel_here, kernel_sem, step).wait()
        rows, heavy = [], []
        for n in range(CHUNK):
            tile = step * CHUNK + n
            pair = two_parts(scale[pl.ds(col_at[tile], 1), :])
            both = dot(pair, kernel_here[tile], NT)
            both = both[0:1, :] + both[1:2, :]
            rows.append(both[:, 0:BLK])
            heavy.append(both[:, BLK : 2 * BLK])
        place = pl.ds(pl.multiple_of(step * CHUNK, CHUNK), CHUNK)
        sums[place, :] = jnp.concatenate(rows, axis=0)
        weighed[place, :] = jnp.concatenate(heavy, axis=0)

    which = spread(row_place[...], SOURCES * KB)
    total = exact_sum(which, sums[...])
    heavy_total = exact_sum(which, weighed[...])
    for s in range(SOURCES):
        c, y = s // NY, s % NY
        rows_out[y * NC + c, 0:KB, :] = total[s * KB : (s + 1) * KB, :]
        rows_out[y * NC + c, KB : 2 * KB, :] = heavy_total[s * KB : (s + 1) * KB, :]


def fourth_pass(count, col_at, row_place, received, column_sum, kernel):
    return pl.pallas_call(
        fourth_kernel,
        in_specs=[SMEM_WHOLE] * 2 + [VMEM_WHOLE] * 3 + [IN_HBM],
        out_specs=[VMEM_WHOLE] * 2,
        scratch_shapes=[
            pltpu.VMEM((POS, 2 * BLK, BLK), BF16),
            pltpu.VMEM((NZ * KB, BLK), F32),
            pltpu.VMEM((POS, BLK), F32),
            pltpu.VMEM((POS, BLK), F32),
            pltpu.SemaphoreType.DMA((CHUNKS,)),
        ],
        out_shape=[
            jax.ShapeDtypeStruct((SOURCES, 2 * KB, BLK), F32),
            jax.ShapeDtypeStruct((KB, BLK), F32),
        ],
        compiler_params=pltpu.CompilerParams(vmem_limit_bytes=GRANT),
    )(count, col_at, row_place, received, column_sum, in_hbm(kernel))


def ring_pieces(block, axis, n):
    up = [(i, (i + 1) % n) for i in range(n)]
    down = [(i, (i - 1) % n) for i in range(n)]
    top, low = block[0], block[1]
    held = [[top, low]] + [[None, None] for _ in range(n - 1)]
    right, left = [top, low], [low, top]
    for k in range(1, n // 2 + 1):
        for i in range(2 if k < n // 2 else 1):
            right[i] = lax.ppermute(right[i], axis, up)
            left[i] = lax.ppermute(left[i], axis, down)
            held[n - k][i] = right[i]
            held[k][1 - i] = left[i]
    return [half for pair in held for half in pair]


def swap(value, axes):
    return lax.all_to_all(value, axes, split_axis=0, concat_axis=0, tiled=True)


def to_all(value, axes, n):
    return swap(jnp.broadcast_to(value[None], (n,) + value.shape), axes)


def columns_to_row(columns):
    over_rep = jnp.sum(to_all(columns, "x", NX).astype(F32), axis=0)
    return to_all(over_rep.astype(BF16), "z", NZ)


def slot_codes(location, pair_block, pair_count):
    slots = pair_block.shape[1]
    stored = location[pair_block.reshape(-1)]
    used = (
        jnp.arange(slots, dtype=jnp.int32)[None, :] < pair_count[:, None]
    ).reshape(-1)
    block = jnp.arange(KB * slots, dtype=jnp.int32) // slots
    owner, local = stored // KB, stored % KB
    holders = jnp.arange(NY * NZ * NC, dtype=jnp.int32)
    match = (owner[None, :] == holders[:, None]) & used[None, :]
    return jnp.max(jnp.where(match, (block * KB + local)[None, :], -1), axis=1)


def in_use(codes):
    at = jnp.arange(POS, dtype=jnp.int32)
    active = codes >= 0
    rank = jnp.sum((active[None, :] & (at[None, :] < at[:, None])).astype(jnp.int32), axis=1)
    count = jnp.sum(active.astype(jnp.int32))
    place = jnp.where(active, at * 256 + codes, 0)
    lands = active[None, :] & (rank[None, :] == at[:, None])
    sorted_ = jnp.max(jnp.where(lands, place[None, :], 0), axis=1)
    used = at < count
    return count, jnp.where(used, sorted_, jnp.max(place)), used


def body(rollout, demo, projection, location, pair_block, pair_count):
    codes = slot_codes(location, pair_block, pair_count)
    codes = codes.reshape(NY, NZ, NC).transpose(0, 2, 1).reshape(SOURCES, 1, NZ)
    codes = swap(codes, ("y", "c")).reshape(SOURCES, NZ)
    own_codes = project_codes(rollout, projection)
    left = lax.all_gather(own_codes, ("y", "c"))
    rights = ring_pieces(project(demo, projection), "z", NZ)
    norms = block_norms(own_codes, rights[2 * (NZ - 3) + 1])
    parts, picks = norm_parts(to_all(norms, ("y", "c"), SOURCES))
    turned = (lax.axis_index("z") + jnp.arange(NZ, dtype=jnp.int32)) % NZ
    pick = turned[:, None] == jnp.arange(NZ, dtype=jnp.int32)[None, :]
    codes = jnp.max(jnp.where(pick[:, None, :], codes[None], -1), axis=2)
    count, place, used = in_use(codes.reshape(POS))
    count = jnp.stack([count, lax.axis_index("z").astype(jnp.int32)])
    piece, source = place // (256 * SOURCES), place // 256 % SOURCES
    col_at = (lax.axis_index("z") + piece) % NZ * KB + place % KB
    row_at = (source % NC * NY + source // NC) * KB + place // KB % KB
    col_place = jnp.where(used, col_at, -1).reshape(1, POS)
    row_place = jnp.where(used, row_at, -1).reshape(1, POS)


    cross, columns = first_pass(
        count, place, col_at, row_at, col_place, row_place, parts, picks, left, rights
    )
    kernel, rows, column_sum = second_pass(
        count, col_at, row_place, columns_to_row(columns), cross
    )
    rows = jnp.sum(swap(rows.reshape(NC, NY * KB, BLK), "c").astype(F32), axis=0)
    rows = jnp.sum(to_all(rows.astype(BF16), "y", NY).astype(F32), axis=0)
    rows = to_all(rows.astype(BF16), "c", NC).reshape(SOURCES * KB, BLK)
    columns = third_pass(count, row_at, col_place, rows, kernel)
    both, demo_pot = fourth_pass(
        count, col_at, row_place, columns_to_row(columns), column_sum, kernel
    )
    both = jnp.sum(swap(both, ("y", "c")), axis=0)
    total = FLOOR + both[:KB]
    reward = -(both[KB:] + UNMATCHED * FLOOR) / total
    roll_pot = EPSILON * (SHIFT - jnp.log(total))
    return reward.reshape(-1), roll_pot.reshape(-1), demo_pot.reshape(-1)


def solution(mesh):
    grid = Mesh(mesh.devices.reshape(NY, NZ, NC, NX), ("y", "z", "c", "x"))
    every, roll = ("y", "z", "c", "x"), ("y", "z", "c")
    return jax.shard_map(
        body,
        mesh=grid,
        in_specs=(P(every, None), P(roll, None), P(), P(), P(every, None), P(every)),
        out_specs=(P(every), P(every), P(roll)),
        check_vma=False,
    )
```

```python
import math

import jax
import jax.numpy as jnp
from jax import lax
from jax.experimental import pallas as pl
from jax.experimental.pallas import tpu as pltpu
from jax.sharding import Mesh
from jax.sharding import PartitionSpec as P

EPSILON = 0.02
UNMATCHED = 2.0
SLACK = 100.0
SHIFT = 46.0
LOG2E = 1.4426950408889634
SHIFT2 = SHIFT * LOG2E
FLOOR = math.exp(SHIFT - SLACK)
OFF = -1.0e30

BLK = 128
E = 256
NY, NZ, NC, NX = 8, 8, 2, 4
KB = 16
HB = KB // 2
HALF = HB * BLK + 2 * HB
SOURCES = NY * NC
POS = SOURCES * NZ
ROWS = KB * BLK
PART = 512
BETA = LOG2E * 2.0 / (E * EPSILON)
MIB = 2**20

F32, BF16 = jnp.float32, jnp.bfloat16
NT = (((1,), (1,)), ((), ()))
NN = (((1,), (0,)), ((), ()))
VMEM_WHOLE = pl.BlockSpec(memory_space=pltpu.VMEM)
SMEM_WHOLE = pl.BlockSpec(memory_space=pltpu.SMEM)
IN_HBM = pl.BlockSpec(memory_space=pltpu.HBM)
GRANT = 40 * MIB


def dot(left, right, dims):
    return lax.dot_general(left, right, dims, preferred_element_type=F32)


def exact_sum(onehot, values):
    return lax.dot_general(
        onehot, values, NN, precision=lax.Precision.HIGHEST, preferred_element_type=F32
    )


def spread(places, count):
    rows = lax.broadcasted_iota(jnp.int32, (count, POS), 0)
    return jnp.where(rows == places, 1.0, 0.0)


def norms_of(codes):
    wide = codes.astype(F32)
    square = wide * wide
    high = square.astype(BF16)
    low = (square - high.astype(F32)).astype(BF16)
    ones = jnp.ones((16, E), BF16)
    return (dot(ones, high, NT) + dot(ones, low, NT))[0:1, :]


def three_parts(norm):
    high = norm.astype(BF16).astype(F32)
    middle = (norm - high).astype(BF16).astype(F32)
    return high, middle, norm - high - middle


def codes_kernel(frames, head, out, here, projection, made, sems, head_sem, out_sems):
    def inward(n):
        rows = pl.ds(n * PART, PART)
        return pltpu.make_async_copy(frames.at[rows], here.at[rows], sems.at[n])

    def outward(n):
        rows = pl.ds(n * PART, PART)
        return pltpu.make_async_copy(made.at[rows], out.at[rows], out_sems.at[n])

    head_copy = pltpu.make_async_copy(head, projection, head_sem)
    inward(0).start()
    head_copy.start()
    for n in range(1, ROWS // PART):
        inward(n).start()
    head_copy.wait()
    for n in range(ROWS // PART):
        rows = pl.ds(n * PART, PART)
        inward(n).wait()
        made[rows, :] = dot(here[rows, :], projection[...], NN).astype(BF16)
        outward(n).start()
    for n in range(ROWS // PART):
        outward(n).wait()


def project_codes(frames, projection):
    return pl.pallas_call(
        codes_kernel,
        out_shape=pltpu.HBM((ROWS, E), BF16),
        in_specs=[IN_HBM, IN_HBM],
        out_specs=IN_HBM,
        scratch_shapes=[
            pltpu.VMEM((ROWS, E), BF16),
            pltpu.VMEM((E, E), BF16),
            pltpu.VMEM((ROWS, E), BF16),
            pltpu.SemaphoreType.DMA((ROWS // PART,)),
            pltpu.SemaphoreType.DMA,
            pltpu.SemaphoreType.DMA((ROWS // PART,)),
        ],
        compiler_params=pltpu.CompilerParams(vmem_limit_bytes=GRANT),
    )(in_hbm(frames), in_hbm(projection))


def norms_kernel(codes, after, out):
    for k in range(KB):
        out[k : k + 1, :] = norms_of(codes[pl.ds(k * BLK, BLK), :])


def block_norms(codes, after):
    return pl.pallas_call(
        norms_kernel,
        out_shape=jax.ShapeDtypeStruct((KB, BLK), F32),
        in_specs=[VMEM_WHOLE, pl.BlockSpec(memory_space=pl.ANY)],
        out_specs=VMEM_WHOLE,
        compiler_params=pltpu.CompilerParams(vmem_limit_bytes=GRANT),
    )(codes, after)


def parts_kernel(received, parts, picks):
    for n in range(SOURCES):
        stacked = [*three_parts(received[n, 0:KB, :]), jnp.zeros((KB, BLK), F32)]
        parts[n] = jnp.concatenate(stacked, axis=0).T.astype(BF16)
    row = lax.broadcasted_iota(jnp.int32, (4 * KB, BLK), 0)
    for k in range(KB):
        ours = (row % KB == k) & (row < 3 * KB)
        picks[k] = jnp.where(ours, -0.5, 0.0).astype(BF16)


def norm_parts(received):
    return pl.pallas_call(
        parts_kernel,
        out_shape=[
            jax.ShapeDtypeStruct((SOURCES, BLK, 4 * KB), BF16),
            jax.ShapeDtypeStruct((KB, 4 * KB, BLK), BF16),
        ],
        in_specs=[VMEM_WHOLE],
        out_specs=[VMEM_WHOLE] * 2,
        compiler_params=pltpu.CompilerParams(vmem_limit_bytes=GRANT),
    )(received)


def project_kernel(frames, head, out, here, projection, made, norms, sems, head_sem, out_sems):
    def inward(n):
        rows = pl.ds(n * PART, PART)
        return pltpu.make_async_copy(frames.at[rows], here.at[rows], sems.at[n])

    def outward(h):
        return pltpu.make_async_copy(made.at[h], out.at[h], out_sems.at[h])

    head_copy = pltpu.make_async_copy(head, projection, head_sem)
    inward(0).start()
    head_copy.start()
    for n in range(1, ROWS // PART):
        inward(n).start()
    head_copy.wait()
    for h in range(2):
        for j in range(HB):
            k = h * HB + j
            if k * BLK % PART == 0:
                inward(k * BLK // PART).wait()
            codes = dot(here[pl.ds(k * BLK, BLK), :], projection[...], NN).astype(BF16)
            made[h, pl.ds(j * BLK, BLK), :] = codes
            norms[j : j + 1, :] = norms_of(codes)
        high, middle, low = three_parts(norms[...])
        left = jnp.concatenate([high, low], axis=0)
        right = jnp.concatenate([middle, jnp.zeros_like(low)], axis=0)
        made[h, HB * BLK : HALF, :] = jnp.concatenate([left, right], axis=1).astype(BF16)
        outward(h).start()
    for h in range(2):
        outward(h).wait()


def project(frames, projection):
    return pl.pallas_call(
        project_kernel,
        out_shape=pltpu.HBM((2, HALF, E), BF16),
        in_specs=[IN_HBM, IN_HBM],
        out_specs=IN_HBM,
        scratch_shapes=[
            pltpu.VMEM((ROWS, E), BF16),
            pltpu.VMEM((E, E), BF16),
            pltpu.VMEM((2, HALF, E), BF16),
            pltpu.VMEM((HB, BLK), F32),
            pltpu.SemaphoreType.DMA((ROWS // PART,)),
            pltpu.SemaphoreType.DMA,
            pltpu.SemaphoreType.DMA((2,)),
        ],
        compiler_params=pltpu.CompilerParams(vmem_limit_bytes=GRANT),
    )(in_hbm(frames), in_hbm(projection))


def in_hbm(value):
    return pltpu.with_memory_space_constraint(value, pltpu.HBM)


AHEAD = 3
SLOTS = AHEAD + 1
CHUNK = 16
CHUNKS = POS // CHUNK


def chunks_of(count):
    return (count[0] + CHUNK - 1) // CHUNK


def first_kernel(count, place, col_at, row_at, col_place, row_place, parts, picks, left, *rest):
    rights = rest[: 2 * NZ]
    (
        cross, columns, sums, taken, held, norms, made, sems, right_sem, out_sem,
    ) = rest[2 * NZ :]
    chunks = chunks_of(count)

    def taken_apart(at):
        value = place[at]
        return value // (256 * SOURCES), value // 256 % SOURCES, value // KB % KB, value % KB

    def moves(i):
        slot = i % SLOTS
        copies = []
        for n in range(CHUNK):
            _, source, k, _ = taken_apart(i * CHUNK + n)
            start = pl.multiple_of(k * BLK, BLK)
            copies.append(
                pltpu.make_async_copy(
                    left.at[source, pl.ds(start, BLK)],
                    taken.at[slot, n],
                    sems.at[slot, n],
                )
            )
        return copies

    def away(i):
        slot = i % SLOTS
        to = cross.at[pl.ds(i * CHUNK, CHUNK)]
        return pltpu.make_async_copy(made.at[slot], to, out_sem.at[slot])

    into = [
        pltpu.make_async_copy(rights[i], held.at[i // 2, i % 2], right_sem.at[i])
        for i in range(2 * NZ)
    ]
    for i in range(AHEAD):
        for copy in into[2 * i : 2 * i + 2]:
            copy.start()

        @pl.when(i < chunks)
        def _():
            for copy in moves(i):
                copy.start()

    for copy in into[2 * AHEAD :]:
        copy.start()
    sums[...] = jnp.zeros_like(sums)

    def last_piece(i):
        return place[i * CHUNK + CHUNK - 1] // (256 * SOURCES)

    def one(i, seen):
        slot = i % SLOTS

        @pl.when(i + AHEAD < chunks)
        def _():
            for copy in moves(i + AHEAD):
                copy.start()

        @pl.when(i >= SLOTS)
        def _():
            away(i - SLOTS).wait()

        needed = last_piece(i)
        for z in range(NZ):

            @pl.when((z > seen) & (z <= needed))
            def _():
                for h in range(2):
                    into[2 * z + h].wait()
                    tail = held[z, h, HB * BLK : HALF, :].astype(F32)
                    norm = tail[0:HB, 0:BLK] + tail[0:HB, BLK:E] + tail[HB : 2 * HB, 0:BLK]
                    norms[z * KB + h * HB : z * KB + (h + 1) * HB, :] = 0.5 * norm

        for copy in moves(i):
            copy.wait()
        rows = []
        for n in range(CHUNK):
            z, source, k, t = taken_apart(i * CHUNK + n)
            off = jnp.where(i * CHUNK + n < count[0], SHIFT2, OFF)
            v = held[z, t // HB, pl.ds(pl.multiple_of(t % HB * BLK, BLK), BLK), :]
            w = dot(taken[slot, n], v, NT) + dot(parts[source], picks[k], NN)
            w = w - norms[pl.ds(z * KB + t, 1), :]
            made[slot, n] = w
            rows.append(jnp.sum(jnp.exp2(w * BETA + off), axis=0, keepdims=True))
        away(i).start()
        sums[pl.ds(pl.multiple_of(i * CHUNK, CHUNK), CHUNK), :] = jnp.concatenate(rows, axis=0)
        return needed

    seen = lax.fori_loop(0, chunks, one, -1)
    columns[...] = exact_sum(spread(col_place[...], NZ * KB), sums[...]).astype(BF16)
    for z in range(NZ):

        @pl.when(z > seen)
        def _():
            for h in range(2):
                into[2 * z + h].wait()

    for n in range(SLOTS):
        i = chunks - 1 - n

        @pl.when(i >= 0)
        def _():
            away(i).wait()


def first_pass(count, place, col_at, row_at, col_place, row_place, parts, picks, left, rights):
    return pl.pallas_call(
        first_kernel,
        in_specs=[SMEM_WHOLE] * 4 + [VMEM_WHOLE] * 4 + [IN_HBM] * (2 * NZ + 1),
        out_specs=[IN_HBM, VMEM_WHOLE],
        scratch_shapes=[
            pltpu.VMEM((POS, BLK), F32),
            pltpu.VMEM((SLOTS, CHUNK, BLK, E), BF16),
            pltpu.VMEM((NZ, 2, HALF, E), BF16),
            pltpu.VMEM((NZ * KB, BLK), F32),
            pltpu.VMEM((SLOTS, CHUNK, BLK, BLK), F32),
            pltpu.SemaphoreType.DMA((SLOTS, CHUNK)),
            pltpu.SemaphoreType.DMA((2 * NZ,)),
            pltpu.SemaphoreType.DMA((SLOTS,)),
        ],
        out_shape=[
            pltpu.HBM((POS, BLK, BLK), F32),
            jax.ShapeDtypeStruct((NZ * KB, BLK), BF16),
        ],
        compiler_params=pltpu.CompilerParams(vmem_limit_bytes=GRANT),
    )(
        count, place, col_at, row_at, col_place, row_place, parts, picks,
        in_hbm(left), *map(in_hbm, rights),
    )


def total_of(received):
    total = received[0].astype(F32)
    for n in range(1, received.shape[0]):
        total += received[n].astype(F32)
    return total


def one_chunk(source, target, sems, n):
    part = pl.ds(n * CHUNK, CHUNK)
    return pltpu.make_async_copy(source.at[part], target.at[part], sems.at[n])


def start_all(source, target, sems, chunks):
    for n in range(CHUNKS):

        @pl.when(n < chunks)
        def _():
            one_chunk(source, target, sems, n).start()


def second_kernel(
    count, col_at, row_place, received, cross, kernel, rows_out, column_sum,
    cross_here, kernel_here, potential, sums, in_sem, kernel_sem,
):
    chunks = chunks_of(count)
    start_all(cross, cross_here, in_sem, chunks)
    sums[...] = jnp.zeros_like(sums)
    column_sum[...] = total_of(received)
    potential[...] = 2.0 * SHIFT2 - jnp.log2(FLOOR + column_sum[...])
    ones = jnp.ones((16, BLK), BF16)

    @pl.loop(0, chunks)
    def _(step):
        one_chunk(cross, cross_here, in_sem, step).wait()
        rows = []
        for n in range(CHUNK):
            tile = step * CHUNK + n
            off = jnp.where(tile < count[0], 0.0, OFF)
            pot = potential[pl.ds(col_at[tile], 1), :] + off
            w = cross_here[tile]
            rounded = jnp.exp2(w * BETA + pot).astype(BF16)
            kernel_here[tile, 0:BLK, :] = rounded
            kernel_here[tile, BLK : 2 * BLK, :] = (
                rounded.astype(F32) * (w * (-2.0 / E))
            ).astype(BF16)
            rows.append(dot(ones, rounded, NT)[0:1, :])
        one_chunk(kernel_here, kernel, kernel_sem, step).start()
        sums[pl.ds(pl.multiple_of(step * CHUNK, CHUNK), CHUNK), :] = jnp.concatenate(rows, axis=0)

    rows_out[...] = exact_sum(spread(row_place[...], SOURCES * KB), sums[...]).astype(BF16)

    @pl.loop(0, chunks)
    def _(step):
        one_chunk(kernel_here, kernel, kernel_sem, step).wait()


def second_pass(count, col_at, row_place, received, cross):
    return pl.pallas_call(
        second_kernel,
        in_specs=[SMEM_WHOLE, SMEM_WHOLE, VMEM_WHOLE, VMEM_WHOLE, IN_HBM],
        out_specs=[IN_HBM, VMEM_WHOLE, VMEM_WHOLE],
        scratch_shapes=[
            pltpu.VMEM((POS, BLK, BLK), F32),
            pltpu.VMEM((POS, 2 * BLK, BLK), BF16),
            pltpu.VMEM((NZ * KB, BLK), F32),
            pltpu.VMEM((POS, BLK), F32),
            pltpu.SemaphoreType.DMA((CHUNKS,)),
            pltpu.SemaphoreType.DMA((CHUNKS,)),
        ],
        out_shape=[
            pltpu.HBM((POS, 2 * BLK, BLK), BF16),
            jax.ShapeDtypeStruct((SOURCES * KB, BLK), BF16),
            jax.ShapeDtypeStruct((NZ * KB, BLK), F32),
        ],
        compiler_params=pltpu.CompilerParams(vmem_limit_bytes=GRANT),
    )(count, col_at, row_place, received, in_hbm(cross))


def two_parts(row):
    high = row.astype(BF16).astype(F32)
    at = lax.broadcasted_iota(jnp.int32, (16, BLK), 0)
    return jnp.where(at == 0, high, jnp.where(at == 1, row - high, 0.0)).astype(BF16)


def third_kernel(
    count, row_at, col_place, received, kernel, columns, kernel_here, scale, sums, in_sem
):
    chunks = chunks_of(count)
    sums[...] = jnp.zeros_like(sums)
    upper = kernel.at[:, pl.ds(0, BLK)]
    start_all(upper, kernel_here, in_sem, chunks)
    scale[...] = 1.0 / (FLOOR + received[...].astype(F32))

    @pl.loop(0, chunks)
    def _(step):
        one_chunk(upper, kernel_here, in_sem, step).wait()
        rows = []
        for n in range(CHUNK):
            tile = step * CHUNK + n
            both = dot(two_parts(scale[pl.ds(row_at[tile], 1), :]), kernel_here[tile], NN)
            rows.append(both[0:1, :] + both[1:2, :])
        sums[pl.ds(pl.multiple_of(step * CHUNK, CHUNK), CHUNK), :] = jnp.concatenate(rows, axis=0)

    columns[...] = exact_sum(spread(col_place[...], NZ * KB), sums[...]).astype(BF16)


def third_pass(count, row_at, col_place, received, kernel):
    return pl.pallas_call(
        third_kernel,
        in_specs=[SMEM_WHOLE, SMEM_WHOLE, VMEM_WHOLE, VMEM_WHOLE, IN_HBM],
        out_specs=VMEM_WHOLE,
        scratch_shapes=[
            pltpu.VMEM((POS, BLK, BLK), BF16),
            pltpu.VMEM((SOURCES * KB, BLK), F32),
            pltpu.VMEM((POS, BLK), F32),
            pltpu.SemaphoreType.DMA((CHUNKS,)),
        ],
        out_shape=jax.ShapeDtypeStruct((NZ * KB, BLK), BF16),
        compiler_params=pltpu.CompilerParams(vmem_limit_bytes=GRANT),
    )(count, row_at, col_place, received, in_hbm(kernel))


def fourth_kernel(
    count, col_at, row_place, received, column_sum, kernel, rows_out, potential,
    kernel_here, scale, sums, weighed, kernel_sem,
):
    chunks = chunks_of(count)
    start_all(kernel, kernel_here, kernel_sem, chunks)
    sums[...] = jnp.zeros_like(sums)
    weighed[...] = jnp.zeros_like(weighed)
    plan_sum = total_of(received)
    scale[...] = EPSILON * (SHIFT - jnp.log(FLOOR + (FLOOR + column_sum[...]) * plan_sum))
    potential[...] = scale[pl.ds(pl.multiple_of(count[1] * KB, KB), KB), :]
    scale[...] = 1.0 / (FLOOR / (FLOOR + column_sum[...]) + plan_sum)

    @pl.loop(0, chunks)
    def _(step):
        one_chunk(kernel, kernel_here, kernel_sem, step).wait()
        rows, heavy = [], []
        for n in range(CHUNK):
            tile = step * CHUNK + n
            pair = two_parts(scale[pl.ds(col_at[tile], 1), :])
            both = dot(pair, kernel_here[tile], NT)
            both = both[0:1, :] + both[1:2, :]
            rows.append(both[:, 0:BLK])
            heavy.append(both[:, BLK : 2 * BLK])
        place = pl.ds(pl.multiple_of(step * CHUNK, CHUNK), CHUNK)
        sums[place, :] = jnp.concatenate(rows, axis=0)
        weighed[place, :] = jnp.concatenate(heavy, axis=0)

    which = spread(row_place[...], SOURCES * KB)
    total = exact_sum(which, sums[...])
    heavy_total = exact_sum(which, weighed[...])
    for s in range(SOURCES):
        c, y = s // NY, s % NY
        rows_out[y * NC + c, 0:KB, :] = total[s * KB : (s + 1) * KB, :]
        rows_out[y * NC + c, KB : 2 * KB, :] = heavy_total[s * KB : (s + 1) * KB, :]


def fourth_pass(count, col_at, row_place, received, column_sum, kernel):
    return pl.pallas_call(
        fourth_kernel,
        in_specs=[SMEM_WHOLE] * 2 + [VMEM_WHOLE] * 3 + [IN_HBM],
        out_specs=[VMEM_WHOLE] * 2,
        scratch_shapes=[
            pltpu.VMEM((POS, 2 * BLK, BLK), BF16),
            pltpu.VMEM((NZ * KB, BLK), F32),
            pltpu.VMEM((POS, BLK), F32),
            pltpu.VMEM((POS, BLK), F32),
            pltpu.SemaphoreType.DMA((CHUNKS,)),
        ],
        out_shape=[
            jax.ShapeDtypeStruct((SOURCES, 2 * KB, BLK), F32),
            jax.ShapeDtypeStruct((KB, BLK), F32),
        ],
        compiler_params=pltpu.CompilerParams(vmem_limit_bytes=GRANT),
    )(count, col_at, row_place, received, column_sum, in_hbm(kernel))


def ring_pieces(block, axis, n):
    up = [(i, (i + 1) % n) for i in range(n)]
    down = [(i, (i - 1) % n) for i in range(n)]
    top, low = block[0], block[1]
    held = [[top, low]] + [[None, None] for _ in range(n - 1)]
    right, left = [top, low], [low, top]
    for k in range(1, n // 2 + 1):
        for i in range(2 if k < n // 2 else 1):
            right[i] = lax.ppermute(right[i], axis, up)
            left[i] = lax.ppermute(left[i], axis, down)
            held[n - k][i] = right[i]
            held[k][1 - i] = left[i]
    return [half for pair in held for half in pair]


def swap(value, axes):
    return lax.all_to_all(value, axes, split_axis=0, concat_axis=0, tiled=True)


def to_all(value, axes, n):
    return swap(jnp.broadcast_to(value[None], (n,) + value.shape), axes)


def columns_to_row(columns):
    over_rep = jnp.sum(to_all(columns, "x", NX).astype(F32), axis=0)
    return to_all(over_rep.astype(BF16), "z", NZ)


def slot_codes(location, pair_block, pair_count):
    slots = pair_block.shape[1]
    stored = location[pair_block.reshape(-1)]
    used = (
        jnp.arange(slots, dtype=jnp.int32)[None, :] < pair_count[:, None]
    ).reshape(-1)
    block = jnp.arange(KB * slots, dtype=jnp.int32) // slots
    owner, local = stored // KB, stored % KB
    holders = jnp.arange(NY * NZ * NC, dtype=jnp.int32)
    match = (owner[None, :] == holders[:, None]) & used[None, :]
    return jnp.max(jnp.where(match, (block * KB + local)[None, :], -1), axis=1)


def in_use(codes):
    at = jnp.arange(POS, dtype=jnp.int32)
    active = codes >= 0
    rank = jnp.sum((active[None, :] & (at[None, :] < at[:, None])).astype(jnp.int32), axis=1)
    count = jnp.sum(active.astype(jnp.int32))
    place = jnp.where(active, at * 256 + codes, 0)
    lands = active[None, :] & (rank[None, :] == at[:, None])
    sorted_ = jnp.max(jnp.where(lands, place[None, :], 0), axis=1)
    used = at < count
    return count, jnp.where(used, sorted_, jnp.max(place)), used


def body(rollout, demo, projection, location, pair_block, pair_count):
    codes = slot_codes(location, pair_block, pair_count)
    codes = codes.reshape(NY, NZ, NC).transpose(0, 2, 1).reshape(SOURCES, 1, NZ)
    codes = swap(codes, ("y", "c")).reshape(SOURCES, NZ)
    own_codes = project_codes(rollout, projection)
    left = lax.all_gather(own_codes, ("y", "c"))
    rights = ring_pieces(project(demo, projection), "z", NZ)
    norms = block_norms(own_codes, rights[2 * (NZ - 2) + 1])
    parts, picks = norm_parts(to_all(norms, ("y", "c"), SOURCES))
    turned = (lax.axis_index("z") + jnp.arange(NZ, dtype=jnp.int32)) % NZ
    pick = turned[:, None] == jnp.arange(NZ, dtype=jnp.int32)[None, :]
    codes = jnp.max(jnp.where(pick[:, None, :], codes[None], -1), axis=2)
    count, place, used = in_use(codes.reshape(POS))
    count = jnp.stack([count, lax.axis_index("z").astype(jnp.int32)])
    piece, source = place // (256 * SOURCES), place // 256 % SOURCES
    col_at = (lax.axis_index("z") + piece) % NZ * KB + place % KB
    row_at = (source % NC * NY + source // NC) * KB + place // KB % KB
    col_place = jnp.where(used, col_at, -1).reshape(1, POS)
    row_place = jnp.where(used, row_at, -1).reshape(1, POS)


    cross, columns = first_pass(
        count, place, col_at, row_at, col_place, row_place, parts, picks, left, rights
    )
    kernel, rows, column_sum = second_pass(
        count, col_at, row_place, columns_to_row(columns), cross
    )
    rows = jnp.sum(swap(rows.reshape(NC, NY * KB, BLK), "c").astype(F32), axis=0)
    rows = jnp.sum(to_all(rows.astype(BF16), "y", NY).astype(F32), axis=0)
    rows = to_all(rows.astype(BF16), "c", NC).reshape(SOURCES * KB, BLK)
    columns = third_pass(count, row_at, col_place, rows, kernel)
    both, demo_pot = fourth_pass(
        count, col_at, row_place, columns_to_row(columns), column_sum, kernel
    )
    both = jnp.sum(swap(both, ("y", "c")), axis=0)
    total = FLOOR + both[:KB]
    reward = -(both[KB:] + UNMATCHED * FLOOR) / total
    roll_pot = EPSILON * (SHIFT - jnp.log(total))
    return reward.reshape(-1), roll_pot.reshape(-1), demo_pot.reshape(-1)


def solution(mesh):
    grid = Mesh(mesh.devices.reshape(NY, NZ, NC, NX), ("y", "z", "c", "x"))
    every, roll = ("y", "z", "c", "x"), ("y", "z", "c")
    return jax.shard_map(
        body,
        mesh=grid,
        in_specs=(P(every, None), P(roll, None), P(), P(), P(every, None), P(every)),
        out_specs=(P(every), P(every), P(roll)),
        check_vma=False,
    )
```

```python
import math

import jax
import jax.numpy as jnp
from jax import lax
from jax.experimental import pallas as pl
from jax.experimental.pallas import tpu as pltpu
from jax.sharding import Mesh
from jax.sharding import PartitionSpec as P

EPSILON = 0.02
UNMATCHED = 2.0
SLACK = 100.0
SHIFT = 46.0
LOG2E = 1.4426950408889634
SHIFT2 = SHIFT * LOG2E
FLOOR = math.exp(SHIFT - SLACK)
OFF = -1.0e30

BLK = 128
E = 256
NY, NZ, NC, NX = 8, 8, 2, 4
KB = 16
HB = KB // 2
HALF = HB * BLK + 2 * HB
SOURCES = NY * NC
POS = SOURCES * NZ
ROWS = KB * BLK
PART = 512
BETA = LOG2E * 2.0 / (E * EPSILON)
MIB = 2**20

F32, BF16 = jnp.float32, jnp.bfloat16
NT = (((1,), (1,)), ((), ()))
NN = (((1,), (0,)), ((), ()))
VMEM_WHOLE = pl.BlockSpec(memory_space=pltpu.VMEM)
SMEM_WHOLE = pl.BlockSpec(memory_space=pltpu.SMEM)
IN_HBM = pl.BlockSpec(memory_space=pltpu.HBM)
GRANT = 40 * MIB


def dot(left, right, dims):
    return lax.dot_general(left, right, dims, preferred_element_type=F32)


def exact_sum(onehot, values):
    return lax.dot_general(
        onehot, values, NN, precision=lax.Precision.HIGHEST, preferred_element_type=F32
    )


def spread(places, count):
    rows = lax.broadcasted_iota(jnp.int32, (count, POS), 0)
    return jnp.where(rows == places, 1.0, 0.0)


def norms_of(codes):
    wide = codes.astype(F32)
    square = wide * wide
    high = square.astype(BF16)
    low = (square - high.astype(F32)).astype(BF16)
    ones = jnp.ones((16, E), BF16)
    return (dot(ones, high, NT) + dot(ones, low, NT))[0:1, :]


def three_parts(norm):
    high = norm.astype(BF16).astype(F32)
    middle = (norm - high).astype(BF16).astype(F32)
    return high, middle, norm - high - middle


def codes_kernel(frames, head, out, here, projection, made, sems, head_sem, out_sems):
    def inward(n):
        rows = pl.ds(n * PART, PART)
        return pltpu.make_async_copy(frames.at[rows], here.at[rows], sems.at[n])

    def outward(n):
        rows = pl.ds(n * PART, PART)
        return pltpu.make_async_copy(made.at[rows], out.at[rows], out_sems.at[n])

    head_copy = pltpu.make_async_copy(head, projection, head_sem)
    inward(0).start()
    head_copy.start()
    for n in range(1, ROWS // PART):
        inward(n).start()
    head_copy.wait()
    for n in range(ROWS // PART):
        rows = pl.ds(n * PART, PART)
        inward(n).wait()
        made[rows, :] = dot(here[rows, :], projection[...], NN).astype(BF16)
        outward(n).start()
    for n in range(ROWS // PART):
        outward(n).wait()


def project_codes(frames, projection):
    return pl.pallas_call(
        codes_kernel,
        out_shape=pltpu.HBM((ROWS, E), BF16),
        in_specs=[IN_HBM, IN_HBM],
        out_specs=IN_HBM,
        scratch_shapes=[
            pltpu.VMEM((ROWS, E), BF16),
            pltpu.VMEM((E, E), BF16),
            pltpu.VMEM((ROWS, E), BF16),
            pltpu.SemaphoreType.DMA((ROWS // PART,)),
            pltpu.SemaphoreType.DMA,
            pltpu.SemaphoreType.DMA((ROWS // PART,)),
        ],
        compiler_params=pltpu.CompilerParams(vmem_limit_bytes=GRANT),
    )(in_hbm(frames), in_hbm(projection))


def norms_kernel(codes, after, out):
    for k in range(KB):
        out[k : k + 1, :] = norms_of(codes[pl.ds(k * BLK, BLK), :])


def block_norms(codes, after):
    return pl.pallas_call(
        norms_kernel,
        out_shape=jax.ShapeDtypeStruct((KB, BLK), F32),
        in_specs=[VMEM_WHOLE, pl.BlockSpec(memory_space=pl.ANY)],
        out_specs=VMEM_WHOLE,
        compiler_params=pltpu.CompilerParams(vmem_limit_bytes=GRANT),
    )(codes, after)


def parts_kernel(received, parts, picks):
    for n in range(SOURCES):
        stacked = [*three_parts(received[n, 0:KB, :]), jnp.zeros((KB, BLK), F32)]
        parts[n] = jnp.concatenate(stacked, axis=0).T.astype(BF16)
    row = lax.broadcasted_iota(jnp.int32, (4 * KB, BLK), 0)
    for k in range(KB):
        ours = (row % KB == k) & (row < 3 * KB)
        picks[k] = jnp.where(ours, -0.5, 0.0).astype(BF16)


def norm_parts(received):
    return pl.pallas_call(
        parts_kernel,
        out_shape=[
            jax.ShapeDtypeStruct((SOURCES, BLK, 4 * KB), BF16),
            jax.ShapeDtypeStruct((KB, 4 * KB, BLK), BF16),
        ],
        in_specs=[VMEM_WHOLE],
        out_specs=[VMEM_WHOLE] * 2,
        compiler_params=pltpu.CompilerParams(vmem_limit_bytes=GRANT),
    )(received)


def project_kernel(frames, head, top, bottom, here, projection, made, norms, sems, head_sem, out_sems):
    def inward(n):
        rows = pl.ds(n * PART, PART)
        return pltpu.make_async_copy(frames.at[rows], here.at[rows], sems.at[n])

    def outward(h):
        return pltpu.make_async_copy(made.at[h], (top, bottom)[h], out_sems.at[h])

    head_copy = pltpu.make_async_copy(head, projection, head_sem)
    inward(0).start()
    head_copy.start()
    for n in range(1, ROWS // PART):
        inward(n).start()
    head_copy.wait()
    for h in range(2):
        for j in range(HB):
            k = h * HB + j
            if k * BLK % PART == 0:
                inward(k * BLK // PART).wait()
            codes = dot(here[pl.ds(k * BLK, BLK), :], projection[...], NN).astype(BF16)
            made[h, pl.ds(j * BLK, BLK), :] = codes
            norms[j : j + 1, :] = norms_of(codes)
        high, middle, low = three_parts(norms[...])
        left = jnp.concatenate([high, low], axis=0)
        right = jnp.concatenate([middle, jnp.zeros_like(low)], axis=0)
        made[h, HB * BLK : HALF, :] = jnp.concatenate([left, right], axis=1).astype(BF16)
        outward(h).start()
    for h in range(2):
        outward(h).wait()


def project(frames, projection):
    return pl.pallas_call(
        project_kernel,
        out_shape=[pltpu.HBM((HALF, E), BF16)] * 2,
        in_specs=[IN_HBM, IN_HBM],
        out_specs=[IN_HBM] * 2,
        scratch_shapes=[
            pltpu.VMEM((ROWS, E), BF16),
            pltpu.VMEM((E, E), BF16),
            pltpu.VMEM((2, HALF, E), BF16),
            pltpu.VMEM((HB, BLK), F32),
            pltpu.SemaphoreType.DMA((ROWS // PART,)),
            pltpu.SemaphoreType.DMA,
            pltpu.SemaphoreType.DMA((2,)),
        ],
        compiler_params=pltpu.CompilerParams(vmem_limit_bytes=GRANT),
    )(in_hbm(frames), in_hbm(projection))


def in_hbm(value):
    return pltpu.with_memory_space_constraint(value, pltpu.HBM)


AHEAD = 3
SLOTS = AHEAD + 1
CHUNK = 16
CHUNKS = POS // CHUNK


def chunks_of(count):
    return (count[0] + CHUNK - 1) // CHUNK


def first_kernel(count, place, col_at, row_at, col_place, row_place, parts, picks, left, *rest):
    rights = rest[: 2 * NZ]
    (
        cross, columns, sums, taken, held, norms, made, sems, right_sem, out_sem,
    ) = rest[2 * NZ :]
    chunks = chunks_of(count)

    def taken_apart(at):
        value = place[at]
        return value // (256 * SOURCES), value // 256 % SOURCES, value // KB % KB, value % KB

    def moves(i):
        slot = i % SLOTS
        copies = []
        for n in range(CHUNK):
            _, source, k, _ = taken_apart(i * CHUNK + n)
            start = pl.multiple_of(k * BLK, BLK)
            copies.append(
                pltpu.make_async_copy(
                    left.at[source, pl.ds(start, BLK)],
                    taken.at[slot, n],
                    sems.at[slot, n],
                )
            )
        return copies

    def away(i):
        slot = i % SLOTS
        to = cross.at[pl.ds(i * CHUNK, CHUNK)]
        return pltpu.make_async_copy(made.at[slot], to, out_sem.at[slot])

    into = [
        pltpu.make_async_copy(rights[i], held.at[i // 2, i % 2], right_sem.at[i])
        for i in range(2 * NZ)
    ]
    for i in range(AHEAD):
        for copy in into[2 * i : 2 * i + 2]:
            copy.start()

        @pl.when(i < chunks)
        def _():
            for copy in moves(i):
                copy.start()

    for copy in into[2 * AHEAD :]:
        copy.start()
    sums[...] = jnp.zeros_like(sums)

    def last_piece(i):
        return place[i * CHUNK + CHUNK - 1] // (256 * SOURCES)

    def one(i, seen):
        slot = i % SLOTS

        @pl.when(i + AHEAD < chunks)
        def _():
            for copy in moves(i + AHEAD):
                copy.start()

        @pl.when(i >= SLOTS)
        def _():
            away(i - SLOTS).wait()

        needed = last_piece(i)
        for z in range(NZ):

            @pl.when((z > seen) & (z <= needed))
            def _():
                for h in range(2):
                    into[2 * z + h].wait()
                    tail = held[z, h, HB * BLK : HALF, :].astype(F32)
                    norm = tail[0:HB, 0:BLK] + tail[0:HB, BLK:E] + tail[HB : 2 * HB, 0:BLK]
                    norms[z * KB + h * HB : z * KB + (h + 1) * HB, :] = 0.5 * norm

        for copy in moves(i):
            copy.wait()
        rows = []
        for n in range(CHUNK):
            z, source, k, t = taken_apart(i * CHUNK + n)
            off = jnp.where(i * CHUNK + n < count[0], SHIFT2, OFF)
            v = held[z, t // HB, pl.ds(pl.multiple_of(t % HB * BLK, BLK), BLK), :]
            w = dot(taken[slot, n], v, NT) + dot(parts[source], picks[k], NN)
            w = w - norms[pl.ds(z * KB + t, 1), :]
            made[slot, n] = w
            rows.append(jnp.sum(jnp.exp2(w * BETA + off), axis=0, keepdims=True))
        away(i).start()
        sums[pl.ds(pl.multiple_of(i * CHUNK, CHUNK), CHUNK), :] = jnp.concatenate(rows, axis=0)
        return needed

    seen = lax.fori_loop(0, chunks, one, -1)
    columns[...] = exact_sum(spread(col_place[...], NZ * KB), sums[...]).astype(BF16)
    for z in range(NZ):

        @pl.when(z > seen)
        def _():
            for h in range(2):
                into[2 * z + h].wait()

    for n in range(SLOTS):
        i = chunks - 1 - n

        @pl.when(i >= 0)
        def _():
            away(i).wait()


def first_pass(count, place, col_at, row_at, col_place, row_place, parts, picks, left, rights):
    return pl.pallas_call(
        first_kernel,
        in_specs=[SMEM_WHOLE] * 4 + [VMEM_WHOLE] * 4 + [IN_HBM] * (2 * NZ + 1),
        out_specs=[IN_HBM, VMEM_WHOLE],
        scratch_shapes=[
            pltpu.VMEM((POS, BLK), F32),
            pltpu.VMEM((SLOTS, CHUNK, BLK, E), BF16),
            pltpu.VMEM((NZ, 2, HALF, E), BF16),
            pltpu.VMEM((NZ * KB, BLK), F32),
            pltpu.VMEM((SLOTS, CHUNK, BLK, BLK), F32),
            pltpu.SemaphoreType.DMA((SLOTS, CHUNK)),
            pltpu.SemaphoreType.DMA((2 * NZ,)),
            pltpu.SemaphoreType.DMA((SLOTS,)),
        ],
        out_shape=[
            pltpu.HBM((POS, BLK, BLK), F32),
            jax.ShapeDtypeStruct((NZ * KB, BLK), BF16),
        ],
        compiler_params=pltpu.CompilerParams(vmem_limit_bytes=GRANT),
    )(
        count, place, col_at, row_at, col_place, row_place, parts, picks,
        in_hbm(left), *map(in_hbm, rights),
    )


def total_of(received):
    total = received[0].astype(F32)
    for n in range(1, received.shape[0]):
        total += received[n].astype(F32)
    return total


def one_chunk(source, target, sems, n):
    part = pl.ds(n * CHUNK, CHUNK)
    return pltpu.make_async_copy(source.at[part], target.at[part], sems.at[n])


def start_all(source, target, sems, chunks):
    for n in range(CHUNKS):

        @pl.when(n < chunks)
        def _():
            one_chunk(source, target, sems, n).start()


def second_kernel(
    count, col_at, row_place, received, cross, kernel, rows_out, column_sum,
    cross_here, kernel_here, potential, sums, in_sem, kernel_sem,
):
    chunks = chunks_of(count)
    start_all(cross, cross_here, in_sem, chunks)
    sums[...] = jnp.zeros_like(sums)
    column_sum[...] = total_of(received)
    potential[...] = 2.0 * SHIFT2 - jnp.log2(FLOOR + column_sum[...])
    ones = jnp.ones((16, BLK), BF16)

    @pl.loop(0, chunks)
    def _(step):
        one_chunk(cross, cross_here, in_sem, step).wait()
        rows = []
        for n in range(CHUNK):
            tile = step * CHUNK + n
            off = jnp.where(tile < count[0], 0.0, OFF)
            pot = potential[pl.ds(col_at[tile], 1), :] + off
            w = cross_here[tile]
            rounded = jnp.exp2(w * BETA + pot).astype(BF16)
            kernel_here[tile, 0:BLK, :] = rounded
            kernel_here[tile, BLK : 2 * BLK, :] = (
                rounded.astype(F32) * (w * (-2.0 / E))
            ).astype(BF16)
            rows.append(dot(ones, rounded, NT)[0:1, :])
        one_chunk(kernel_here, kernel, kernel_sem, step).start()
        sums[pl.ds(pl.multiple_of(step * CHUNK, CHUNK), CHUNK), :] = jnp.concatenate(rows, axis=0)

    rows_out[...] = exact_sum(spread(row_place[...], SOURCES * KB), sums[...]).astype(BF16)

    @pl.loop(0, chunks)
    def _(step):
        one_chunk(kernel_here, kernel, kernel_sem, step).wait()


def second_pass(count, col_at, row_place, received, cross):
    return pl.pallas_call(
        second_kernel,
        in_specs=[SMEM_WHOLE, SMEM_WHOLE, VMEM_WHOLE, VMEM_WHOLE, IN_HBM],
        out_specs=[IN_HBM, VMEM_WHOLE, VMEM_WHOLE],
        scratch_shapes=[
            pltpu.VMEM((POS, BLK, BLK), F32),
            pltpu.VMEM((POS, 2 * BLK, BLK), BF16),
            pltpu.VMEM((NZ * KB, BLK), F32),
            pltpu.VMEM((POS, BLK), F32),
            pltpu.SemaphoreType.DMA((CHUNKS,)),
            pltpu.SemaphoreType.DMA((CHUNKS,)),
        ],
        out_shape=[
            pltpu.HBM((POS, 2 * BLK, BLK), BF16),
            jax.ShapeDtypeStruct((SOURCES * KB, BLK), BF16),
            jax.ShapeDtypeStruct((NZ * KB, BLK), F32),
        ],
        compiler_params=pltpu.CompilerParams(vmem_limit_bytes=GRANT),
    )(count, col_at, row_place, received, in_hbm(cross))


def two_parts(row):
    high = row.astype(BF16).astype(F32)
    at = lax.broadcasted_iota(jnp.int32, (16, BLK), 0)
    return jnp.where(at == 0, high, jnp.where(at == 1, row - high, 0.0)).astype(BF16)


def third_kernel(
    count, row_at, col_place, received, kernel, columns, kernel_here, scale, sums, in_sem
):
    chunks = chunks_of(count)
    sums[...] = jnp.zeros_like(sums)
    upper = kernel.at[:, pl.ds(0, BLK)]
    start_all(upper, kernel_here, in_sem, chunks)
    scale[...] = 1.0 / (FLOOR + received[...].astype(F32))

    @pl.loop(0, chunks)
    def _(step):
        one_chunk(upper, kernel_here, in_sem, step).wait()
        rows = []
        for n in range(CHUNK):
            tile = step * CHUNK + n
            both = dot(two_parts(scale[pl.ds(row_at[tile], 1), :]), kernel_here[tile], NN)
            rows.append(both[0:1, :] + both[1:2, :])
        sums[pl.ds(pl.multiple_of(step * CHUNK, CHUNK), CHUNK), :] = jnp.concatenate(rows, axis=0)

    columns[...] = exact_sum(spread(col_place[...], NZ * KB), sums[...]).astype(BF16)


def third_pass(count, row_at, col_place, received, kernel):
    return pl.pallas_call(
        third_kernel,
        in_specs=[SMEM_WHOLE, SMEM_WHOLE, VMEM_WHOLE, VMEM_WHOLE, IN_HBM],
        out_specs=VMEM_WHOLE,
        scratch_shapes=[
            pltpu.VMEM((POS, BLK, BLK), BF16),
            pltpu.VMEM((SOURCES * KB, BLK), F32),
            pltpu.VMEM((POS, BLK), F32),
            pltpu.SemaphoreType.DMA((CHUNKS,)),
        ],
        out_shape=jax.ShapeDtypeStruct((NZ * KB, BLK), BF16),
        compiler_params=pltpu.CompilerParams(vmem_limit_bytes=GRANT),
    )(count, row_at, col_place, received, in_hbm(kernel))


def fourth_kernel(
    count, col_at, row_place, received, column_sum, kernel, rows_out, potential,
    kernel_here, scale, sums, weighed, kernel_sem,
):
    chunks = chunks_of(count)
    start_all(kernel, kernel_here, kernel_sem, chunks)
    sums[...] = jnp.zeros_like(sums)
    weighed[...] = jnp.zeros_like(weighed)
    plan_sum = total_of(received)
    scale[...] = EPSILON * (SHIFT - jnp.log(FLOOR + (FLOOR + column_sum[...]) * plan_sum))
    potential[...] = scale[pl.ds(pl.multiple_of(count[1] * KB, KB), KB), :]
    scale[...] = 1.0 / (FLOOR / (FLOOR + column_sum[...]) + plan_sum)

    @pl.loop(0, chunks)
    def _(step):
        one_chunk(kernel, kernel_here, kernel_sem, step).wait()
        rows, heavy = [], []
        for n in range(CHUNK):
            tile = step * CHUNK + n
            pair = two_parts(scale[pl.ds(col_at[tile], 1), :])
            both = dot(pair, kernel_here[tile], NT)
            both = both[0:1, :] + both[1:2, :]
            rows.append(both[:, 0:BLK])
            heavy.append(both[:, BLK : 2 * BLK])
        place = pl.ds(pl.multiple_of(step * CHUNK, CHUNK), CHUNK)
        sums[place, :] = jnp.concatenate(rows, axis=0)
        weighed[place, :] = jnp.concatenate(heavy, axis=0)

    which = spread(row_place[...], SOURCES * KB)
    total = exact_sum(which, sums[...])
    heavy_total = exact_sum(which, weighed[...])
    for s in range(SOURCES):
        c, y = s // NY, s % NY
        rows_out[y * NC + c, 0:KB, :] = total[s * KB : (s + 1) * KB, :]
        rows_out[y * NC + c, KB : 2 * KB, :] = heavy_total[s * KB : (s + 1) * KB, :]


def fourth_pass(count, col_at, row_place, received, column_sum, kernel):
    return pl.pallas_call(
        fourth_kernel,
        in_specs=[SMEM_WHOLE] * 2 + [VMEM_WHOLE] * 3 + [IN_HBM],
        out_specs=[VMEM_WHOLE] * 2,
        scratch_shapes=[
            pltpu.VMEM((POS, 2 * BLK, BLK), BF16),
            pltpu.VMEM((NZ * KB, BLK), F32),
            pltpu.VMEM((POS, BLK), F32),
            pltpu.VMEM((POS, BLK), F32),
            pltpu.SemaphoreType.DMA((CHUNKS,)),
        ],
        out_shape=[
            jax.ShapeDtypeStruct((SOURCES, 2 * KB, BLK), F32),
            jax.ShapeDtypeStruct((KB, BLK), F32),
        ],
        compiler_params=pltpu.CompilerParams(vmem_limit_bytes=GRANT),
    )(count, col_at, row_place, received, column_sum, in_hbm(kernel))


def ring_pieces(block, axis, n):
    up = [(i, (i + 1) % n) for i in range(n)]
    down = [(i, (i - 1) % n) for i in range(n)]
    top, low = block[0], block[1]
    held = [[top, low]] + [[None, None] for _ in range(n - 1)]
    right, left = [top, low], [low, top]
    for k in range(1, n // 2 + 1):
        for i in range(2 if k < n // 2 else 1):
            right[i] = lax.ppermute(right[i], axis, up)
            left[i] = lax.ppermute(left[i], axis, down)
            held[n - k][i] = right[i]
            held[k][1 - i] = left[i]
    return [half for pair in held for half in pair]


def swap(value, axes):
    return lax.all_to_all(value, axes, split_axis=0, concat_axis=0, tiled=True)


def to_all(value, axes, n):
    return swap(jnp.broadcast_to(value[None], (n,) + value.shape), axes)


def columns_to_row(columns):
    over_rep = jnp.sum(to_all(columns, "x", NX).astype(F32), axis=0)
    return to_all(over_rep.astype(BF16), "z", NZ)


def slot_codes(location, pair_block, pair_count):
    slots = pair_block.shape[1]
    stored = location[pair_block.reshape(-1)]
    used = (
        jnp.arange(slots, dtype=jnp.int32)[None, :] < pair_count[:, None]
    ).reshape(-1)
    block = jnp.arange(KB * slots, dtype=jnp.int32) // slots
    owner, local = stored // KB, stored % KB
    holders = jnp.arange(NY * NZ * NC, dtype=jnp.int32)
    match = (owner[None, :] == holders[:, None]) & used[None, :]
    return jnp.max(jnp.where(match, (block * KB + local)[None, :], -1), axis=1)


def in_use(codes):
    at = jnp.arange(POS, dtype=jnp.int32)
    active = codes >= 0
    rank = jnp.sum((active[None, :] & (at[None, :] < at[:, None])).astype(jnp.int32), axis=1)
    count = jnp.sum(active.astype(jnp.int32))
    place = jnp.where(active, at * 256 + codes, 0)
    lands = active[None, :] & (rank[None, :] == at[:, None])
    sorted_ = jnp.max(jnp.where(lands, place[None, :], 0), axis=1)
    used = at < count
    return count, jnp.where(used, sorted_, jnp.max(place)), used


def body(rollout, demo, projection, location, pair_block, pair_count):
    codes = slot_codes(location, pair_block, pair_count)
    codes = codes.reshape(NY, NZ, NC).transpose(0, 2, 1).reshape(SOURCES, 1, NZ)
    codes = swap(codes, ("y", "c")).reshape(SOURCES, NZ)
    own_codes = project_codes(rollout, projection)
    left = lax.all_gather(own_codes, ("y", "c"))
    rights = ring_pieces(project(demo, projection), "z", NZ)
    norms = block_norms(own_codes, rights[2 * (NZ - 2) + 1])
    parts, picks = norm_parts(to_all(norms, ("y", "c"), SOURCES))
    turned = (lax.axis_index("z") + jnp.arange(NZ, dtype=jnp.int32)) % NZ
    pick = turned[:, None] == jnp.arange(NZ, dtype=jnp.int32)[None, :]
    codes = jnp.max(jnp.where(pick[:, None, :], codes[None], -1), axis=2)
    count, place, used = in_use(codes.reshape(POS))
    count = jnp.stack([count, lax.axis_index("z").astype(jnp.int32)])
    piece, source = place // (256 * SOURCES), place // 256 % SOURCES
    col_at = (lax.axis_index("z") + piece) % NZ * KB + place % KB
    row_at = (source % NC * NY + source // NC) * KB + place // KB % KB
    col_place = jnp.where(used, col_at, -1).reshape(1, POS)
    row_place = jnp.where(used, row_at, -1).reshape(1, POS)


    cross, columns = first_pass(
        count, place, col_at, row_at, col_place, row_place, parts, picks, left, rights
    )
    kernel, rows, column_sum = second_pass(
        count, col_at, row_place, columns_to_row(columns), cross
    )
    rows = jnp.sum(swap(rows.reshape(NC, NY * KB, BLK), "c").astype(F32), axis=0)
    rows = jnp.sum(to_all(rows.astype(BF16), "y", NY).astype(F32), axis=0)
    rows = to_all(rows.astype(BF16), "c", NC).reshape(SOURCES * KB, BLK)
    columns = third_pass(count, row_at, col_place, rows, kernel)
    both, demo_pot = fourth_pass(
        count, col_at, row_place, columns_to_row(columns), column_sum, kernel
    )
    both = jnp.sum(swap(both, ("y", "c")), axis=0)
    total = FLOOR + both[:KB]
    reward = -(both[KB:] + UNMATCHED * FLOOR) / total
    roll_pot = EPSILON * (SHIFT - jnp.log(total))
    return reward.reshape(-1), roll_pot.reshape(-1), demo_pot.reshape(-1)


def solution(mesh):
    grid = Mesh(mesh.devices.reshape(NY, NZ, NC, NX), ("y", "z", "c", "x"))
    every, roll = ("y", "z", "c", "x"), ("y", "z", "c")
    return jax.shard_map(
        body,
        mesh=grid,
        in_specs=(P(every, None), P(roll, None), P(), P(), P(every, None), P(every)),
        out_specs=(P(every), P(every), P(roll)),
        check_vma=False,
    )
```

```python
import functools
import math

import jax
import jax.numpy as jnp
from jax import lax
from jax.experimental import pallas as pl
from jax.experimental.pallas import tpu as pltpu
from jax.sharding import Mesh
from jax.sharding import PartitionSpec as P

EPSILON = 0.02
UNMATCHED = 2.0
SLACK = 100.0
SHIFT = 46.0
LOG2E = 1.4426950408889634
SHIFT2 = SHIFT * LOG2E
FLOOR = math.exp(SHIFT - SLACK)
OFF = -1.0e30

BLK = 128
E = 256
NY, NZ, NC, NX = 8, 8, 2, 4
KB = 16
HB = KB // 2
HALF = HB * BLK + 2 * HB
SOURCES = NY * NC
POS = SOURCES * NZ
ROWS = KB * BLK
PART = 512
BETA = LOG2E * 2.0 / (E * EPSILON)
MIB = 2**20

F32, BF16 = jnp.float32, jnp.bfloat16
NT = (((1,), (1,)), ((), ()))
NN = (((1,), (0,)), ((), ()))
VMEM_WHOLE = pl.BlockSpec(memory_space=pltpu.VMEM)
SMEM_WHOLE = pl.BlockSpec(memory_space=pltpu.SMEM)
IN_HBM = pl.BlockSpec(memory_space=pltpu.HBM)
GRANT = 40 * MIB


def dot(left, right, dims):
    return lax.dot_general(left, right, dims, preferred_element_type=F32)


def exact_sum(onehot, values):
    return lax.dot_general(
        onehot, values, NN, precision=lax.Precision.HIGHEST, preferred_element_type=F32
    )


def spread(places, count):
    rows = lax.broadcasted_iota(jnp.int32, (count, POS), 0)
    return jnp.where(rows == places, 1.0, 0.0)


def norms_of(codes):
    wide = codes.astype(F32)
    square = wide * wide
    high = square.astype(BF16)
    low = (square - high.astype(F32)).astype(BF16)
    ones = jnp.ones((16, E), BF16)
    return (dot(ones, high, NT) + dot(ones, low, NT))[0:1, :]


def three_parts(norm):
    high = norm.astype(BF16).astype(F32)
    middle = (norm - high).astype(BF16).astype(F32)
    return high, middle, norm - high - middle


def codes_kernel(frames, head, out, here, projection, made, sems, head_sem, out_sems):
    def inward(n):
        rows = pl.ds(n * PART, PART)
        return pltpu.make_async_copy(frames.at[rows], here.at[rows], sems.at[n])

    def outward(n):
        rows = pl.ds(n * PART, PART)
        return pltpu.make_async_copy(made.at[rows], out.at[rows], out_sems.at[n])

    head_copy = pltpu.make_async_copy(head, projection, head_sem)
    inward(0).start()
    head_copy.start()
    for n in range(1, ROWS // PART):
        inward(n).start()
    head_copy.wait()
    for n in range(ROWS // PART):
        rows = pl.ds(n * PART, PART)
        inward(n).wait()
        made[rows, :] = dot(here[rows, :], projection[...], NN).astype(BF16)
        outward(n).start()
    for n in range(ROWS // PART):
        outward(n).wait()


def project_codes(frames, projection):
    return pl.pallas_call(
        codes_kernel,
        out_shape=pltpu.HBM((ROWS, E), BF16),
        in_specs=[IN_HBM, IN_HBM],
        out_specs=IN_HBM,
        scratch_shapes=[
            pltpu.VMEM((ROWS, E), BF16),
            pltpu.VMEM((E, E), BF16),
            pltpu.VMEM((ROWS, E), BF16),
            pltpu.SemaphoreType.DMA((ROWS // PART,)),
            pltpu.SemaphoreType.DMA,
            pltpu.SemaphoreType.DMA((ROWS // PART,)),
        ],
        compiler_params=pltpu.CompilerParams(vmem_limit_bytes=GRANT),
    )(in_hbm(frames), in_hbm(projection))


def norms_kernel(codes, after, out):
    for k in range(KB):
        out[k : k + 1, :] = norms_of(codes[pl.ds(k * BLK, BLK), :])


def block_norms(codes, after):
    return pl.pallas_call(
        norms_kernel,
        out_shape=jax.ShapeDtypeStruct((KB, BLK), F32),
        in_specs=[VMEM_WHOLE, pl.BlockSpec(memory_space=pl.ANY)],
        out_specs=VMEM_WHOLE,
        compiler_params=pltpu.CompilerParams(vmem_limit_bytes=GRANT),
    )(codes, after)


def parts_kernel(received, parts, picks):
    for n in range(SOURCES):
        stacked = [*three_parts(received[n, 0:KB, :]), jnp.zeros((KB, BLK), F32)]
        parts[n] = jnp.concatenate(stacked, axis=0).T.astype(BF16)
    row = lax.broadcasted_iota(jnp.int32, (4 * KB, BLK), 0)
    for k in range(KB):
        ours = (row % KB == k) & (row < 3 * KB)
        picks[k] = jnp.where(ours, -0.5, 0.0).astype(BF16)


def norm_parts(received):
    return pl.pallas_call(
        parts_kernel,
        out_shape=[
            jax.ShapeDtypeStruct((SOURCES, BLK, 4 * KB), BF16),
            jax.ShapeDtypeStruct((KB, 4 * KB, BLK), BF16),
        ],
        in_specs=[VMEM_WHOLE],
        out_specs=[VMEM_WHOLE] * 2,
        compiler_params=pltpu.CompilerParams(vmem_limit_bytes=GRANT),
    )(received)


def project_kernel(h, frames, head, out, here, projection, made, norms, sems, head_sem, out_sem):
    def inward(n):
        rows = pl.ds(n * PART, PART)
        return pltpu.make_async_copy(
            frames.at[pl.ds(h * HB * BLK + n * PART, PART)], here.at[rows], sems.at[n]
        )

    head_copy = pltpu.make_async_copy(head, projection, head_sem)
    inward(0).start()
    head_copy.start()
    for n in range(1, HB * BLK // PART):
        inward(n).start()
    head_copy.wait()
    for j in range(HB):
        if j * BLK % PART == 0:
            inward(j * BLK // PART).wait()
        codes = dot(here[pl.ds(j * BLK, BLK), :], projection[...], NN).astype(BF16)
        made[pl.ds(j * BLK, BLK), :] = codes
        norms[j : j + 1, :] = norms_of(codes)
    high, middle, low = three_parts(norms[...])
    left = jnp.concatenate([high, low], axis=0)
    right = jnp.concatenate([middle, jnp.zeros_like(low)], axis=0)
    made[HB * BLK : HALF, :] = jnp.concatenate([left, right], axis=1).astype(BF16)
    outward = pltpu.make_async_copy(made, out, out_sem)
    outward.start()
    outward.wait()


def project(frames, projection):
    return [
        pl.pallas_call(
            functools.partial(project_kernel, h),
            out_shape=pltpu.HBM((HALF, E), BF16),
            in_specs=[IN_HBM, IN_HBM],
            out_specs=IN_HBM,
            scratch_shapes=[
                pltpu.VMEM((HB * BLK, E), BF16),
                pltpu.VMEM((E, E), BF16),
                pltpu.VMEM((HALF, E), BF16),
                pltpu.VMEM((HB, BLK), F32),
                pltpu.SemaphoreType.DMA((HB * BLK // PART,)),
                pltpu.SemaphoreType.DMA,
                pltpu.SemaphoreType.DMA,
            ],
            compiler_params=pltpu.CompilerParams(vmem_limit_bytes=GRANT),
        )(in_hbm(frames), in_hbm(projection))
        for h in range(2)
    ]


def in_hbm(value):
    return pltpu.with_memory_space_constraint(value, pltpu.HBM)


AHEAD = 3
SLOTS = AHEAD + 1
CHUNK = 16
CHUNKS = POS // CHUNK


def chunks_of(count):
    return (count[0] + CHUNK - 1) // CHUNK


def first_kernel(count, place, col_at, row_at, col_place, row_place, parts, picks, left, *rest):
    rights = rest[: 2 * NZ]
    (
        cross, columns, sums, taken, held, norms, made, sems, right_sem, out_sem,
    ) = rest[2 * NZ :]
    chunks = chunks_of(count)

    def taken_apart(at):
        value = place[at]
        return value // (256 * SOURCES), value // 256 % SOURCES, value // KB % KB, value % KB

    def moves(i):
        slot = i % SLOTS
        copies = []
        for n in range(CHUNK):
            _, source, k, _ = taken_apart(i * CHUNK + n)
            start = pl.multiple_of(k * BLK, BLK)
            copies.append(
                pltpu.make_async_copy(
                    left.at[source, pl.ds(start, BLK)],
                    taken.at[slot, n],
                    sems.at[slot, n],
                )
            )
        return copies

    def away(i):
        slot = i % SLOTS
        to = cross.at[pl.ds(i * CHUNK, CHUNK)]
        return pltpu.make_async_copy(made.at[slot], to, out_sem.at[slot])

    into = [
        pltpu.make_async_copy(rights[i], held.at[i // 2, i % 2], right_sem.at[i])
        for i in range(2 * NZ)
    ]
    for i in range(AHEAD):
        for copy in into[2 * i : 2 * i + 2]:
            copy.start()

        @pl.when(i < chunks)
        def _():
            for copy in moves(i):
                copy.start()

    for copy in into[2 * AHEAD :]:
        copy.start()
    sums[...] = jnp.zeros_like(sums)

    def last_piece(i):
        return place[i * CHUNK + CHUNK - 1] // (256 * SOURCES)

    def one(i, seen):
        slot = i % SLOTS

        @pl.when(i + AHEAD < chunks)
        def _():
            for copy in moves(i + AHEAD):
                copy.start()

        @pl.when(i >= SLOTS)
        def _():
            away(i - SLOTS).wait()

        needed = last_piece(i)
        for z in range(NZ):

            @pl.when((z > seen) & (z <= needed))
            def _():
                for h in range(2):
                    into[2 * z + h].wait()
                    tail = held[z, h, HB * BLK : HALF, :].astype(F32)
                    norm = tail[0:HB, 0:BLK] + tail[0:HB, BLK:E] + tail[HB : 2 * HB, 0:BLK]
                    norms[z * KB + h * HB : z * KB + (h + 1) * HB, :] = 0.5 * norm

        for copy in moves(i):
            copy.wait()
        rows = []
        for n in range(CHUNK):
            z, source, k, t = taken_apart(i * CHUNK + n)
            off = jnp.where(i * CHUNK + n < count[0], SHIFT2, OFF)
            v = held[z, t // HB, pl.ds(pl.multiple_of(t % HB * BLK, BLK), BLK), :]
            w = dot(taken[slot, n], v, NT) + dot(parts[source], picks[k], NN)
            w = w - norms[pl.ds(z * KB + t, 1), :]
            made[slot, n] = w
            rows.append(jnp.sum(jnp.exp2(w * BETA + off), axis=0, keepdims=True))
        away(i).start()
        sums[pl.ds(pl.multiple_of(i * CHUNK, CHUNK), CHUNK), :] = jnp.concatenate(rows, axis=0)
        return needed

    seen = lax.fori_loop(0, chunks, one, -1)
    columns[...] = exact_sum(spread(col_place[...], NZ * KB), sums[...]).astype(BF16)
    for z in range(NZ):

        @pl.when(z > seen)
        def _():
            for h in range(2):
                into[2 * z + h].wait()

    for n in range(SLOTS):
        i = chunks - 1 - n

        @pl.when(i >= 0)
        def _():
            away(i).wait()


def first_pass(count, place, col_at, row_at, col_place, row_place, parts, picks, left, rights):
    return pl.pallas_call(
        first_kernel,
        in_specs=[SMEM_WHOLE] * 4 + [VMEM_WHOLE] * 4 + [IN_HBM] * (2 * NZ + 1),
        out_specs=[IN_HBM, VMEM_WHOLE],
        scratch_shapes=[
            pltpu.VMEM((POS, BLK), F32),
            pltpu.VMEM((SLOTS, CHUNK, BLK, E), BF16),
            pltpu.VMEM((NZ, 2, HALF, E), BF16),
            pltpu.VMEM((NZ * KB, BLK), F32),
            pltpu.VMEM((SLOTS, CHUNK, BLK, BLK), F32),
            pltpu.SemaphoreType.DMA((SLOTS, CHUNK)),
            pltpu.SemaphoreType.DMA((2 * NZ,)),
            pltpu.SemaphoreType.DMA((SLOTS,)),
        ],
        out_shape=[
            pltpu.HBM((POS, BLK, BLK), F32),
            jax.ShapeDtypeStruct((NZ * KB, BLK), BF16),
        ],
        compiler_params=pltpu.CompilerParams(vmem_limit_bytes=GRANT),
    )(
        count, place, col_at, row_at, col_place, row_place, parts, picks,
        in_hbm(left), *map(in_hbm, rights),
    )


def total_of(received):
    total = received[0].astype(F32)
    for n in range(1, received.shape[0]):
        total += received[n].astype(F32)
    return total


def one_chunk(source, target, sems, n):
    part = pl.ds(n * CHUNK, CHUNK)
    return pltpu.make_async_copy(source.at[part], target.at[part], sems.at[n])


def start_all(source, target, sems, chunks):
    for n in range(CHUNKS):

        @pl.when(n < chunks)
        def _():
            one_chunk(source, target, sems, n).start()


def second_kernel(
    count, col_at, row_place, received, cross, kernel, rows_out, column_sum,
    cross_here, kernel_here, potential, sums, in_sem, kernel_sem,
):
    chunks = chunks_of(count)
    start_all(cross, cross_here, in_sem, chunks)
    sums[...] = jnp.zeros_like(sums)
    column_sum[...] = total_of(received)
    potential[...] = 2.0 * SHIFT2 - jnp.log2(FLOOR + column_sum[...])
    ones = jnp.ones((16, BLK), BF16)

    @pl.loop(0, chunks)
    def _(step):
        one_chunk(cross, cross_here, in_sem, step).wait()
        rows = []
        for n in range(CHUNK):
            tile = step * CHUNK + n
            off = jnp.where(tile < count[0], 0.0, OFF)
            pot = potential[pl.ds(col_at[tile], 1), :] + off
            w = cross_here[tile]
            rounded = jnp.exp2(w * BETA + pot).astype(BF16)
            kernel_here[tile, 0:BLK, :] = rounded
            kernel_here[tile, BLK : 2 * BLK, :] = (
                rounded.astype(F32) * (w * (-2.0 / E))
            ).astype(BF16)
            rows.append(dot(ones, rounded, NT)[0:1, :])
        one_chunk(kernel_here, kernel, kernel_sem, step).start()
        sums[pl.ds(pl.multiple_of(step * CHUNK, CHUNK), CHUNK), :] = jnp.concatenate(rows, axis=0)

    rows_out[...] = exact_sum(spread(row_place[...], SOURCES * KB), sums[...]).astype(BF16)

    @pl.loop(0, chunks)
    def _(step):
        one_chunk(kernel_here, kernel, kernel_sem, step).wait()


def second_pass(count, col_at, row_place, received, cross):
    return pl.pallas_call(
        second_kernel,
        in_specs=[SMEM_WHOLE, SMEM_WHOLE, VMEM_WHOLE, VMEM_WHOLE, IN_HBM],
        out_specs=[IN_HBM, VMEM_WHOLE, VMEM_WHOLE],
        scratch_shapes=[
            pltpu.VMEM((POS, BLK, BLK), F32),
            pltpu.VMEM((POS, 2 * BLK, BLK), BF16),
            pltpu.VMEM((NZ * KB, BLK), F32),
            pltpu.VMEM((POS, BLK), F32),
            pltpu.SemaphoreType.DMA((CHUNKS,)),
            pltpu.SemaphoreType.DMA((CHUNKS,)),
        ],
        out_shape=[
            pltpu.HBM((POS, 2 * BLK, BLK), BF16),
            jax.ShapeDtypeStruct((SOURCES * KB, BLK), BF16),
            jax.ShapeDtypeStruct((NZ * KB, BLK), F32),
        ],
        compiler_params=pltpu.CompilerParams(vmem_limit_bytes=GRANT),
    )(count, col_at, row_place, received, in_hbm(cross))


def two_parts(row):
    high = row.astype(BF16).astype(F32)
    at = lax.broadcasted_iota(jnp.int32, (16, BLK), 0)
    return jnp.where(at == 0, high, jnp.where(at == 1, row - high, 0.0)).astype(BF16)


def third_kernel(
    count, row_at, col_place, received, kernel, columns, kernel_here, scale, sums, in_sem
):
    chunks = chunks_of(count)
    sums[...] = jnp.zeros_like(sums)
    upper = kernel.at[:, pl.ds(0, BLK)]
    start_all(upper, kernel_here, in_sem, chunks)
    scale[...] = 1.0 / (FLOOR + received[...].astype(F32))

    @pl.loop(0, chunks)
    def _(step):
        one_chunk(upper, kernel_here, in_sem, step).wait()
        rows = []
        for n in range(CHUNK):
            tile = step * CHUNK + n
            both = dot(two_parts(scale[pl.ds(row_at[tile], 1), :]), kernel_here[tile], NN)
            rows.append(both[0:1, :] + both[1:2, :])
        sums[pl.ds(pl.multiple_of(step * CHUNK, CHUNK), CHUNK), :] = jnp.concatenate(rows, axis=0)

    columns[...] = exact_sum(spread(col_place[...], NZ * KB), sums[...]).astype(BF16)


def third_pass(count, row_at, col_place, received, kernel):
    return pl.pallas_call(
        third_kernel,
        in_specs=[SMEM_WHOLE, SMEM_WHOLE, VMEM_WHOLE, VMEM_WHOLE, IN_HBM],
        out_specs=VMEM_WHOLE,
        scratch_shapes=[
            pltpu.VMEM((POS, BLK, BLK), BF16),
            pltpu.VMEM((SOURCES * KB, BLK), F32),
            pltpu.VMEM((POS, BLK), F32),
            pltpu.SemaphoreType.DMA((CHUNKS,)),
        ],
        out_shape=jax.ShapeDtypeStruct((NZ * KB, BLK), BF16),
        compiler_params=pltpu.CompilerParams(vmem_limit_bytes=GRANT),
    )(count, row_at, col_place, received, in_hbm(kernel))


def fourth_kernel(
    count, col_at, row_place, received, column_sum, kernel, rows_out, potential,
    kernel_here, scale, sums, weighed, kernel_sem,
):
    chunks = chunks_of(count)
    start_all(kernel, kernel_here, kernel_sem, chunks)
    sums[...] = jnp.zeros_like(sums)
    weighed[...] = jnp.zeros_like(weighed)
    plan_sum = total_of(received)
    scale[...] = EPSILON * (SHIFT - jnp.log(FLOOR + (FLOOR + column_sum[...]) * plan_sum))
    potential[...] = scale[pl.ds(pl.multiple_of(count[1] * KB, KB), KB), :]
    scale[...] = 1.0 / (FLOOR / (FLOOR + column_sum[...]) + plan_sum)

    @pl.loop(0, chunks)
    def _(step):
        one_chunk(kernel, kernel_here, kernel_sem, step).wait()
        rows, heavy = [], []
        for n in range(CHUNK):
            tile = step * CHUNK + n
            pair = two_parts(scale[pl.ds(col_at[tile], 1), :])
            both = dot(pair, kernel_here[tile], NT)
            both = both[0:1, :] + both[1:2, :]
            rows.append(both[:, 0:BLK])
            heavy.append(both[:, BLK : 2 * BLK])
        place = pl.ds(pl.multiple_of(step * CHUNK, CHUNK), CHUNK)
        sums[place, :] = jnp.concatenate(rows, axis=0)
        weighed[place, :] = jnp.concatenate(heavy, axis=0)

    which = spread(row_place[...], SOURCES * KB)
    total = exact_sum(which, sums[...])
    heavy_total = exact_sum(which, weighed[...])
    for s in range(SOURCES):
        c, y = s // NY, s % NY
        rows_out[y * NC + c, 0:KB, :] = total[s * KB : (s + 1) * KB, :]
        rows_out[y * NC + c, KB : 2 * KB, :] = heavy_total[s * KB : (s + 1) * KB, :]


def fourth_pass(count, col_at, row_place, received, column_sum, kernel):
    return pl.pallas_call(
        fourth_kernel,
        in_specs=[SMEM_WHOLE] * 2 + [VMEM_WHOLE] * 3 + [IN_HBM],
        out_specs=[VMEM_WHOLE] * 2,
        scratch_shapes=[
            pltpu.VMEM((POS, 2 * BLK, BLK), BF16),
            pltpu.VMEM((NZ * KB, BLK), F32),
            pltpu.VMEM((POS, BLK), F32),
            pltpu.VMEM((POS, BLK), F32),
            pltpu.SemaphoreType.DMA((CHUNKS,)),
        ],
        out_shape=[
            jax.ShapeDtypeStruct((SOURCES, 2 * KB, BLK), F32),
            jax.ShapeDtypeStruct((KB, BLK), F32),
        ],
        compiler_params=pltpu.CompilerParams(vmem_limit_bytes=GRANT),
    )(count, col_at, row_place, received, column_sum, in_hbm(kernel))


def ring_pieces(block, axis, n):
    up = [(i, (i + 1) % n) for i in range(n)]
    down = [(i, (i - 1) % n) for i in range(n)]
    top, low = block[0], block[1]
    held = [[top, low]] + [[None, None] for _ in range(n - 1)]
    right, left = [top, low], [low, top]
    for k in range(1, n // 2 + 1):
        for i in range(2 if k < n // 2 else 1):
            right[i] = lax.ppermute(right[i], axis, up)
            left[i] = lax.ppermute(left[i], axis, down)
            held[n - k][i] = right[i]
            held[k][1 - i] = left[i]
    return [half for pair in held for half in pair]


def swap(value, axes):
    return lax.all_to_all(value, axes, split_axis=0, concat_axis=0, tiled=True)


def to_all(value, axes, n):
    return swap(jnp.broadcast_to(value[None], (n,) + value.shape), axes)


def columns_to_row(columns):
    over_rep = jnp.sum(to_all(columns, "x", NX).astype(F32), axis=0)
    return to_all(over_rep.astype(BF16), "z", NZ)


def slot_codes(location, pair_block, pair_count):
    slots = pair_block.shape[1]
    stored = location[pair_block.reshape(-1)]
    used = (
        jnp.arange(slots, dtype=jnp.int32)[None, :] < pair_count[:, None]
    ).reshape(-1)
    block = jnp.arange(KB * slots, dtype=jnp.int32) // slots
    owner, local = stored // KB, stored % KB
    holders = jnp.arange(NY * NZ * NC, dtype=jnp.int32)
    match = (owner[None, :] == holders[:, None]) & used[None, :]
    return jnp.max(jnp.where(match, (block * KB + local)[None, :], -1), axis=1)


def in_use(codes):
    at = jnp.arange(POS, dtype=jnp.int32)
    active = codes >= 0
    rank = jnp.sum((active[None, :] & (at[None, :] < at[:, None])).astype(jnp.int32), axis=1)
    count = jnp.sum(active.astype(jnp.int32))
    place = jnp.where(active, at * 256 + codes, 0)
    lands = active[None, :] & (rank[None, :] == at[:, None])
    sorted_ = jnp.max(jnp.where(lands, place[None, :], 0), axis=1)
    used = at < count
    return count, jnp.where(used, sorted_, jnp.max(place)), used


def body(rollout, demo, projection, location, pair_block, pair_count):
    codes = slot_codes(location, pair_block, pair_count)
    codes = codes.reshape(NY, NZ, NC).transpose(0, 2, 1).reshape(SOURCES, 1, NZ)
    codes = swap(codes, ("y", "c")).reshape(SOURCES, NZ)
    own_codes = project_codes(rollout, projection)
    left = lax.all_gather(own_codes, ("y", "c"))
    rights = ring_pieces(project(demo, projection), "z", NZ)
    norms = block_norms(own_codes, rights[2 * (NZ - 2) + 1])
    parts, picks = norm_parts(to_all(norms, ("y", "c"), SOURCES))
    turned = (lax.axis_index("z") + jnp.arange(NZ, dtype=jnp.int32)) % NZ
    pick = turned[:, None] == jnp.arange(NZ, dtype=jnp.int32)[None, :]
    codes = jnp.max(jnp.where(pick[:, None, :], codes[None], -1), axis=2)
    count, place, used = in_use(codes.reshape(POS))
    count = jnp.stack([count, lax.axis_index("z").astype(jnp.int32)])
    piece, source = place // (256 * SOURCES), place // 256 % SOURCES
    col_at = (lax.axis_index("z") + piece) % NZ * KB + place % KB
    row_at = (source % NC * NY + source // NC) * KB + place // KB % KB
    col_place = jnp.where(used, col_at, -1).reshape(1, POS)
    row_place = jnp.where(used, row_at, -1).reshape(1, POS)


    cross, columns = first_pass(
        count, place, col_at, row_at, col_place, row_place, parts, picks, left, rights
    )
    kernel, rows, column_sum = second_pass(
        count, col_at, row_place, columns_to_row(columns), cross
    )
    rows = jnp.sum(swap(rows.reshape(NC, NY * KB, BLK), "c").astype(F32), axis=0)
    rows = jnp.sum(to_all(rows.astype(BF16), "y", NY).astype(F32), axis=0)
    rows = to_all(rows.astype(BF16), "c", NC).reshape(SOURCES * KB, BLK)
    columns = third_pass(count, row_at, col_place, rows, kernel)
    both, demo_pot = fourth_pass(
        count, col_at, row_place, columns_to_row(columns), column_sum, kernel
    )
    both = jnp.sum(swap(both, ("y", "c")), axis=0)
    total = FLOOR + both[:KB]
    reward = -(both[KB:] + UNMATCHED * FLOOR) / total
    roll_pot = EPSILON * (SHIFT - jnp.log(total))
    return reward.reshape(-1), roll_pot.reshape(-1), demo_pot.reshape(-1)


def solution(mesh):
    grid = Mesh(mesh.devices.reshape(NY, NZ, NC, NX), ("y", "z", "c", "x"))
    every, roll = ("y", "z", "c", "x"), ("y", "z", "c")
    return jax.shard_map(
        body,
        mesh=grid,
        in_specs=(P(every, None), P(roll, None), P(), P(), P(every, None), P(every)),
        out_specs=(P(every), P(every), P(roll)),
        check_vma=False,
    )
```
